32 devices in a mesh: dp: 4 (over y, x), seq: 8 (over z, core).
Axes of the slice: x: 2, y: 2, z: 4, core: 2. Of those that a mesh axis runs over, the one named last changes fastest.
Arguments:
- tokens: int32 [128, 1024], P('dp', 'seq'), may hold values from 0 to 255
- targets: int32 [128, 1024], P('dp', 'seq'), may hold values from 0 to 255
- counted: int32 [128, 1024], P('dp', 'seq'), may hold values from 0 to 1, as said below
- table: float32 [256, 512], P(('dp', 'seq')), may hold values from -0.625 to 0.625
- w_in: float32 [1, 512, 2048], P(None, ('dp', 'seq')), may hold values from -0.25 to 0.25
- w_out: float32 [1, 1024, 512], P(None, ('dp', 'seq')), may hold values from -0.1875 to 0.1875
- w_up: float32 [1, 512, 2048], P(None, ('dp', 'seq')), may hold values from -0.25 to 0.25
- w_down: float32 [1, 2048, 512], P(None, ('dp', 'seq')), may hold values from -0.125 to 0.125
- gains: float32 [3, 512], replicated, as said below
- conv_taps: float32 [1, 4, 512], replicated, may hold values from -3 to 3
- gate_bias: float32 [1, 1024], replicated, as said below
- m_table: float32 [256, 512], P(('dp', 'seq')), may hold values from -3.0517578e-05 to 3.0517578e-05
- m_in: float32 [1, 512, 2048], P(None, ('dp', 'seq')), may hold values from -3.0517578e-05 to 3.0517578e-05
- m_out: float32 [1, 1024, 512], P(None, ('dp', 'seq')), may hold values from -3.0517578e-05 to 3.0517578e-05
- m_up: float32 [1, 512, 2048], P(None, ('dp', 'seq')), may hold values from -3.0517578e-05 to 3.0517578e-05
- m_down: float32 [1, 2048, 512], P(None, ('dp', 'seq')), may hold values from -3.0517578e-05 to 3.0517578e-05
- m_gains: float32 [3, 512], replicated, may hold values from -0.00012207031 to 0.00012207031
- m_taps: float32 [1, 4, 512], replicated, may hold values from -0.00012207031 to 0.00012207031
- m_bias: float32 [1, 1024], replicated, may hold values from -0.00012207031 to 0.00012207031
- v_table: float32 [256, 512], P(('dp', 'seq')), may hold values from 2.6276403e-11 to 1.0510561e-10
- v_in: float32 [1, 512, 2048], P(None, ('dp', 'seq')), may hold values from 2.6276403e-11 to 1.0510561e-10
- v_out: float32 [1, 1024, 512], P(None, ('dp', 'seq')), may hold values from 2.6276403e-11 to 1.0510561e-10
- v_up: float32 [1, 512, 2048], P(None, ('dp', 'seq')), may hold values from 2.6276403e-11 to 1.0510561e-10
- v_down: float32 [1, 2048, 512], P(None, ('dp', 'seq')), may hold values from 2.6276403e-11 to 1.0510561e-10
- v_gains: float32 [3, 512], replicated, may hold values from 4.2042245e-10 to 1.6816898e-09
- v_taps: float32 [1, 4, 512], replicated, may hold values from 4.2042245e-10 to 1.6816898e-09
- v_bias: float32 [1, 1024], replicated, may hold values from 4.2042245e-10 to 1.6816898e-09
Outputs:
- loss_sum: float32 [], replicated
- count_total: float32 [], replicated
- grad_norm: float32 [], replicated
- new_table: float32 [256, 512], P(('dp', 'seq'))
- new_in: float32 [1, 512, 2048], P(None, ('dp', 'seq'))
- new_out: float32 [1, 1024, 512], P(None, ('dp', 'seq'))
- new_up: float32 [1, 512, 2048], P(None, ('dp', 'seq'))
- new_down: float32 [1, 2048, 512], P(None, ('dp', 'seq'))
- new_gains: float32 [3, 512], replicated
- new_taps: float32 [1, 4, 512], replicated
- new_bias: float32 [1, 1024], replicated
- next_m_table: float32 [256, 512], P(('dp', 'seq'))
- next_m_in: float32 [1, 512, 2048], P(None, ('dp', 'seq'))
- next_m_out: float32 [1, 1024, 512], P(None, ('dp', 'seq'))
- next_m_up: float32 [1, 512, 2048], P(None, ('dp', 'seq'))
- next_m_down: float32 [1, 2048, 512], P(None, ('dp', 'seq'))
- next_m_gains: float32 [3, 512], replicated
- next_m_taps: float32 [1, 4, 512], replicated
- next_m_bias: float32 [1, 1024], replicated
- next_v_table: float32 [256, 512], P(('dp', 'seq'))
- next_v_in: float32 [1, 512, 2048], P(None, ('dp', 'seq'))
- next_v_out: float32 [1, 1024, 512], P(None, ('dp', 'seq'))
- next_v_up: float32 [1, 512, 2048], P(None, ('dp', 'seq'))
- next_v_down: float32 [1, 2048, 512], P(None, ('dp', 'seq'))
- next_v_gains: float32 [3, 512], replicated
- next_v_taps: float32 [1, 4, 512], replicated
- next_v_bias: float32 [1, 1024], replicated
The draws below stay inside these ranges and needn't reach their ends.
Inputs may be any that keep to these rules, and one draw needn't show every extreme that they name: `counted`: each position's chance of counting rises along the sequence. `gains`: positive. `gate_bias`: negative or zero.
All inputs are finite; a program needn't handle non-finite values.
Results may differ from the reference program's by a relative error of at most 0.0006.
The reference program's roundings to bfloat16 on the way count: a program that leaves them out, or rounds other values in their place, can miss the bound.
Values may be sent and summed in bfloat16 or wider, within the bound.
A program may use at most 384 MiB of HBM per device.

```python
import math
import jax
import jax.numpy as jnp
import numpy as np
from jax import lax

D = 512
H = 1024
F = 2048
V = 256
KERNEL = 4
LAYERS = 1
STEP = 3
LENGTH = 1024
SEQS = 128
PARAMS = 3805696


def draw_counted(key, part):
    key = jax.random.fold_in(key, 2)
    position = jnp.arange(LENGTH, dtype=jnp.int32)
    roll = jax.random.randint(key, (SEQS, LENGTH), 0, 4 * LENGTH)
    return (roll < LENGTH + 2 * position).astype(jnp.int32)


def draw_gains(key, part):
    key = jax.random.fold_in(key, 3)
    ramp = jnp.arange(D, dtype=jnp.float32) / (D - 1)
    base = 0.6 + 1.2 * ramp
    spread = jax.random.uniform(key, (2 * LAYERS + 1, D), jnp.float32, 0.8, 1.25)
    return base * spread


def draw_gate_bias(key, part):
    key = jax.random.fold_in(key, 4)
    first, second, third = jax.random.split(key, 3)
    share = 0.5
    slow = jax.random.uniform(first, (LAYERS, H), jnp.float32) < share
    slow_value = -math.log(LENGTH) + jax.random.uniform(second, (LAYERS, H), jnp.float32, -1.5, 0.0)
    fast_value = jax.random.uniform(third, (LAYERS, H), jnp.float32, -4.0, 0.0)
    return jnp.where(slow, slow_value, fast_value)


def place_ends(array, stream_key, least, top_value):
    dims = array.shape
    index_at = [jax.random.randint(jax.random.fold_in(stream_key, axis), (), 0, dims[axis]) for axis in range(len(dims))]
    array = array.at[tuple(index_at)].set(least)
    longest = dims.index(max(dims))
    index_at[longest] = (index_at[longest] + 1) % dims[longest]
    return array.at[tuple(index_at)].set(top_value)


def levels(stream_key, dims, cuts, smallest, top_value):
    factor_of = 1.0
    for axis_at, shards_of in cuts:
        heights = jax.random.uniform(jax.random.fold_in(jax.random.fold_in(stream_key, 6), axis_at), (shards_of,), jnp.float32, smallest / len(cuts), top_value / len(cuts))
        factor_of = factor_of * jnp.repeat(jnp.exp(heights), dims[axis_at] // shards_of).reshape((-1,) + (1,) * (len(dims) - 1 - axis_at))
    return factor_of


def rank_bounds(count, skew):
    loads = [(1 << 20) // math.isqrt(rank ** skew) + 1 for rank in range(1, count + 1)]
    scale = 1 + sum(loads) // (1 << 30)
    return np.cumsum(np.array([max(1, weight // scale) for weight in loads]))


def skewed_ids(key, dims, amount, skew):
    listing = rank_bounds(amount, skew)
    lot = jax.random.randint(jax.random.fold_in(key, 1), dims, 0, int(listing[amount - 1]))
    grade = jnp.searchsorted(jnp.asarray(listing, jnp.int32), lot, side="right")
    return jax.random.permutation(jax.random.fold_in(key, 2), amount)[grade].astype(jnp.int32)


def bell_draw(rng, dims, scale, reach, cuts=(), kind=jnp.bfloat16):
    drawn = scale * jax.random.normal(rng, dims, jnp.float32)
    if cuts:
        drawn = drawn * levels(rng, dims, cuts, -0.22, 0.18)
    return jnp.clip(drawn, -reach, reach).astype(kind)


def setup_inputs(seed: int = 0) -> dict:
    seeds = jax.random.split(jax.random.key(seed), 28)
    return {
        "tokens": place_ends(skewed_ids(seeds[0], (SEQS, LENGTH), V, 2), jax.random.fold_in(seeds[0], 3), 0, V - 1).astype(jnp.int32),
        "targets": place_ends(skewed_ids(seeds[1], (SEQS, LENGTH), V, 2), jax.random.fold_in(seeds[1], 3), 0, V - 1).astype(jnp.int32),
        "counted": draw_counted(jax.random.fold_in(seeds[27], 71), 0),
        "table": bell_draw(seeds[3], (V, D), 0.1, 0.625, ((0, 32),), jnp.float32),
        "w_in": bell_draw(seeds[4], (LAYERS, D, 2 * H), D ** -0.5, 0.25, ((1, 32),), jnp.float32),
        "w_out": bell_draw(seeds[5], (LAYERS, H, D), H ** -0.5, 0.1875, ((1, 32),), jnp.float32),
        "w_up": bell_draw(seeds[6], (LAYERS, D, F), D ** -0.5, 0.25, ((1, 32),), jnp.float32),
        "w_down": bell_draw(seeds[7], (LAYERS, F, D), F ** -0.5, 0.125, ((1, 32),), jnp.float32),
        "gains": draw_gains(jax.random.fold_in(seeds[27], 71), 0),
        "conv_taps": bell_draw(seeds[9], (LAYERS, KERNEL, D), 0.5, 3.0, (), jnp.float32),
        "gate_bias": draw_gate_bias(jax.random.fold_in(seeds[27], 71), 0),
        "m_table": bell_draw(seeds[11], (V, D), (0.01 * PARAMS ** -0.5), 3.0517578125e-05, ((0, 32),), jnp.float32),
        "m_in": bell_draw(seeds[12], (LAYERS, D, 2 * H), (0.01 * PARAMS ** -0.5), 3.0517578125e-05, ((1, 32),), jnp.float32),
        "m_out": bell_draw(seeds[13], (LAYERS, H, D), (0.01 * PARAMS ** -0.5), 3.0517578125e-05, ((1, 32),), jnp.float32),
        "m_up": bell_draw(seeds[14], (LAYERS, D, F), (0.01 * PARAMS ** -0.5), 3.0517578125e-05, ((1, 32),), jnp.float32),
        "m_down": bell_draw(seeds[15], (LAYERS, F, D), (0.01 * PARAMS ** -0.5), 3.0517578125e-05, ((1, 32),), jnp.float32),
        "m_gains": bell_draw(seeds[16], (2 * LAYERS + 1, D), (0.04 * PARAMS ** -0.5), 0.00012207031, (), jnp.float32),
        "m_taps": bell_draw(seeds[17], (LAYERS, KERNEL, D), (0.04 * PARAMS ** -0.5), 0.00012207031, (), jnp.float32),
        "m_bias": bell_draw(seeds[18], (LAYERS, H), (0.04 * PARAMS ** -0.5), 0.00012207031, (), jnp.float32),
        "v_table": jnp.clip(jnp.exp(math.log(1.0510561171406252e-10) - 1.3862944 * jax.random.uniform(seeds[19], (V, D), jnp.float32) ** levels(seeds[19], (V, D), ((0, 32),), -0.2, 0.2)), 2.627640292851563e-11, 1.0510561171406252e-10),
        "v_in": jnp.clip(jnp.exp(math.log(1.0510561171406252e-10) - 1.3862944 * jax.random.uniform(seeds[20], (LAYERS, D, 2 * H), jnp.float32) ** levels(seeds[20], (LAYERS, D, 2 * H), ((1, 32),), -0.2, 0.2)), 2.627640292851563e-11, 1.0510561171406252e-10),
        "v_out": jnp.clip(jnp.exp(math.log(1.0510561171406252e-10) - 1.3862944 * jax.random.uniform(seeds[21], (LAYERS, H, D), jnp.float32) ** levels(seeds[21], (LAYERS, H, D), ((1, 32),), -0.2, 0.2)), 2.627640292851563e-11, 1.0510561171406252e-10),
        "v_up": jnp.clip(jnp.exp(math.log(1.0510561171406252e-10) - 1.3862944 * jax.random.uniform(seeds[22], (LAYERS, D, F), jnp.float32) ** levels(seeds[22], (LAYERS, D, F), ((1, 32),), -0.2, 0.2)), 2.627640292851563e-11, 1.0510561171406252e-10),
        "v_down": jnp.clip(jnp.exp(math.log(1.0510561171406252e-10) - 1.3862944 * jax.random.uniform(seeds[23], (LAYERS, F, D), jnp.float32) ** levels(seeds[23], (LAYERS, F, D), ((1, 32),), -0.2, 0.2)), 2.627640292851563e-11, 1.0510561171406252e-10),
        "v_gains": jnp.clip(jnp.exp(jax.random.uniform(seeds[24], (2 * LAYERS + 1, D), jnp.float32, math.log(4.204224468562501e-10), math.log(1.6816897874250003e-09))), 4.204224468562501e-10, 1.6816897874250003e-09),
        "v_taps": jnp.clip(jnp.exp(jax.random.uniform(seeds[25], (LAYERS, KERNEL, D), jnp.float32, math.log(4.204224468562501e-10), math.log(1.6816897874250003e-09))), 4.204224468562501e-10, 1.6816897874250003e-09),
        "v_bias": jnp.clip(jnp.exp(jax.random.uniform(seeds[26], (LAYERS, H), jnp.float32, math.log(4.204224468562501e-10), math.log(1.6816897874250003e-09))), 4.204224468562501e-10, 1.6816897874250003e-09),
    }


EPS = 1e-06
CLIP = 0.01
BETA_ONE = 0.5
BETA_TWO = 0.5
ADAM_EPS = 1e-08
RATE_MATRIX = 0.03
RATE_VECTOR = 0.3
WEIGHT_DECAY = 0.1

@jax.custom_vjp
def low(v):
    return lax.optimization_barrier(v.astype(jnp.bfloat16)).astype(jnp.float32)

@jax.custom_vjp
def low_back(v):
    return v

def low_keep(v):
    return (low(v), None)

def low_pass(kept, grad):
    return (grad,)

def back_keep(v):
    return (v, None)

def back_low(kept, grad):
    return (low(grad),)
low.defvjp(low_keep, low_pass)
low_back.defvjp(back_keep, back_low)

def rms_norm(values, gain):
    return values * lax.rsqrt(lax.optimization_barrier(jnp.mean(values * values, axis=-1, keepdims=True)) + EPS) * gain

def combine(earlier, later):
    return (earlier[0] * later[0], later[0] * earlier[1] + later[1])

def gates(gate, cand):
    return (jax.nn.sigmoid(-gate), jax.nn.sigmoid(gate) * jax.nn.softplus(cand))

def conv_apply(padded, taps, length):
    total = taps[0] * padded[:, 0:length]
    for k in range(1, taps.shape[0]):
        total = total + taps[k] * padded[:, k:k + length]
    return total

def product(left, right):
    return jnp.einsum('gtd,de->gte', left, right, precision=lax.Precision.HIGHEST)

def adam(weight, grad, first, second, rate, decay):
    first = BETA_ONE * first + (1.0 - BETA_ONE) * grad
    second = BETA_TWO * second + (1.0 - BETA_TWO) * grad * grad
    fix_one = 1.0 - BETA_ONE ** STEP
    fix_two = 1.0 - BETA_TWO ** STEP
    update = first / fix_one / (jnp.sqrt(second / fix_two) + ADAM_EPS)
    return (weight - rate * (update + decay * weight), first, second)

def model_loss(params, tok, tgt, msk):
    table, w_in, w_out, w_up, w_down, gains, conv_taps, gate_bias = params
    tab = low(table)
    resid = tab[tok]
    length = tok.shape[1]
    hidden = gate_bias.shape[1]
    for layer in range(LAYERS):
        queue = low_back(low(rms_norm(resid, gains[2 * layer])))
        padded = jnp.pad(queue, ((0, 0), (KERNEL - 1, 0), (0, 0)))
        conv = conv_apply(padded, conv_taps[layer], length)
        pre = low_back(product(low(conv), low(w_in[layer])))
        keep, write = gates(pre[..., :hidden] + gate_bias[layer], pre[..., hidden:])
        state = lax.associative_scan(combine, (keep, write), axis=1)[1]
        resid = resid + low_back(product(low(state), low(w_out[layer])))
        lifted = low_back(product(low(rms_norm(resid, gains[2 * layer + 1])), low(w_up[layer])))
        resid = resid + low_back(product(low(jax.nn.gelu(lifted)), low(w_down[layer])))
    normed = low(rms_norm(resid, gains[2 * LAYERS]))
    logits = low_back(jnp.einsum('gtd,vd->gtv', normed, tab, precision=lax.Precision.HIGHEST))
    lse = jax.nn.logsumexp(logits, axis=-1)
    picked = jnp.take_along_axis(logits, tgt[..., None], axis=-1)[..., 0]
    return jnp.sum(msk * (lse - picked))

def reference(tokens, targets, counted, table, w_in, w_out, w_up, w_down, gains, conv_taps, gate_bias, m_table, m_in, m_out, m_up, m_down, m_gains, m_taps, m_bias, v_table, v_in, v_out, v_up, v_down, v_gains, v_taps, v_bias):
    params = (table, w_in, w_out, w_up, w_down, gains, conv_taps, gate_bias)
    firsts = (m_table, m_in, m_out, m_up, m_down, m_gains, m_taps, m_bias)
    seconds = (v_table, v_in, v_out, v_up, v_down, v_gains, v_taps, v_bias)
    mask = counted.astype(jnp.float32)
    count = jnp.sum(mask)
    group = max((d for d in range(1, SEQS + 1) if SEQS % d == 0 and d * LENGTH <= max(4096, LENGTH)))
    blocks = SEQS // group
    tok = tokens.reshape(blocks, group, LENGTH)
    tgt = targets.reshape(blocks, group, LENGTH)
    msk = mask.reshape(blocks, group, LENGTH)

    def one_block(carry, pieces):
        grads, total = carry
        value, back = jax.vjp(lambda p: model_loss(p, pieces[0], pieces[1], pieces[2]), params)
        step, = back(1.0 / count)
        return ((jax.tree.map(lambda a, b: a + b, grads, step), total + value), None)
    zeros = jax.tree.map(jnp.zeros_like, params)
    (grads, loss_sum), _ = lax.scan(one_block, (zeros, jnp.zeros((), jnp.float32)), (tok, tgt, msk))
    squares = jnp.zeros((), jnp.float32)
    for grad in grads:
        squares = squares + jnp.sum(grad * grad)
    norm = jnp.sqrt(squares)
    scale = jnp.minimum(1.0, CLIP / (norm + 1e-06))
    news, next_m, next_v = ([], [], [])
    for index in range(8):
        rate = RATE_MATRIX if index < 5 else RATE_VECTOR
        decay = WEIGHT_DECAY if index < 5 else 0.0
        weight, first, second = adam(params[index], grads[index] * scale, firsts[index], seconds[index], rate, decay)
        news.append(weight)
        next_m.append(first)
        next_v.append(second)
    return (loss_sum, count, norm, news[0], news[1], news[2], news[3], news[4], news[5], news[6], news[7], next_m[0], next_m[1], next_m[2], next_m[3], next_m[4], next_m[5], next_m[6], next_m[7], next_v[0], next_v[1], next_v[2], next_v[3], next_v[4], next_v[5], next_v[6], next_v[7])
```

```python
import functools

import jax
import jax.numpy as jnp
from jax import lax
from jax.experimental import pallas as pl
from jax.experimental.pallas import tpu as pltpu
from jax.sharding import PartitionSpec as P

V = 256
MICRO = 2
STEP = 3


EPS = 1e-06
CLIP = 0.01
BETA_ONE = 0.5
BETA_TWO = 0.5
ADAM_EPS = 1e-08
RATE_MATRIX = 0.03
RATE_VECTOR = 0.3
WEIGHT_DECAY = 0.1


def from_behind(x, axis, by):
    devices = lax.axis_size(axis)
    pairs = [(i, i + by) for i in range(devices) if 0 <= i + by < devices]
    return lax.ppermute(x, axis, pairs)


def carried_in(part, axis, combine, identity, reverse):
    count = lax.axis_size(axis)
    place = lax.axis_index(axis)
    ahead = count - 1 - place if reverse else place
    gathered = jax.tree.map(lambda a: lax.all_gather(a, axis), part)
    state = jax.tree.map(lambda a, e: jnp.zeros_like(a) + jnp.asarray(e, a.dtype), part, identity)

    def one(lap, state):
        source = count - 1 - lap if reverse else lap
        return combine(
            state, jax.tree.map(lambda a: lax.dynamic_index_in_dim(a, source, 0, False), gathered)
        )

    return lax.fori_loop(0, ahead, one, state)


def matmul(left, right):
    return jnp.dot(left, right, preferred_element_type=jnp.float32)


def matmul_tn(left, right):
    return lax.dot_general(
        left, right, (((0,), (0,)), ((), ())), preferred_element_type=jnp.float32
    )


def matmul_nt(left, right):
    return lax.dot_general(
        left, right, (((1,), (1,)), ((), ())), preferred_element_type=jnp.float32
    )


def rms_norm(values, gain):
    return values * lax.rsqrt(jnp.mean(values * values, axis=-1, keepdims=True) + EPS) * gain


def combine(earlier, later):
    return (earlier[0] * later[0], later[0] * earlier[1] + later[1])


def gates(gate, cand):
    return (jax.nn.sigmoid(-gate), jax.nn.sigmoid(gate) * jax.nn.softplus(cand))


def conv_apply(padded, taps, length):
    total = taps[0] * padded[0:length].astype(jnp.float32)
    for k in range(1, taps.shape[0]):
        total = total + taps[k] * padded[k : k + length].astype(jnp.float32)
    return total


def adam(weight, grad, first, second, rate, decay):
    first = BETA_ONE * first + (1.0 - BETA_ONE) * grad
    second = BETA_TWO * second + (1.0 - BETA_TWO) * grad * grad
    fix_one = 1.0 - BETA_ONE**STEP
    fix_two = 1.0 - BETA_TWO**STEP
    update = first / fix_one / (jnp.sqrt(second / fix_two) + ADAM_EPS)
    return (weight - rate * (update + decay * weight), first, second)


def mixer_front(queue, rim, taps, bias, w_in):
    span, seqs, width = queue.shape
    padded = jnp.concatenate([rim, queue], axis=0)
    conv_low = conv_apply(padded, taps, span).astype(jnp.bfloat16)
    pre = matmul(conv_low.reshape(span * seqs, width), w_in).reshape(span, seqs, -1)
    hidden = bias.shape[0]
    keep, write = gates(pre[..., :hidden] + bias, pre[..., hidden:])
    return (padded, conv_low, pre, keep, write)


def block_tail(state, resid, gain_b, w_out, w_up, w_down):
    span, seqs, width = resid.shape
    state_low = state.astype(jnp.bfloat16).reshape(span * seqs, -1)
    mixed = resid + matmul(state_low, w_out).reshape(span, seqs, width)
    normed_low = rms_norm(mixed, gain_b).astype(jnp.bfloat16).reshape(span * seqs, width)
    lifted = matmul(normed_low, w_up)
    active_low = jax.nn.gelu(lifted).astype(jnp.bfloat16)
    result = mixed + matmul(active_low, w_down).reshape(span, seqs, width)
    return (result, (state_low, mixed, normed_low, lifted, active_low))


def layer_forward(resid, taps, gain_a, gain_b, bias, mats):
    span = resid.shape[0]
    kernel = taps.shape[0]
    queue = rms_norm(resid, gain_a).astype(jnp.bfloat16)
    rim = from_behind(queue[span - kernel + 1 :], "seq", 1)
    padded, conv_low, pre, keep, write = mixer_front(queue, rim, taps, bias, mats[0])
    decay, local = lax.associative_scan(combine, (keep, write), axis=0)
    ones = jnp.ones_like(local[0])
    carry_in = carried_in(
        (decay[-1], local[-1]), "seq", combine, (ones, jnp.zeros_like(ones)), False
    )[1]
    state = local + decay * carry_in[None]
    result, unused = block_tail(state, resid, gain_b, mats[1], mats[2], mats[3])
    return (result, rim, carry_in)


def layer_backward(grad, resid, rim, carry_in, taps, gain_a, gain_b, bias, mats):
    w_in, w_out, w_up, w_down = mats
    span, seqs, width = resid.shape
    kernel = taps.shape[0]
    hidden = bias.shape[0]
    normed_a, norm_back = jax.vjp(rms_norm, resid, gain_a)
    queue = normed_a.astype(jnp.bfloat16)
    padded, conv_low, pre, keep, write = mixer_front(queue, rim, taps, bias, w_in)
    decay, local = lax.associative_scan(combine, (keep, write), axis=0)
    state = local + decay * carry_in[None]
    result, (state_low, mixed, normed_low, lifted, active_low) = block_tail(
        state, resid, gain_b, w_out, w_up, w_down
    )
    grad_low = grad.astype(jnp.bfloat16).reshape(span * seqs, width)
    g_down = matmul_tn(active_low, grad_low)
    d_active = matmul_nt(grad_low, w_down)
    d_lifted_low = jax.vjp(jax.nn.gelu, lifted)[1](d_active)[0].astype(jnp.bfloat16)
    g_up = matmul_tn(normed_low, d_lifted_low)
    d_normed = matmul_nt(d_lifted_low, w_up).reshape(span, seqs, width)
    d_mixed, d_gain_b = jax.vjp(rms_norm, mixed, gain_b)[1](d_normed)
    d_mixed = grad + d_mixed
    mixed_low = d_mixed.astype(jnp.bfloat16).reshape(span * seqs, width)
    g_out = matmul_tn(state_low, mixed_low)
    d_state = matmul_nt(mixed_low, w_out).reshape(span, seqs, hidden)
    follow = jnp.concatenate([keep[1:], jnp.ones_like(keep[:1])], axis=0)
    reach, back_local = lax.associative_scan(combine, (follow, d_state), axis=0, reverse=True)
    ones = jnp.ones_like(keep[0])
    summary = (keep[0] * reach[0], keep[0] * back_local[0])
    carry_out = carried_in(summary, "seq", combine, (ones, jnp.zeros_like(ones)), True)[1]
    adjoint = back_local + reach * carry_out[None]
    before = jnp.concatenate([carry_in[None], state[:-1]], axis=0)
    d_gate, d_cand = jax.vjp(gates, pre[..., :hidden] + bias, pre[..., hidden:])[1](
        (adjoint * before, adjoint)
    )
    d_bias = jnp.sum(d_gate, axis=(0, 1))
    d_pre = (
        jnp.concatenate([d_gate, d_cand], axis=-1)
        .astype(jnp.bfloat16)
        .reshape(span * seqs, 2 * hidden)
    )
    g_in = matmul_tn(conv_low.reshape(span * seqs, width), d_pre)
    d_conv = matmul_nt(d_pre, w_in).reshape(span, seqs, width)
    beyond = from_behind(d_conv[: kernel - 1].astype(jnp.bfloat16), "seq", -1).astype(jnp.float32)
    extended = jnp.concatenate([d_conv, beyond], axis=0)
    d_queue = taps[0] * extended[kernel - 1 : kernel - 1 + span]
    tap_grads = [jnp.sum(d_conv * padded[0:span].astype(jnp.float32), axis=(0, 1))]
    for k in range(1, kernel):
        d_queue = d_queue + taps[k] * extended[kernel - 1 - k : kernel - 1 - k + span]
        tap_grads.append(jnp.sum(d_conv * padded[k : k + span].astype(jnp.float32), axis=(0, 1)))
    rounded = lax.optimization_barrier(d_queue.astype(jnp.bfloat16)).astype(jnp.float32)
    d_resid, d_gain_a = norm_back(rounded)
    return (
        d_mixed + d_resid,
        (g_in, g_out, g_up, g_down),
        (jnp.stack(tap_grads), d_gain_a, d_gain_b, d_bias),
    )


def body(
    tokens,
    targets,
    counted,
    table,
    w_in,
    w_out,
    w_up,
    w_down,
    gains,
    conv_taps,
    gate_bias,
    m_table,
    m_in,
    m_out,
    m_up,
    m_down,
    m_gains,
    m_taps,
    m_bias,
    v_table,
    v_in,
    v_out,
    v_up,
    v_down,
    v_gains,
    v_taps,
    v_bias,
):
    layers = w_in.shape[0]
    seq_dev, span = tokens.shape
    rows = seq_dev // MICRO
    width = table.shape[1]
    vocab = V
    mask = counted.astype(jnp.float32)
    count = lax.psum(jnp.sum(mask), ("dp", "seq"))
    shards = (
        w_in.astype(jnp.bfloat16),
        w_out.astype(jnp.bfloat16),
        w_up.astype(jnp.bfloat16),
        w_down.astype(jnp.bfloat16),
    )
    layer_gains = gains[: 2 * layers].reshape(layers, 2, width)
    columns = jnp.arange(vocab, dtype=jnp.int32)

    def forward_step(resid, inputs):
        pieces, taps, pair, bias = inputs
        mats = (
            lax.all_gather(pieces[0], ("dp", "seq"), axis=0, tiled=True),
            lax.all_gather(pieces[1], ("dp", "seq"), axis=0, tiled=True),
            lax.all_gather(pieces[2], ("dp", "seq"), axis=0, tiled=True),
            lax.all_gather(pieces[3], ("dp", "seq"), axis=0, tiled=True),
        )
        result, rim, carry_in = layer_forward(resid, taps, pair[0], pair[1], bias, mats)
        return (result, (resid, rim, carry_in))

    def backward_step(grad, inputs):
        saved, pieces, taps, pair, bias = inputs
        mats = (
            lax.all_gather(pieces[0], ("dp", "seq"), axis=0, tiled=True),
            lax.all_gather(pieces[1], ("dp", "seq"), axis=0, tiled=True),
            lax.all_gather(pieces[2], ("dp", "seq"), axis=0, tiled=True),
            lax.all_gather(pieces[3], ("dp", "seq"), axis=0, tiled=True),
        )
        grad, full, small = layer_backward(
            grad, saved[0], saved[1], saved[2], taps, pair[0], pair[1], bias, mats
        )
        full = (
            lax.psum_scatter(full[0], ("dp", "seq"), scatter_dimension=0, tiled=True),
            lax.psum_scatter(full[1], ("dp", "seq"), scatter_dimension=0, tiled=True),
            lax.psum_scatter(full[2], ("dp", "seq"), scatter_dimension=0, tiled=True),
            lax.psum_scatter(full[3], ("dp", "seq"), scatter_dimension=0, tiled=True),
        )
        return (grad, (full, small))

    loss = jnp.zeros((), jnp.float32)
    g_table = jnp.zeros((vocab, width), jnp.float32)
    acc_full = None
    acc_small = None
    for index in range(MICRO):
        tok = tokens[index * rows : (index + 1) * rows].T.reshape(-1)
        tgt = targets[index * rows : (index + 1) * rows].T.reshape(-1)
        weights = mask[index * rows : (index + 1) * rows].T.reshape(-1)
        tab = lax.all_gather(table.astype(jnp.bfloat16), ("dp", "seq"), axis=0, tiled=True)
        picks = tok[:, None] == columns[None, :]
        resid = matmul(picks.astype(jnp.bfloat16), tab).reshape(span, rows, width)
        final, saved = lax.scan(forward_step, resid, (shards, conv_taps, layer_gains, gate_bias))
        normed_f, final_back = jax.vjp(rms_norm, final, gains[2 * layers])
        normed_low = normed_f.astype(jnp.bfloat16).reshape(span * rows, width)
        logits = matmul_nt(normed_low, tab)
        top = jnp.max(logits, axis=-1, keepdims=True)
        lse = jnp.log(jnp.sum(jnp.exp(logits - top), axis=-1)) + top[:, 0]
        hits = (tgt[:, None] == columns[None, :]).astype(jnp.float32)
        picked = jnp.sum(hits * logits, axis=-1)
        loss = loss + jnp.sum(weights * (lse - picked))
        d_logits = ((jnp.exp(logits - lse[:, None]) - hits) * (weights / count)[:, None]).astype(
            jnp.bfloat16
        )
        g_table = g_table + matmul_tn(d_logits, normed_low)
        d_normed = matmul(d_logits, tab).reshape(span, rows, width)
        d_final, d_gain_f = final_back(d_normed)
        grad0, (full, small) = lax.scan(
            backward_step, d_final, (saved, shards, conv_taps, layer_gains, gate_bias), reverse=True
        )
        g_table = g_table + lax.dot_general(
            picks.astype(jnp.float32),
            grad0.reshape(span * rows, width),
            (((0,), (0,)), ((), ())),
            precision=lax.Precision.HIGHEST,
        )
        layer_gain_grads = jnp.stack([small[1], small[2]], axis=1).reshape(2 * layers, width)
        vectors = (jnp.concatenate([layer_gain_grads, d_gain_f[None]], axis=0), small[0], small[3])
        if index == 0:
            acc_full, acc_small = (full, vectors)
        else:
            acc_full = jax.tree.map(lambda a, b: a + b, acc_full, full)
            acc_small = jax.tree.map(lambda a, b: a + b, acc_small, vectors)
    table_shard = lax.psum_scatter(g_table, ("dp", "seq"), scatter_dimension=0, tiled=True)
    g_gains, g_taps, g_bias = lax.psum((acc_small[0], acc_small[1], acc_small[2]), ("dp", "seq"))
    matrices = (table_shard, acc_full[0], acc_full[1], acc_full[2], acc_full[3])
    squares = jnp.zeros((), jnp.float32)
    for grad in matrices:
        squares = squares + jnp.sum(grad * grad)
    squares_all, loss_all = lax.psum((squares, loss), ("dp", "seq"))
    small_squares = jnp.sum(g_gains * g_gains) + jnp.sum(g_taps * g_taps) + jnp.sum(g_bias * g_bias)
    norm = jnp.sqrt(squares_all + small_squares)
    scale = jnp.minimum(1.0, CLIP / (norm + 1e-06))
    params = (table, w_in, w_out, w_up, w_down, gains, conv_taps, gate_bias)
    grads = matrices + (g_gains, g_taps, g_bias)
    firsts = (m_table, m_in, m_out, m_up, m_down, m_gains, m_taps, m_bias)
    seconds = (v_table, v_in, v_out, v_up, v_down, v_gains, v_taps, v_bias)
    news, next_m, next_v = ([], [], [])
    for index in range(8):
        rate = RATE_MATRIX if index < 5 else RATE_VECTOR
        decay = WEIGHT_DECAY if index < 5 else 0.0
        weight, first, second = adam(
            params[index], grads[index] * scale, firsts[index], seconds[index], rate, decay
        )
        news.append(weight)
        next_m.append(first)
        next_v.append(second)
    return (
        loss_all,
        count,
        norm,
        news[0],
        news[1],
        news[2],
        news[3],
        news[4],
        news[5],
        news[6],
        news[7],
        next_m[0],
        next_m[1],
        next_m[2],
        next_m[3],
        next_m[4],
        next_m[5],
        next_m[6],
        next_m[7],
        next_v[0],
        next_v[1],
        next_v[2],
        next_v[3],
        next_v[4],
        next_v[5],
        next_v[6],
        next_v[7],
    )


BF = jnp.bfloat16
F32 = jnp.float32
MIB = 1 << 20
LANES = 128
ROWS = 8
GELU_A = 0.7978845608028654
GELU_B = 0.044715


def nn(left, right):
    return jnp.dot(left, right, preferred_element_type=F32)


def tn(left, right):
    return lax.dot_general(left, right, (((0,), (0,)), ((), ())), preferred_element_type=F32)


def nt(left, right):
    return lax.dot_general(left, right, (((1,), (1,)), ((), ())), preferred_element_type=F32)


def inv_rms(values):
    return lax.rsqrt(jnp.mean(values * values, axis=-1, keepdims=True) + EPS)


def norm_back(values, inverse, gain, grad):
    width = values.shape[-1]
    scaled = grad * gain
    dot = jnp.sum(scaled * values, axis=-1, keepdims=True)
    return inverse * scaled - values * (inverse * inverse * inverse * dot * (1.0 / width))


def column_sum(values):
    return jnp.sum(values, axis=0, keepdims=True)


def swap_halves(tile):
    return pltpu.roll(tile, ROWS // 2, tile.ndim - 2)


def one_hot(column, vocab):
    lane = lax.broadcasted_iota(jnp.int32, (column.shape[0], vocab), 1)
    return (column == lane).astype(F32).astype(BF)


def one_hot_t(row, vocab):
    place = lax.broadcasted_iota(jnp.int32, (vocab, row.shape[1]), 0)
    return (row == place).astype(F32).astype(BF)


def forward_kernel(
    ids, tab, count, gains, taps, bias, w_in, w_out, w_up, w_down,
    keep_o, p_o, q_o, ds_o, conv_o, queue_o, g_down, g_up, g_out, g_tab, small_o,
    tab_low, qtab, padq, tail_s, carry_s, big, state_low, active, mixed_s, normed_s,
):
    step = pl.program_id(0)
    rows, hidden = keep_o.shape
    vocab, width = tab.shape
    ff = w_up.shape[1]
    kernel = taps.shape[0]
    rim = (kernel - 1) * ROWS
    steps = rows // ROWS
    chunk = 256

    @pl.when(step == 0)
    def _():
        low = tab[...].astype(BF)
        tab_low[...] = low
        wide = low.astype(F32)
        qtab[...] = (wide * inv_rms(wide) * gains[0:1]).astype(BF)
        g_down[...] = jnp.zeros_like(g_down)
        g_up[...] = jnp.zeros_like(g_up)
        g_out[...] = jnp.zeros_like(g_out)
        g_tab[...] = jnp.zeros_like(g_tab)
        small_o[...] = jnp.zeros_like(small_o)
        tail_s[...] = jnp.zeros_like(tail_s)
        carry_s[...] = jnp.zeros_like(carry_s)

    wide_ids = ids[0]
    columns = wide_ids.T
    hot = one_hot(columns[:, 0:1], vocab)
    queue = nn(hot, qtab[...])
    queue_o[...] = queue.astype(BF)
    padq[rim:, :] = queue
    half = (
        lax.broadcasted_iota(jnp.int32, (rim, width), 0) % ROWS < ROWS // 2
    )
    before = tail_s[...].reshape(kernel - 1, ROWS, width)
    latest = padq[rows:, :].reshape(kernel - 1, ROWS, width)
    padq[0:rim, :] = jnp.where(
        half, swap_halves(before).reshape(rim, width), swap_halves(latest).reshape(rim, width)
    )
    tail_s[...] = padq[rows:, :]
    conv = taps[0:1] * padq[0:rows, :]
    for k in range(1, kernel):
        conv = conv + taps[k : k + 1] * padq[k * ROWS : k * ROWS + rows, :]
    conv_o[...] = conv.astype(BF)

    for j in range(hidden // chunk):
        cols = slice(j * chunk, (j + 1) * chunk)
        gate = nn(conv_o[...], w_in[:, j * chunk : (j + 1) * chunk]) + bias[0:1, cols]
        cand = nn(conv_o[...], w_in[:, hidden + j * chunk : hidden + (j + 1) * chunk])
        eg = jnp.exp(-jnp.abs(gate))
        rg = pl.reciprocal(1.0 + eg)
        sg = eg * rg
        up = gate >= 0
        write_gate = jnp.where(up, rg, sg)
        keep_o[:, cols] = jnp.where(up, sg, rg)
        ec = jnp.exp(-jnp.abs(cand))
        rc = pl.reciprocal(1.0 + ec)
        slope = jnp.where(cand >= 0, rc, ec * rc)
        soft = jnp.maximum(cand, 0.0) + jnp.where(
            ec < 1e-3, ec * (1.0 - 0.5 * ec), jnp.log(1.0 + ec)
        )
        p_o[:, cols] = write_gate
        q_o[:, cols] = write_gate * slope
        big[:, cols] = write_gate * soft

    low_half = lax.broadcasted_iota(jnp.int32, (ROWS, hidden), 0) < ROWS // 2
    carry = carry_s[...]
    ones = jnp.where(low_half, 0.0, 1.0)

    def scan_one(tau, held):
        state, reach = held
        at = pl.ds(pl.multiple_of(tau * ROWS, ROWS), ROWS)
        keep = keep_o[at, :]
        state = keep * state + big[at, 0:hidden]
        reach = keep * reach
        ds_o[at, :] = state
        big[at, hidden : 2 * hidden] = reach
        return state, reach

    end, _ = lax.fori_loop(0, steps, scan_one, (carry, ones), unroll=4)
    entry = jnp.where(low_half, 0.0, swap_halves(end))

    def fix_one(pair, previous):
        lows = []
        for half_step in range(2):
            at = pl.ds(pl.multiple_of(pair * 2 * ROWS + half_step * ROWS, ROWS), ROWS)
            state = ds_o[at, :] + big[at, hidden : 2 * hidden] * entry
            p_o[at, :] = keep_o[at, :] * (big[at, 0:hidden] - p_o[at, :] * previous)
            previous = state
            lows.append(state)
        both = pl.ds(pl.multiple_of(pair * 2 * ROWS, 2 * ROWS), 2 * ROWS)
        state_low[both, :] = jnp.concatenate(lows, axis=0).astype(BF)
        return previous

    last = lax.fori_loop(
        0, steps // 2, fix_one, jnp.where(low_half, carry, entry), unroll=4
    )
    carry_s[...] = jnp.where(low_half, swap_halves(last), 0.0)

    mixed = nn(hot, tab_low[...]) + nn(state_low[...], w_out[...])
    mixed_s[...] = mixed
    inverse_b = inv_rms(mixed)
    normed_s[...] = (mixed * inverse_b * gains[1:2]).astype(BF)
    for j in range(ff // chunk):
        cols = slice(j * chunk, (j + 1) * chunk)
        lifted = nn(normed_s[...], w_up[:, cols])
        square = lifted * lifted
        curve = jnp.tanh(lifted * (GELU_A + (GELU_A * GELU_B) * square))
        cdf = 0.5 + 0.5 * curve
        active[:, cols] = (lifted * cdf).astype(BF)
        big[:, cols] = cdf + (0.5 * lifted) * (1.0 - curve * curve) * (
            GELU_A + (3.0 * GELU_A * GELU_B) * square
        )
    result = mixed + nn(active[...], w_down[...])
    inverse_f = inv_rms(result)
    unit_f = result * inverse_f
    normed_f = (unit_f * gains[2:3]).astype(BF)

    logits = nt(normed_f, tab_low[...])
    top = jnp.max(logits, axis=-1, keepdims=True)
    powers = jnp.exp(logits - top)
    total = jnp.sum(powers, axis=-1, keepdims=True)
    lse = jnp.log(total) + top
    target = columns[:, 1:2] == lax.broadcasted_iota(jnp.int32, (rows, vocab), 1)
    picked = jnp.sum(jnp.where(target, logits, 0.0), axis=-1, keepdims=True)
    weight = columns[:, 2:3].astype(F32)
    loss = column_sum(weight * (lse - picked))
    share = weight * (1.0 / jnp.sum(count[:, 0:1, 0:1]))
    d_logits = ((powers * (1.0 / total) - jnp.where(target, 1.0, 0.0)) * share).astype(BF)
    g_tab[...] += tn(d_logits, normed_f)
    d_normed_f = nn(d_logits, tab_low[...])
    small_o[2:3, :] += column_sum(d_normed_f * unit_f)
    small_o[3:4, :] += jnp.broadcast_to(loss, (1, width))
    d_final = norm_back(result, inverse_f, gains[2:3], d_normed_f)
    grad_low = d_final.astype(BF)

    for j in range(ff // chunk):
        cols = slice(j * chunk, (j + 1) * chunk)
        d_active = nt(grad_low, w_down[cols, :])
        g_down[cols, :] += tn(active[:, cols], grad_low)
        active[:, cols] = (d_active * big[:, cols]).astype(BF)
    g_up[...] += tn(normed_s[...], active[...])
    d_normed = nt(active[...], w_up[...])
    mixed = mixed_s[...]
    inverse_b = inv_rms(mixed)
    small_o[1:2, :] += column_sum(d_normed * (mixed * inverse_b))
    d_mixed = d_final + norm_back(mixed, inverse_b, gains[1:2], d_normed)
    mixed_low = d_mixed.astype(BF)
    rest = (d_mixed - mixed_low.astype(F32)).astype(BF)
    g_out[...] += tn(state_low[...], mixed_low)
    ds_o[...] = nt(mixed_low, w_out[...])
    hot_t = one_hot_t(wide_ids[0:1, :], vocab)
    g_tab[...] += nn(hot_t, mixed_low) + nn(hot_t, rest)


def whole(shape):
    zeros = (0,) * len(shape)
    return pl.BlockSpec(shape, lambda i: zeros, pipeline_mode=pl.Buffered(1))


def run_forward(ids, tab, count, gains, taps, bias, w_in, w_out, w_up, w_down):
    blocks, _, rows = ids.shape
    vocab, width = tab.shape
    hidden = w_out.shape[0]
    ff = w_up.shape[1]
    kernel = taps.shape[0]
    total = blocks * rows
    rim = (kernel - 1) * ROWS
    wide = pl.BlockSpec((rows, hidden), lambda i: (i, 0))
    thin = pl.BlockSpec((rows, width), lambda i: (i, 0))
    macs = 3 * (width * 2 * hidden // 3 + hidden * width + 2 * width * ff + vocab * width) + 4 * vocab * width
    return pl.pallas_call(
        forward_kernel,
        grid=(blocks,),
        in_specs=[pl.BlockSpec((1, ROWS, rows), lambda i: (i, 0, 0))]
        + [whole(a.shape) for a in (tab, count, gains, taps, bias, w_in, w_out, w_up, w_down)],
        out_specs=[wide, wide, wide, wide, thin, thin]
        + [whole(s) for s in ((ff, width), (width, ff), (hidden, width), (vocab, width), (ROWS, width))],
        out_shape=[jax.ShapeDtypeStruct((total, hidden), F32)] * 4
        + [jax.ShapeDtypeStruct((total, width), BF)] * 2
        + [
            jax.ShapeDtypeStruct(s, F32)
            for s in ((ff, width), (width, ff), (hidden, width), (vocab, width), (ROWS, width))
        ],
        scratch_shapes=[
            pltpu.VMEM((vocab, width), BF),
            pltpu.VMEM((vocab, width), BF),
            pltpu.VMEM((rim + rows, width), F32),
            pltpu.VMEM((rim, width), F32),
            pltpu.VMEM((ROWS, hidden), F32),
            pltpu.VMEM((rows, max(ff, 2 * hidden)), F32),
            pltpu.VMEM((rows, hidden), BF),
            pltpu.VMEM((rows, ff), BF),
            pltpu.VMEM((rows, width), F32),
            pltpu.VMEM((rows, width), BF),
        ],
        compiler_params=pltpu.CompilerParams(
            dimension_semantics=("arbitrary",), vmem_limit_bytes=62 * MIB
        ),
        cost_estimate=pl.CostEstimate(
            flops=2 * macs * total, bytes_accessed=total * hidden * 16, transcendentals=total * (5 * hidden + ff)
        ),
        name="forward_and_tail_back",
    )(ids, tab, count, gains, taps, bias, w_in, w_out, w_up, w_down)


def backward_kernel(
    ids, keep, p, q, ds, conv, queue, tab, gains, taps, w_in, g_tab_in, small_in,
    g_in, g_tab, small_o,
    lam_s, reach_s, d_pre, ext, head_s, carry_s, hot_sum,
):
    step = pl.program_id(0)
    rows, hidden = keep.shape
    vocab, width = tab.shape
    kernel = taps.shape[0]
    rim = (kernel - 1) * ROWS
    steps = rows // ROWS
    bias_rows = hidden // width

    @pl.when(step == 0)
    def _():
        g_in[...] = jnp.zeros_like(g_in)
        hot_sum[...] = jnp.zeros_like(hot_sum)
        small_o[...] = jnp.zeros_like(small_o)
        small_o[0:ROWS, :] = small_in[...]
        head_s[...] = jnp.zeros_like(head_s)
        carry_s[...] = jnp.zeros_like(carry_s)

    low_half = lax.broadcasted_iota(jnp.int32, (ROWS, hidden), 0) < ROWS // 2

    def scan_one(i, held):
        carry, reach = held
        at = pl.ds(pl.multiple_of((steps - 1 - i) * ROWS, ROWS), ROWS)
        lam = ds[at, :] + carry
        lam_s[at, :] = lam
        reach_s[at, :] = reach
        k = keep[at, :]
        return k * lam, k * reach

    first, _ = lax.fori_loop(
        0, steps, scan_one, (carry_s[...], jnp.where(low_half, 1.0, 0.0)), unroll=4
    )
    entry = jnp.where(low_half, swap_halves(first), 0.0)
    reach0 = keep[0:ROWS, :] * reach_s[0:ROWS, :]
    carry_s[...] = jnp.where(low_half, 0.0, swap_halves(first + reach0 * entry))

    def fix_one(pair, sums):
        gates, cands = [], []
        for half_step in range(2):
            at = pl.ds(pl.multiple_of(pair * 2 * ROWS + half_step * ROWS, ROWS), ROWS)
            lam = lam_s[at, :] + reach_s[at, :] * entry
            d_gate = lam * p[at, :]
            sums = sums + d_gate
            gates.append(d_gate)
            cands.append(lam * q[at, :])
        both = pl.ds(pl.multiple_of(pair * 2 * ROWS, 2 * ROWS), 2 * ROWS)
        d_pre[both, 0:hidden] = jnp.concatenate(gates, axis=0).astype(BF)
        d_pre[both, hidden : 2 * hidden] = jnp.concatenate(cands, axis=0).astype(BF)
        return sums

    sums = lax.fori_loop(
        0, steps // 2, fix_one, jnp.zeros((ROWS, hidden), F32), unroll=4
    )
    d_bias = column_sum(sums)
    base = ROWS + kernel
    for r in range(bias_rows):
        small_o[base + r : base + r + 1, :] += d_bias[:, r * width : (r + 1) * width]

    g_in[...] += tn(conv[...], d_pre[...])
    ext[0:rows, :] = nt(d_pre[...], w_in[...])
    half = lax.broadcasted_iota(jnp.int32, (rim, width), 0) % ROWS < ROWS // 2
    mine = ext[0:rim, :]
    ext[rows:, :] = jnp.where(
        half,
        swap_halves(mine.reshape(kernel - 1, ROWS, width)).reshape(rim, width),
        swap_halves(head_s[...].reshape(kernel - 1, ROWS, width)).reshape(rim, width),
    )
    head_s[...] = mine
    known = queue[...].astype(F32)
    d_queue = None
    for k in range(kernel):
        shift = (kernel - 1 - k) * ROWS
        part = ext[shift : shift + rows, :]
        term = taps[k : k + 1] * part
        d_queue = term if d_queue is None else d_queue + term
        small_o[ROWS + k : ROWS + k + 1, :] += column_sum(part * known)
    hot_t = one_hot_t(ids[0][0:1, :], vocab)
    hot_sum[...] += nn(hot_t, d_queue.astype(BF))

    @pl.when(step == pl.num_programs(0) - 1)
    def _():
        wide = tab[...].astype(BF).astype(F32)
        inverse = inv_rms(wide)
        total = hot_sum[...]
        small_o[0:1, :] = column_sum(total * (wide * inverse))
        g_tab[...] = g_tab_in[...] + norm_back(wide, inverse, gains[0:1], total)


def run_backward(ids, keep, p, q, ds, conv, queue, tab, gains, taps, w_in, g_tab, small):
    blocks, _, rows = ids.shape
    vocab, width = tab.shape
    hidden = keep.shape[1]
    kernel = taps.shape[0]
    total = blocks * rows
    rim = (kernel - 1) * ROWS
    last = blocks - 1
    wide = pl.BlockSpec((rows, hidden), lambda i: (last - i, 0))
    thin = pl.BlockSpec((rows, width), lambda i: (last - i, 0))
    out = ((width, 2 * hidden), (vocab, width), (2 * ROWS, width))
    return pl.pallas_call(
        backward_kernel,
        grid=(blocks,),
        in_specs=[pl.BlockSpec((1, ROWS, rows), lambda i: (last - i, 0, 0)), wide, wide, wide, wide, thin, thin]
        + [whole(a.shape) for a in (tab, gains, taps, w_in, g_tab, small)],
        out_specs=[whole(s) for s in out],
        out_shape=[jax.ShapeDtypeStruct(s, F32) for s in out],
        scratch_shapes=[
            pltpu.VMEM((rows, hidden), F32),
            pltpu.VMEM((rows, hidden), F32),
            pltpu.VMEM((rows, 2 * hidden), BF),
            pltpu.VMEM((rim + rows, width), F32),
            pltpu.VMEM((rim, width), F32),
            pltpu.VMEM((ROWS, hidden), F32),
            pltpu.VMEM((vocab, width), F32),
        ],
        compiler_params=pltpu.CompilerParams(
            dimension_semantics=("arbitrary",), vmem_limit_bytes=62 * MIB
        ),
        cost_estimate=pl.CostEstimate(
            flops=2 * total * width * (4 * hidden + vocab), bytes_accessed=total * hidden * 16, transcendentals=0
        ),
        name="front_back",
    )(ids, keep, p, q, ds, conv, queue, tab, gains, taps, w_in, g_tab, small)


def place():
    dp = lax.axis_index("dp")
    seq = lax.axis_index("seq")
    return dp // 2, dp % 2, seq // 2, seq % 2


def device(y, x, z, core):
    return (y * 2 + x, z * 2 + core)


def greet(y, x, z, core, depth):
    barrier = pltpu.get_barrier_semaphore()
    peers = [device(1 - y, x, z, core), device(y, 1 - x, z, core)]
    for dz in range(depth):
        for dc in range(2):
            if dz or dc:
                peers.append(device(y, x, (z + dz) % depth, (core + dc) % 2))
    for peer in peers:
        pl.semaphore_signal(barrier, inc=1, device_id=peer, device_id_type=pl.DeviceIdType.MESH)
    pl.semaphore_wait(barrier, len(peers))


def remote(src, dst, send, recv, peer):
    return pltpu.make_async_remote_copy(
        src_ref=src,
        dst_ref=dst,
        send_sem=send,
        recv_sem=recv,
        device_id=peer,
        device_id_type=pl.DeviceIdType.MESH,
    )


def in_order(items, phases, act):
    for time in range(items + phases - 1):
        for phase in range(phases - 1, -1, -1):
            item = time - phase
            if 0 <= item < items:
                act(item, phase)


def gather_kernel(plan, depth, ids, *refs):
    count = 1 + max(p[0] for p in plan)
    srcs = refs[:count]
    ids_o = refs[count]
    outs = refs[count + 1 : 2 * count + 1]
    own_sem, ids_send, ids_recv, send, recv = refs[2 * count + 1 :]
    y, x, z, core = place()
    me = z * 2 + core
    greet(y, x, z, core, depth)
    started = []

    own = [
        pltpu.make_async_copy(srcs[t], outs[t].at[y, x, z, core], own_sem.at[t])
        for t in range(count)
    ]
    own.append(pltpu.make_async_copy(ids.at[me], ids_o.at[me], own_sem.at[count]))
    for copy in own:
        copy.start()
    spread = []
    for dz in range(depth):
        for dc in range(2):
            if dz or dc:
                pz, pc = (z + dz) % depth, (core + dc) % 2
                at = dz * 2 + dc
                copy = remote(
                    ids.at[pz * 2 + pc], ids_o.at[me], ids_send.at[at], ids_recv.at[at], device(y, x, pz, pc)
                )
                copy.start()
                spread.append(copy)
    first = []
    for i, (t, lo, hi, _) in enumerate(plan):
        cols = pl.ds(lo, hi - lo)
        group = []
        for dz in range(1, depth):
            copy = remote(
                srcs[t].at[:, cols],
                outs[t].at[y, x, z, core, :, cols],
                send.at[i, dz - 1],
                recv.at[i, dz - 1],
                device(y, x, (z + dz) % depth, core),
            )
            copy.start()
            group.append(copy)
        first.append(group)
    for copy in own:
        copy.wait()
    held = {}

    def act(i, phase):
        t, lo, hi, along_x = plan[i]
        cols = pl.ds(lo, hi - lo)
        out = outs[t]
        if phase == 0:
            for copy in first[i]:
                copy.wait_recv()
            started.extend(first[i])
            if along_x:
                part, peer = out.at[y, x, :, core, :, cols], device(y, 1 - x, z, core)
            else:
                part, peer = out.at[y, x, :, core, :, cols], device(1 - y, x, z, core)
        else:
            held[i].wait_recv()
            started.append(held[i])
            if phase == 1:
                if along_x:
                    part, peer = out.at[y, :, :, core, :, cols], device(1 - y, x, z, core)
                else:
                    part, peer = out.at[:, x, :, core, :, cols], device(y, 1 - x, z, core)
            elif phase == 2:
                part, peer = out.at[:, :, :, core, :, cols], device(y, x, z, 1 - core)
            else:
                return
        at = depth - 1 + phase
        held[i] = remote(part, part, send.at[i, at], recv.at[i, at], peer)
        held[i].start()

    in_order(len(plan), 4, act)
    for copy in spread:
        copy.wait_recv()
    for copy in spread + started:
        copy.wait_send()


def run_gather(depth, ids, tensors):
    plan = []
    for t, a in enumerate(tensors):
        cols = a.shape[1]
        if a.dtype == F32:
            plan.append((t, 0, cols, True))
        else:
            plan.append((t, 0, cols // 2, True))
            plan.append((t, cols // 2, cols, False))
    any_spec = pl.BlockSpec(memory_space=pl.ANY)
    n = len(tensors)
    return pl.pallas_call(
        functools.partial(gather_kernel, plan, depth),
        in_specs=[any_spec] * (n + 1),
        out_specs=[any_spec] * (n + 1),
        out_shape=[jax.ShapeDtypeStruct(ids.shape, ids.dtype)]
        + [jax.ShapeDtypeStruct((2, 2, depth, 2) + a.shape, a.dtype) for a in tensors],
        scratch_shapes=[
            pltpu.SemaphoreType.DMA((n + 1,)),
            pltpu.SemaphoreType.DMA((2 * depth,)),
            pltpu.SemaphoreType.DMA((2 * depth,)),
            pltpu.SemaphoreType.DMA((len(plan), depth + 2)),
            pltpu.SemaphoreType.DMA((len(plan), depth + 2)),
        ],
        compiler_params=pltpu.CompilerParams(collective_id=0, has_side_effects=True),
        name="gather_weights",
    )(ids, *tensors)


def add_into(target, other, rank):
    lead = target.shape[: len(target.shape) - 2]
    total = 1
    for d in lead:
        total *= d

    def one(i, _):
        index = []
        for d in reversed(lead):
            index.append(lax.rem(i, d))
            i = lax.div(i, d)
        index = tuple(reversed(index))
        target[index] = target[index] + other[index]
        return _

    lax.fori_loop(0, total, one, 0)


def reduce_kernel(plan, depth, tensors, *refs):
    n = len(tensors)
    items = len(plan)
    grads = refs[:n]
    small = refs[n]
    outs = refs[n + 1 : 2 * n + 1]
    small_o, norm_o = refs[2 * n + 1 : 2 * n + 3]
    scratch = refs[2 * n + 3 :]
    sizes = 4
    bufs = [scratch[i * sizes : (i + 1) * sizes] for i in range(items)]
    rest = scratch[items * sizes :]
    small_r, square_s, square_r = rest[0:3]
    own_sem, send, recv, small_send, small_recv, sq_send, sq_recv = rest[3:]
    y, x, z, core = place()
    greet(y, x, z, core, depth)
    started = []
    peer_of = {
        "core": device(y, x, z, 1 - core),
        "x": device(y, 1 - x, z, core),
        "y": device(1 - y, x, z, core),
    }

    loads, held = [], {}
    for i, (t, lo, hi, _) in enumerate(plan):
        cols = pl.ds(lo, hi - lo)
        copy = remote(
            grads[t].at[:, :, :, 1 - core, :, cols], bufs[i][1], send.at[i, 0], recv.at[i, 0], peer_of["core"]
        )
        copy.start()
        held[i] = [copy]
        load = pltpu.make_async_copy(grads[t].at[:, :, :, core, :, cols], bufs[i][0], own_sem.at[i])
        load.start()
        loads.append(load)

    def act(i, phase):
        t, lo, hi, along_x = plan[i]
        whole_b, core_b, half_b, quarter_b = bufs[i]
        for copy in held[i]:
            copy.wait_recv()
        started.extend(held[i])
        if phase == 0:
            loads[i].wait()
            add_into(whole_b, core_b, 3)
            if along_x:
                src, peer = whole_b.at[1 - y], peer_of["y"]
            else:
                src, peer = whole_b.at[:, 1 - x], peer_of["x"]
            held[i] = [remote(src, half_b, send.at[i, 1], recv.at[i, 1], peer)]
        elif phase == 1:
            if along_x:
                add_into(half_b, whole_b.at[y], 2)
                src, peer = half_b.at[1 - x], peer_of["x"]
            else:
                add_into(half_b, whole_b.at[:, x], 2)
                src, peer = half_b.at[1 - y], peer_of["y"]
            held[i] = [remote(src, quarter_b.at[0], send.at[i, 2], recv.at[i, 2], peer)]
        elif phase == 2:
            mine = half_b.at[x] if along_x else half_b.at[y]
            add_into(quarter_b.at[0], mine, 1)
            held[i] = []
            for dz in range(1, depth):
                pz = (z + dz) % depth
                held[i].append(
                    remote(
                        quarter_b.at[0, pz],
                        quarter_b.at[1, dz],
                        send.at[i, 2 + dz],
                        recv.at[i, 2 + dz],
                        device(y, x, pz, core),
                    )
                )
        else:
            total = quarter_b[0, z]
            for dz in range(1, depth):
                total = total + quarter_b[1, dz]
            outs[t][:, lo:hi] = total
            return
        for copy in held[i]:
            copy.start()

    def everywhere(value, slots, sends, recvs):
        slots[0] = value
        for at, name in enumerate(("core", "x", "y")):
            copy = remote(slots.at[2 * at], slots.at[2 * at + 1], sends.at[at], recvs.at[at], peer_of[name])
            copy.start()
            copy.wait()
            slots[2 * at + 2] = slots[2 * at] + slots[2 * at + 1]
        copies = []
        for dz in range(1, depth):
            copy = remote(
                slots.at[6],
                slots.at[7 + z],
                sends.at[2 + dz],
                recvs.at[2 + dz],
                device(y, x, (z + dz) % depth, core),
            )
            copy.start()
            copies.append(copy)
        slots[7 + z] = slots[6]
        for copy in copies:
            copy.wait()
        total = slots[7]
        for dz in range(1, depth):
            total = total + slots[7 + dz]
        return total

    in_order(items, 4, act)
    sums = everywhere(small[...], small_r, small_send, small_recv)
    small_o[...] = sums
    square = jnp.zeros((1, 1), F32)
    for out in outs:
        value = out[...]
        square = square + jnp.sum(jnp.sum(value * value, axis=1, keepdims=True), axis=0, keepdims=True)
    squares = everywhere(jnp.broadcast_to(square, (ROWS, LANES)), square_r, sq_send, sq_recv)
    norm_o[...] = squares
    for copy in started:
        copy.wait_send()


def run_reduce(depth, tensors, small):
    plan = []
    for t, a in enumerate(tensors):
        cols = a.shape[-1]
        plan.append((t, 0, cols // 2, True))
        plan.append((t, cols // 2, cols, False))
    shapes = tuple(a.shape for a in tensors)
    scratch = []
    for t, lo, hi, along_x in plan:
        rows = shapes[t][-2]
        piece = (rows, hi - lo)
        scratch.append(pltpu.VMEM((2, 2, depth) + piece, F32))
        scratch.append(pltpu.VMEM((2, 2, depth) + piece, F32))
        scratch.append(pltpu.VMEM((2, depth) + piece, F32))
        scratch.append(pltpu.VMEM((2, depth) + piece, F32))
    any_spec = pl.BlockSpec(memory_space=pl.ANY)
    vmem = pl.BlockSpec(memory_space=pltpu.VMEM)
    n = len(tensors)
    return pl.pallas_call(
        functools.partial(reduce_kernel, plan, depth, shapes),
        in_specs=[any_spec] * n + [vmem],
        out_specs=[vmem] * (n + 2),
        out_shape=[jax.ShapeDtypeStruct(s[-2:], F32) for s in shapes]
        + [jax.ShapeDtypeStruct(small.shape, F32), jax.ShapeDtypeStruct((ROWS, LANES), F32)],
        scratch_shapes=scratch
        + [
            pltpu.VMEM((7 + depth,) + small.shape, F32),
            pltpu.VMEM((ROWS, LANES), F32),
            pltpu.VMEM((7 + depth, ROWS, LANES), F32),
            pltpu.SemaphoreType.DMA((len(plan),)),
            pltpu.SemaphoreType.DMA((len(plan), depth + 2)),
            pltpu.SemaphoreType.DMA((len(plan), depth + 2)),
            pltpu.SemaphoreType.DMA((depth + 2,)),
            pltpu.SemaphoreType.DMA((depth + 2,)),
            pltpu.SemaphoreType.DMA((depth + 2,)),
            pltpu.SemaphoreType.DMA((depth + 2,)),
        ],
        compiler_params=pltpu.CompilerParams(
            collective_id=1, has_side_effects=True, vmem_limit_bytes=60 * MIB
        ),
        name="reduce_grads",
    )(*tensors, small)


def adam_kernel(shapes, small, squares, count, *refs):
    mats = refs[:5]
    weights, firsts, seconds = refs[5:13], refs[13:21], refs[21:29]
    loss_o, count_o, norm_o = refs[29:32]
    new_w, new_m, new_v = refs[32:40], refs[40:48], refs[48:56]
    kernel, bias_rows = shapes
    width = small.shape[1]
    grads = [m[...] for m in mats]
    grads.append(small[0:3, :])
    grads.append(small[ROWS : ROWS + kernel, :])
    base = ROWS + kernel
    grads.append(
        jnp.concatenate([small[base + r : base + r + 1, :] for r in range(bias_rows)], axis=1)
    )
    square = squares[0:1, 0:1]
    for grad in grads[5:]:
        square = square + jnp.sum(jnp.sum(grad * grad, axis=1, keepdims=True), axis=0, keepdims=True)
    norm = jnp.sqrt(square)
    scale = jnp.minimum(1.0, CLIP / (norm + 1e-06))
    norm_o[...] = norm
    loss_o[...] = small[3:4, 0:1]
    count_o[...] = jnp.sum(count[:, 0:1, 0:1], axis=0)
    for i in range(8):
        rate = RATE_MATRIX if i < 5 else RATE_VECTOR
        decay = WEIGHT_DECAY if i < 5 else 0.0
        w, m, v = adam(weights[i][...], grads[i] * scale, firsts[i][...], seconds[i][...], rate, decay)
        new_w[i][...] = w
        new_m[i][...] = m
        new_v[i][...] = v


def run_adam(shapes, mats, small, squares, count, weights, firsts, seconds):
    one = jax.ShapeDtypeStruct((1, 1), F32)
    like = [jax.ShapeDtypeStruct(w.shape, F32) for w in weights]
    vmem = pl.BlockSpec(memory_space=pltpu.VMEM)
    args = (small, squares, count) + tuple(mats) + tuple(weights) + tuple(firsts) + tuple(seconds)
    return pl.pallas_call(
        functools.partial(adam_kernel, shapes),
        in_specs=[vmem] * len(args),
        out_specs=[vmem] * 27,
        out_shape=[one] * 3 + like * 3,
        compiler_params=pltpu.CompilerParams(vmem_limit_bytes=40 * MIB),
        name="adam_update",
    )(*args)


def spread_ids(tokens, targets, counted, depth):
    seqs, span = tokens.shape
    ways = 2 * depth

    def one(a):
        parts = a.reshape(ways, seqs // ways, 2, span // 2)
        return parts.transpose(0, 3, 2, 1).reshape(ways, 1, -1)

    rows = [one(tokens), one(targets), one(counted)]
    fill = jnp.zeros((ways, ROWS - 3, rows[0].shape[-1]), jnp.int32)
    return jnp.concatenate(rows + [fill], axis=1)


def body_moved(depth, *args):
    tokens, targets, counted = args[:3]
    weights, firsts, seconds = args[3:11], args[11:19], args[19:27]
    table, w_in, w_out, w_up, w_down, gains, conv_taps, gate_bias = weights
    ids = spread_ids(tokens, targets, counted, depth)
    share = jnp.sum(counted.astype(F32))
    first = jnp.concatenate([table, jnp.broadcast_to(share, (table.shape[0], LANES))], axis=1)
    mats = [w[0].astype(BF) for w in (w_in, w_out, w_up, w_down)]
    got = run_gather(depth, ids, [first, mats[0], mats[1], mats[2], mats[3]])
    ids = got[0]
    width = table.shape[1]
    tab = got[1][..., :width].reshape(-1, width)
    count = got[1][..., width:].reshape(-1, table.shape[0], LANES)
    full = [g.reshape(-1, g.shape[-1]) for g in got[2:]]
    taps = conv_taps[0]
    keep, p, q, ds, conv, queue, g_down, g_up, g_out, g_tab, small = run_forward(
        ids, tab, count, gains, taps, gate_bias, *full
    )
    g_in, g_tab, small = run_backward(ids, keep, p, q, ds, conv, queue, tab, gains, taps, full[0], g_tab, small)
    whole_grads = [
        g.reshape((2, 2, depth, 2, -1, g.shape[-1])) for g in (g_tab, g_in, g_out, g_up, g_down)
    ]
    *mats, small, squares = run_reduce(depth, whole_grads, small)
    flat = lambda group: [group[0]] + [a[0] for a in group[1:5]] + [group[5], group[6][0], group[7]]
    out = run_adam(
        (conv_taps.shape[1], gate_bias.shape[1] // width),
        mats, small, squares, count, flat(weights), flat(firsts), flat(seconds),
    )
    shaped = [o.reshape(()) for o in out[:3]]
    for i, o in enumerate(out[3:]):
        shaped.append(o.reshape(weights[i % 8].shape))
    return tuple(shaped)


def choose(mesh, *args):
    ways = mesh.shape["seq"]
    seqs, span = args[0].shape
    if mesh.shape["dp"] == 4 and ways == 8 and seqs == 4 * ways and span == LANES:
        return body_moved(ways // 2, *args)
    return body(*args)


def solution(mesh):
    return jax.shard_map(
        functools.partial(choose, mesh),
        mesh=mesh,
        in_specs=(
            P("dp", "seq"),
            P("dp", "seq"),
            P("dp", "seq"),
            P(("dp", "seq"), None),
            P(None, ("dp", "seq"), None),
            P(None, ("dp", "seq"), None),
            P(None, ("dp", "seq"), None),
            P(None, ("dp", "seq"), None),
            P(),
            P(),
            P(),
            P(("dp", "seq"), None),
            P(None, ("dp", "seq"), None),
            P(None, ("dp", "seq"), None),
            P(None, ("dp", "seq"), None),
            P(None, ("dp", "seq"), None),
            P(),
            P(),
            P(),
            P(("dp", "seq"), None),
            P(None, ("dp", "seq"), None),
            P(None, ("dp", "seq"), None),
            P(None, ("dp", "seq"), None),
            P(None, ("dp", "seq"), None),
            P(),
            P(),
            P(),
        ),
        out_specs=(
            P(),
            P(),
            P(),
            P(("dp", "seq"), None),
            P(None, ("dp", "seq"), None),
            P(None, ("dp", "seq"), None),
            P(None, ("dp", "seq"), None),
            P(None, ("dp", "seq"), None),
            P(),
            P(),
            P(),
            P(("dp", "seq"), None),
            P(None, ("dp", "seq"), None),
            P(None, ("dp", "seq"), None),
            P(None, ("dp", "seq"), None),
            P(None, ("dp", "seq"), None),
            P(),
            P(),
            P(),
            P(("dp", "seq"), None),
            P(None, ("dp", "seq"), None),
            P(None, ("dp", "seq"), None),
            P(None, ("dp", "seq"), None),
            P(None, ("dp", "seq"), None),
            P(),
            P(),
            P(),
        ),
        check_vma=False,
    )
```

```python
import functools

import jax
import jax.numpy as jnp
from jax import lax
from jax.experimental import pallas as pl
from jax.experimental.pallas import tpu as pltpu
from jax.sharding import PartitionSpec as P

V = 256
MICRO = 2
STEP = 3


EPS = 1e-06
CLIP = 0.01
BETA_ONE = 0.5
BETA_TWO = 0.5
ADAM_EPS = 1e-08
RATE_MATRIX = 0.03
RATE_VECTOR = 0.3
WEIGHT_DECAY = 0.1


def from_behind(x, axis, by):
    devices = lax.axis_size(axis)
    pairs = [(i, i + by) for i in range(devices) if 0 <= i + by < devices]
    return lax.ppermute(x, axis, pairs)


def carried_in(part, axis, combine, identity, reverse):
    count = lax.axis_size(axis)
    place = lax.axis_index(axis)
    ahead = count - 1 - place if reverse else place
    gathered = jax.tree.map(lambda a: lax.all_gather(a, axis), part)
    state = jax.tree.map(lambda a, e: jnp.zeros_like(a) + jnp.asarray(e, a.dtype), part, identity)

    def one(lap, state):
        source = count - 1 - lap if reverse else lap
        return combine(
            state, jax.tree.map(lambda a: lax.dynamic_index_in_dim(a, source, 0, False), gathered)
        )

    return lax.fori_loop(0, ahead, one, state)


def matmul(left, right):
    return jnp.dot(left, right, preferred_element_type=jnp.float32)


def matmul_tn(left, right):
    return lax.dot_general(
        left, right, (((0,), (0,)), ((), ())), preferred_element_type=jnp.float32
    )


def matmul_nt(left, right):
    return lax.dot_general(
        left, right, (((1,), (1,)), ((), ())), preferred_element_type=jnp.float32
    )


def rms_norm(values, gain):
    return values * lax.rsqrt(jnp.mean(values * values, axis=-1, keepdims=True) + EPS) * gain


def combine(earlier, later):
    return (earlier[0] * later[0], later[0] * earlier[1] + later[1])


def gates(gate, cand):
    return (jax.nn.sigmoid(-gate), jax.nn.sigmoid(gate) * jax.nn.softplus(cand))


def conv_apply(padded, taps, length):
    total = taps[0] * padded[0:length].astype(jnp.float32)
    for k in range(1, taps.shape[0]):
        total = total + taps[k] * padded[k : k + length].astype(jnp.float32)
    return total


def adam(weight, grad, first, second, rate, decay):
    first = BETA_ONE * first + (1.0 - BETA_ONE) * grad
    second = BETA_TWO * second + (1.0 - BETA_TWO) * grad * grad
    fix_one = 1.0 - BETA_ONE**STEP
    fix_two = 1.0 - BETA_TWO**STEP
    update = first / fix_one / (jnp.sqrt(second / fix_two) + ADAM_EPS)
    return (weight - rate * (update + decay * weight), first, second)


def mixer_front(queue, rim, taps, bias, w_in):
    span, seqs, width = queue.shape
    padded = jnp.concatenate([rim, queue], axis=0)
    conv_low = conv_apply(padded, taps, span).astype(jnp.bfloat16)
    pre = matmul(conv_low.reshape(span * seqs, width), w_in).reshape(span, seqs, -1)
    hidden = bias.shape[0]
    keep, write = gates(pre[..., :hidden] + bias, pre[..., hidden:])
    return (padded, conv_low, pre, keep, write)


def block_tail(state, resid, gain_b, w_out, w_up, w_down):
    span, seqs, width = resid.shape
    state_low = state.astype(jnp.bfloat16).reshape(span * seqs, -1)
    mixed = resid + matmul(state_low, w_out).reshape(span, seqs, width)
    normed_low = rms_norm(mixed, gain_b).astype(jnp.bfloat16).reshape(span * seqs, width)
    lifted = matmul(normed_low, w_up)
    active_low = jax.nn.gelu(lifted).astype(jnp.bfloat16)
    result = mixed + matmul(active_low, w_down).reshape(span, seqs, width)
    return (result, (state_low, mixed, normed_low, lifted, active_low))


def layer_forward(resid, taps, gain_a, gain_b, bias, mats):
    span = resid.shape[0]
    kernel = taps.shape[0]
    queue = rms_norm(resid, gain_a).astype(jnp.bfloat16)
    rim = from_behind(queue[span - kernel + 1 :], "seq", 1)
    padded, conv_low, pre, keep, write = mixer_front(queue, rim, taps, bias, mats[0])
    decay, local = lax.associative_scan(combine, (keep, write), axis=0)
    ones = jnp.ones_like(local[0])
    carry_in = carried_in(
        (decay[-1], local[-1]), "seq", combine, (ones, jnp.zeros_like(ones)), False
    )[1]
    state = local + decay * carry_in[None]
    result, unused = block_tail(state, resid, gain_b, mats[1], mats[2], mats[3])
    return (result, rim, carry_in)


def layer_backward(grad, resid, rim, carry_in, taps, gain_a, gain_b, bias, mats):
    w_in, w_out, w_up, w_down = mats
    span, seqs, width = resid.shape
    kernel = taps.shape[0]
    hidden = bias.shape[0]
    normed_a, norm_back = jax.vjp(rms_norm, resid, gain_a)
    queue = normed_a.astype(jnp.bfloat16)
    padded, conv_low, pre, keep, write = mixer_front(queue, rim, taps, bias, w_in)
    decay, local = lax.associative_scan(combine, (keep, write), axis=0)
    state = local + decay * carry_in[None]
    result, (state_low, mixed, normed_low, lifted, active_low) = block_tail(
        state, resid, gain_b, w_out, w_up, w_down
    )
    grad_low = grad.astype(jnp.bfloat16).reshape(span * seqs, width)
    g_down = matmul_tn(active_low, grad_low)
    d_active = matmul_nt(grad_low, w_down)
    d_lifted_low = jax.vjp(jax.nn.gelu, lifted)[1](d_active)[0].astype(jnp.bfloat16)
    g_up = matmul_tn(normed_low, d_lifted_low)
    d_normed = matmul_nt(d_lifted_low, w_up).reshape(span, seqs, width)
    d_mixed, d_gain_b = jax.vjp(rms_norm, mixed, gain_b)[1](d_normed)
    d_mixed = grad + d_mixed
    mixed_low = d_mixed.astype(jnp.bfloat16).reshape(span * seqs, width)
    g_out = matmul_tn(state_low, mixed_low)
    d_state = matmul_nt(mixed_low, w_out).reshape(span, seqs, hidden)
    follow = jnp.concatenate([keep[1:], jnp.ones_like(keep[:1])], axis=0)
    reach, back_local = lax.associative_scan(combine, (follow, d_state), axis=0, reverse=True)
    ones = jnp.ones_like(keep[0])
    summary = (keep[0] * reach[0], keep[0] * back_local[0])
    carry_out = carried_in(summary, "seq", combine, (ones, jnp.zeros_like(ones)), True)[1]
    adjoint = back_local + reach * carry_out[None]
    before = jnp.concatenate([carry_in[None], state[:-1]], axis=0)
    d_gate, d_cand = jax.vjp(gates, pre[..., :hidden] + bias, pre[..., hidden:])[1](
        (adjoint * before, adjoint)
    )
    d_bias = jnp.sum(d_gate, axis=(0, 1))
    d_pre = (
        jnp.concatenate([d_gate, d_cand], axis=-1)
        .astype(jnp.bfloat16)
        .reshape(span * seqs, 2 * hidden)
    )
    g_in = matmul_tn(conv_low.reshape(span * seqs, width), d_pre)
    d_conv = matmul_nt(d_pre, w_in).reshape(span, seqs, width)
    beyond = from_behind(d_conv[: kernel - 1].astype(jnp.bfloat16), "seq", -1).astype(jnp.float32)
    extended = jnp.concatenate([d_conv, beyond], axis=0)
    d_queue = taps[0] * extended[kernel - 1 : kernel - 1 + span]
    tap_grads = [jnp.sum(d_conv * padded[0:span].astype(jnp.float32), axis=(0, 1))]
    for k in range(1, kernel):
        d_queue = d_queue + taps[k] * extended[kernel - 1 - k : kernel - 1 - k + span]
        tap_grads.append(jnp.sum(d_conv * padded[k : k + span].astype(jnp.float32), axis=(0, 1)))
    rounded = lax.optimization_barrier(d_queue.astype(jnp.bfloat16)).astype(jnp.float32)
    d_resid, d_gain_a = norm_back(rounded)
    return (
        d_mixed + d_resid,
        (g_in, g_out, g_up, g_down),
        (jnp.stack(tap_grads), d_gain_a, d_gain_b, d_bias),
    )


def body(
    tokens,
    targets,
    counted,
    table,
    w_in,
    w_out,
    w_up,
    w_down,
    gains,
    conv_taps,
    gate_bias,
    m_table,
    m_in,
    m_out,
    m_up,
    m_down,
    m_gains,
    m_taps,
    m_bias,
    v_table,
    v_in,
    v_out,
    v_up,
    v_down,
    v_gains,
    v_taps,
    v_bias,
):
    layers = w_in.shape[0]
    seq_dev, span = tokens.shape
    rows = seq_dev // MICRO
    width = table.shape[1]
    vocab = V
    mask = counted.astype(jnp.float32)
    count = lax.psum(jnp.sum(mask), ("dp", "seq"))
    shards = (
        w_in.astype(jnp.bfloat16),
        w_out.astype(jnp.bfloat16),
        w_up.astype(jnp.bfloat16),
        w_down.astype(jnp.bfloat16),
    )
    layer_gains = gains[: 2 * layers].reshape(layers, 2, width)
    columns = jnp.arange(vocab, dtype=jnp.int32)

    def forward_step(resid, inputs):
        pieces, taps, pair, bias = inputs
        mats = (
            lax.all_gather(pieces[0], ("dp", "seq"), axis=0, tiled=True),
            lax.all_gather(pieces[1], ("dp", "seq"), axis=0, tiled=True),
            lax.all_gather(pieces[2], ("dp", "seq"), axis=0, tiled=True),
            lax.all_gather(pieces[3], ("dp", "seq"), axis=0, tiled=True),
        )
        result, rim, carry_in = layer_forward(resid, taps, pair[0], pair[1], bias, mats)
        return (result, (resid, rim, carry_in))

    def backward_step(grad, inputs):
        saved, pieces, taps, pair, bias = inputs
        mats = (
            lax.all_gather(pieces[0], ("dp", "seq"), axis=0, tiled=True),
            lax.all_gather(pieces[1], ("dp", "seq"), axis=0, tiled=True),
            lax.all_gather(pieces[2], ("dp", "seq"), axis=0, tiled=True),
            lax.all_gather(pieces[3], ("dp", "seq"), axis=0, tiled=True),
        )
        grad, full, small = layer_backward(
            grad, saved[0], saved[1], saved[2], taps, pair[0], pair[1], bias, mats
        )
        full = (
            lax.psum_scatter(full[0], ("dp", "seq"), scatter_dimension=0, tiled=True),
            lax.psum_scatter(full[1], ("dp", "seq"), scatter_dimension=0, tiled=True),
            lax.psum_scatter(full[2], ("dp", "seq"), scatter_dimension=0, tiled=True),
            lax.psum_scatter(full[3], ("dp", "seq"), scatter_dimension=0, tiled=True),
        )
        return (grad, (full, small))

    loss = jnp.zeros((), jnp.float32)
    g_table = jnp.zeros((vocab, width), jnp.float32)
    acc_full = None
    acc_small = None
    for index in range(MICRO):
        tok = tokens[index * rows : (index + 1) * rows].T.reshape(-1)
        tgt = targets[index * rows : (index + 1) * rows].T.reshape(-1)
        weights = mask[index * rows : (index + 1) * rows].T.reshape(-1)
        tab = lax.all_gather(table.astype(jnp.bfloat16), ("dp", "seq"), axis=0, tiled=True)
        picks = tok[:, None] == columns[None, :]
        resid = matmul(picks.astype(jnp.bfloat16), tab).reshape(span, rows, width)
        final, saved = lax.scan(forward_step, resid, (shards, conv_taps, layer_gains, gate_bias))
        normed_f, final_back = jax.vjp(rms_norm, final, gains[2 * layers])
        normed_low = normed_f.astype(jnp.bfloat16).reshape(span * rows, width)
        logits = matmul_nt(normed_low, tab)
        top = jnp.max(logits, axis=-1, keepdims=True)
        lse = jnp.log(jnp.sum(jnp.exp(logits - top), axis=-1)) + top[:, 0]
        hits = (tgt[:, None] == columns[None, :]).astype(jnp.float32)
        picked = jnp.sum(hits * logits, axis=-1)
        loss = loss + jnp.sum(weights * (lse - picked))
        d_logits = ((jnp.exp(logits - lse[:, None]) - hits) * (weights / count)[:, None]).astype(
            jnp.bfloat16
        )
        g_table = g_table + matmul_tn(d_logits, normed_low)
        d_normed = matmul(d_logits, tab).reshape(span, rows, width)
        d_final, d_gain_f = final_back(d_normed)
        grad0, (full, small) = lax.scan(
            backward_step, d_final, (saved, shards, conv_taps, layer_gains, gate_bias), reverse=True
        )
        g_table = g_table + lax.dot_general(
            picks.astype(jnp.float32),
            grad0.reshape(span * rows, width),
            (((0,), (0,)), ((), ())),
            precision=lax.Precision.HIGHEST,
        )
        layer_gain_grads = jnp.stack([small[1], small[2]], axis=1).reshape(2 * layers, width)
        vectors = (jnp.concatenate([layer_gain_grads, d_gain_f[None]], axis=0), small[0], small[3])
        if index == 0:
            acc_full, acc_small = (full, vectors)
        else:
            acc_full = jax.tree.map(lambda a, b: a + b, acc_full, full)
            acc_small = jax.tree.map(lambda a, b: a + b, acc_small, vectors)
    table_shard = lax.psum_scatter(g_table, ("dp", "seq"), scatter_dimension=0, tiled=True)
    g_gains, g_taps, g_bias = lax.psum((acc_small[0], acc_small[1], acc_small[2]), ("dp", "seq"))
    matrices = (table_shard, acc_full[0], acc_full[1], acc_full[2], acc_full[3])
    squares = jnp.zeros((), jnp.float32)
    for grad in matrices:
        squares = squares + jnp.sum(grad * grad)
    squares_all, loss_all = lax.psum((squares, loss), ("dp", "seq"))
    small_squares = jnp.sum(g_gains * g_gains) + jnp.sum(g_taps * g_taps) + jnp.sum(g_bias * g_bias)
    norm = jnp.sqrt(squares_all + small_squares)
    scale = jnp.minimum(1.0, CLIP / (norm + 1e-06))
    params = (table, w_in, w_out, w_up, w_down, gains, conv_taps, gate_bias)
    grads = matrices + (g_gains, g_taps, g_bias)
    firsts = (m_table, m_in, m_out, m_up, m_down, m_gains, m_taps, m_bias)
    seconds = (v_table, v_in, v_out, v_up, v_down, v_gains, v_taps, v_bias)
    news, next_m, next_v = ([], [], [])
    for index in range(8):
        rate = RATE_MATRIX if index < 5 else RATE_VECTOR
        decay = WEIGHT_DECAY if index < 5 else 0.0
        weight, first, second = adam(
            params[index], grads[index] * scale, firsts[index], seconds[index], rate, decay
        )
        news.append(weight)
        next_m.append(first)
        next_v.append(second)
    return (
        loss_all,
        count,
        norm,
        news[0],
        news[1],
        news[2],
        news[3],
        news[4],
        news[5],
        news[6],
        news[7],
        next_m[0],
        next_m[1],
        next_m[2],
        next_m[3],
        next_m[4],
        next_m[5],
        next_m[6],
        next_m[7],
        next_v[0],
        next_v[1],
        next_v[2],
        next_v[3],
        next_v[4],
        next_v[5],
        next_v[6],
        next_v[7],
    )


BF = jnp.bfloat16
F32 = jnp.float32
MIB = 1 << 20
LANES = 128
ROWS = 8
GELU_A = 0.7978845608028654
GELU_B = 0.044715


def nn(left, right):
    return jnp.dot(left, right, preferred_element_type=F32)


def tn(left, right):
    return lax.dot_general(left, right, (((0,), (0,)), ((), ())), preferred_element_type=F32)


def nt(left, right):
    return lax.dot_general(left, right, (((1,), (1,)), ((), ())), preferred_element_type=F32)


def inv_rms(values):
    return lax.rsqrt(jnp.mean(values * values, axis=-1, keepdims=True) + EPS)


def norm_back(values, inverse, gain, grad):
    width = values.shape[-1]
    scaled = grad * gain
    dot = jnp.sum(scaled * values, axis=-1, keepdims=True)
    return inverse * scaled - values * (inverse * inverse * inverse * dot * (1.0 / width))


def column_sum(values):
    return jnp.sum(values, axis=0, keepdims=True)


def swap_halves(tile):
    return pltpu.roll(tile, ROWS // 2, tile.ndim - 2)


def one_hot(column, vocab):
    lane = lax.broadcasted_iota(jnp.int32, (column.shape[0], vocab), 1)
    return (column == lane).astype(F32).astype(BF)


def one_hot_t(row, vocab):
    place = lax.broadcasted_iota(jnp.int32, (vocab, row.shape[1]), 0)
    return (row == place).astype(F32).astype(BF)


def forward_kernel(
    ids, tab, count, gains, taps, bias, w_in, w_out, w_up, w_down,
    keep_o, p_o, q_o, ds_o, conv_o, queue_o, g_down, g_up, g_out, g_tab, small_o,
    tab_low, qtab, padq, tail_s, carry_s, big, state_low, active, mixed_s, normed_s,
):
    step = pl.program_id(0)
    rows, hidden = keep_o.shape
    vocab, width = tab.shape
    ff = w_up.shape[1]
    kernel = taps.shape[0]
    rim = (kernel - 1) * ROWS
    steps = rows // ROWS
    chunk = 256

    @pl.when(step == 0)
    def _():
        low = tab[...].astype(BF)
        tab_low[...] = low
        wide = low.astype(F32)
        qtab[...] = (wide * inv_rms(wide) * gains[0:1]).astype(BF)
        g_down[...] = jnp.zeros_like(g_down)
        g_up[...] = jnp.zeros_like(g_up)
        g_out[...] = jnp.zeros_like(g_out)
        g_tab[...] = jnp.zeros_like(g_tab)
        small_o[...] = jnp.zeros_like(small_o)
        tail_s[...] = jnp.zeros_like(tail_s)
        carry_s[...] = jnp.zeros_like(carry_s)

    wide_ids = ids[0]
    columns = wide_ids.T
    hot = one_hot(columns[:, 0:1], vocab)
    queue = nn(hot, qtab[...])
    queue_o[...] = queue.astype(BF)
    padq[rim:, :] = queue
    half = (
        lax.broadcasted_iota(jnp.int32, (rim, width), 0) % ROWS < ROWS // 2
    )
    before = tail_s[...].reshape(kernel - 1, ROWS, width)
    latest = padq[rows:, :].reshape(kernel - 1, ROWS, width)
    padq[0:rim, :] = jnp.where(
        half, swap_halves(before).reshape(rim, width), swap_halves(latest).reshape(rim, width)
    )
    tail_s[...] = padq[rows:, :]
    conv = taps[0:1] * padq[0:rows, :]
    for k in range(1, kernel):
        conv = conv + taps[k : k + 1] * padq[k * ROWS : k * ROWS + rows, :]
    conv_o[...] = conv.astype(BF)

    for j in range(hidden // chunk):
        cols = slice(j * chunk, (j + 1) * chunk)
        gate = nn(conv_o[...], w_in[:, j * chunk : (j + 1) * chunk]) + bias[0:1, cols]
        cand = nn(conv_o[...], w_in[:, hidden + j * chunk : hidden + (j + 1) * chunk])
        eg = jnp.exp(-jnp.abs(gate))
        rg = pl.reciprocal(1.0 + eg)
        sg = eg * rg
        up = gate >= 0
        write_gate = jnp.where(up, rg, sg)
        keep_o[:, cols] = jnp.where(up, sg, rg)
        ec = jnp.exp(-jnp.abs(cand))
        rc = pl.reciprocal(1.0 + ec)
        slope = jnp.where(cand >= 0, rc, ec * rc)
        soft = jnp.maximum(cand, 0.0) + jnp.where(
            ec < 1e-3, ec * (1.0 - 0.5 * ec), jnp.log(1.0 + ec)
        )
        p_o[:, cols] = write_gate
        q_o[:, cols] = write_gate * slope
        big[:, cols] = write_gate * soft

    low_half = lax.broadcasted_iota(jnp.int32, (ROWS, hidden), 0) < ROWS // 2
    carry = carry_s[...]
    ones = jnp.where(low_half, 0.0, 1.0)

    def scan_one(tau, held):
        state, reach = held
        at = pl.ds(pl.multiple_of(tau * ROWS, ROWS), ROWS)
        keep = keep_o[at, :]
        state = keep * state + big[at, 0:hidden]
        reach = keep * reach
        ds_o[at, :] = state
        big[at, hidden : 2 * hidden] = reach
        return state, reach

    end, _ = lax.fori_loop(0, steps, scan_one, (carry, ones), unroll=4)
    entry = jnp.where(low_half, 0.0, swap_halves(end))

    def fix_one(pair, previous):
        lows = []
        for half_step in range(2):
            at = pl.ds(pl.multiple_of(pair * 2 * ROWS + half_step * ROWS, ROWS), ROWS)
            state = ds_o[at, :] + big[at, hidden : 2 * hidden] * entry
            p_o[at, :] = keep_o[at, :] * (big[at, 0:hidden] - p_o[at, :] * previous)
            previous = state
            lows.append(state)
        both = pl.ds(pl.multiple_of(pair * 2 * ROWS, 2 * ROWS), 2 * ROWS)
        state_low[both, :] = jnp.concatenate(lows, axis=0).astype(BF)
        return previous

    last = lax.fori_loop(
        0, steps // 2, fix_one, jnp.where(low_half, carry, entry), unroll=4
    )
    carry_s[...] = jnp.where(low_half, swap_halves(last), 0.0)

    mixed = nn(hot, tab_low[...]) + nn(state_low[...], w_out[...])
    mixed_s[...] = mixed
    inverse_b = inv_rms(mixed)
    normed_s[...] = (mixed * inverse_b * gains[1:2]).astype(BF)
    for j in range(ff // chunk):
        cols = slice(j * chunk, (j + 1) * chunk)
        lifted = nn(normed_s[...], w_up[:, cols])
        square = lifted * lifted
        curve = jnp.tanh(lifted * (GELU_A + (GELU_A * GELU_B) * square))
        cdf = 0.5 + 0.5 * curve
        active[:, cols] = (lifted * cdf).astype(BF)
        big[:, cols] = cdf + (0.5 * lifted) * (1.0 - curve * curve) * (
            GELU_A + (3.0 * GELU_A * GELU_B) * square
        )
    result = mixed + nn(active[...], w_down[...])
    inverse_f = inv_rms(result)
    unit_f = result * inverse_f
    normed_f = (unit_f * gains[2:3]).astype(BF)

    logits = nt(normed_f, tab_low[...])
    top = jnp.max(logits, axis=-1, keepdims=True)
    powers = jnp.exp(logits - top)
    total = jnp.sum(powers, axis=-1, keepdims=True)
    lse = jnp.log(total) + top
    target = columns[:, 1:2] == lax.broadcasted_iota(jnp.int32, (rows, vocab), 1)
    picked = jnp.sum(jnp.where(target, logits, 0.0), axis=-1, keepdims=True)
    weight = columns[:, 2:3].astype(F32)
    loss = column_sum(weight * (lse - picked))
    share = weight * (1.0 / jnp.sum(count[:, 0:1, 0:1]))
    d_logits = ((powers * (1.0 / total) - jnp.where(target, 1.0, 0.0)) * share).astype(BF)
    g_tab[...] += tn(d_logits, normed_f)
    d_normed_f = nn(d_logits, tab_low[...])
    small_o[2:3, :] += column_sum(d_normed_f * unit_f)
    small_o[3:4, :] += jnp.broadcast_to(loss, (1, width))
    d_final = norm_back(result, inverse_f, gains[2:3], d_normed_f)
    grad_low = d_final.astype(BF)

    for j in range(ff // chunk):
        cols = slice(j * chunk, (j + 1) * chunk)
        d_active = nt(grad_low, w_down[cols, :])
        g_down[cols, :] += tn(active[:, cols], grad_low)
        active[:, cols] = (d_active * big[:, cols]).astype(BF)
    g_up[...] += tn(normed_s[...], active[...])
    d_normed = nt(active[...], w_up[...])
    mixed = mixed_s[...]
    inverse_b = inv_rms(mixed)
    small_o[1:2, :] += column_sum(d_normed * (mixed * inverse_b))
    d_mixed = d_final + norm_back(mixed, inverse_b, gains[1:2], d_normed)
    mixed_low = d_mixed.astype(BF)
    rest = (d_mixed - mixed_low.astype(F32)).astype(BF)
    g_out[...] += tn(state_low[...], mixed_low)
    ds_o[...] = nt(mixed_low, w_out[...])
    hot_t = one_hot_t(wide_ids[0:1, :], vocab)
    g_tab[...] += nn(hot_t, mixed_low) + nn(hot_t, rest)


def whole(shape):
    zeros = (0,) * len(shape)
    return pl.BlockSpec(shape, lambda i: zeros, pipeline_mode=pl.Buffered(1))


def run_forward(ids, tab, count, gains, taps, bias, w_in, w_out, w_up, w_down):
    blocks, _, rows = ids.shape
    vocab, width = tab.shape
    hidden = w_out.shape[0]
    ff = w_up.shape[1]
    kernel = taps.shape[0]
    total = blocks * rows
    rim = (kernel - 1) * ROWS
    wide = pl.BlockSpec((rows, hidden), lambda i: (i, 0))
    thin = pl.BlockSpec((rows, width), lambda i: (i, 0))
    macs = 3 * (width * 2 * hidden // 3 + hidden * width + 2 * width * ff + vocab * width) + 4 * vocab * width
    return pl.pallas_call(
        forward_kernel,
        grid=(blocks,),
        in_specs=[pl.BlockSpec((1, ROWS, rows), lambda i: (i, 0, 0))]
        + [whole(a.shape) for a in (tab, count, gains, taps, bias, w_in, w_out, w_up, w_down)],
        out_specs=[wide, wide, wide, wide, thin, thin]
        + [whole(s) for s in ((ff, width), (width, ff), (hidden, width), (vocab, width), (ROWS, width))],
        out_shape=[jax.ShapeDtypeStruct((total, hidden), F32)] * 4
        + [jax.ShapeDtypeStruct((total, width), BF)] * 2
        + [
            jax.ShapeDtypeStruct(s, F32)
            for s in ((ff, width), (width, ff), (hidden, width), (vocab, width), (ROWS, width))
        ],
        scratch_shapes=[
            pltpu.VMEM((vocab, width), BF),
            pltpu.VMEM((vocab, width), BF),
            pltpu.VMEM((rim + rows, width), F32),
            pltpu.VMEM((rim, width), F32),
            pltpu.VMEM((ROWS, hidden), F32),
            pltpu.VMEM((rows, max(ff, 2 * hidden)), F32),
            pltpu.VMEM((rows, hidden), BF),
            pltpu.VMEM((rows, ff), BF),
            pltpu.VMEM((rows, width), F32),
            pltpu.VMEM((rows, width), BF),
        ],
        compiler_params=pltpu.CompilerParams(
            dimension_semantics=("arbitrary",), vmem_limit_bytes=62 * MIB
        ),
        cost_estimate=pl.CostEstimate(
            flops=2 * macs * total, bytes_accessed=total * hidden * 16, transcendentals=total * (5 * hidden + ff)
        ),
        name="forward_and_tail_back",
    )(ids, tab, count, gains, taps, bias, w_in, w_out, w_up, w_down)


def place():
    dp = lax.axis_index("dp")
    seq = lax.axis_index("seq")
    return dp // 2, dp % 2, seq // 2, seq % 2


def device(y, x, z, core):
    return (y * 2 + x, z * 2 + core)


def greet(y, x, z, core, depth):
    barrier = pltpu.get_barrier_semaphore()
    peers = [device(1 - y, x, z, core), device(y, 1 - x, z, core)]
    for dz in range(depth):
        for dc in range(2):
            if dz or dc:
                peers.append(device(y, x, (z + dz) % depth, (core + dc) % 2))
    for peer in peers:
        pl.semaphore_signal(barrier, inc=1, device_id=peer, device_id_type=pl.DeviceIdType.MESH)
    pl.semaphore_wait(barrier, len(peers))


def remote(src, dst, send, recv, peer):
    return pltpu.make_async_remote_copy(
        src_ref=src,
        dst_ref=dst,
        send_sem=send,
        recv_sem=recv,
        device_id=peer,
        device_id_type=pl.DeviceIdType.MESH,
    )


def in_order(groups, phases, act):
    for time in range(len(groups) + phases - 1):
        for phase in range(phases - 1, -1, -1):
            at = time - phase
            if 0 <= at < len(groups):
                for item in groups[at]:
                    act(item, phase)


def grouped(plan):
    groups = {}
    for i, part in enumerate(plan):
        groups.setdefault(part[0], []).append(i)
    return list(groups.values())


def gather_kernel(plan, depth, ids, *refs):
    count = 1 + max(p[0] for p in plan)
    srcs = refs[:count]
    ids_o = refs[count]
    outs = refs[count + 1 : 2 * count + 1]
    own_sem, ids_send, ids_recv, send, recv = refs[2 * count + 1 :]
    y, x, z, core = place()
    me = z * 2 + core
    greet(y, x, z, core, depth)
    started = []

    own = [
        pltpu.make_async_copy(srcs[t], outs[t].at[y, x, z, core], own_sem.at[t])
        for t in range(count)
    ]
    own.append(pltpu.make_async_copy(ids.at[me], ids_o.at[me], own_sem.at[count]))
    for copy in own:
        copy.start()
    spread = []
    for dz in range(depth):
        for dc in range(2):
            if dz or dc:
                pz, pc = (z + dz) % depth, (core + dc) % 2
                at = dz * 2 + dc
                copy = remote(
                    ids.at[pz * 2 + pc], ids_o.at[me], ids_send.at[at], ids_recv.at[at], device(y, x, pz, pc)
                )
                copy.start()
                spread.append(copy)
    first = []
    for i, (t, lo, hi, _) in enumerate(plan):
        cols = pl.ds(lo, hi - lo)
        group = []
        for dz in range(1, depth):
            copy = remote(
                srcs[t].at[:, cols],
                outs[t].at[y, x, z, core, :, cols],
                send.at[i, dz - 1],
                recv.at[i, dz - 1],
                device(y, x, (z + dz) % depth, core),
            )
            copy.start()
            group.append(copy)
        first.append(group)
    for copy in own:
        copy.wait()
    held = {}

    def act(i, phase):
        t, lo, hi, along_x = plan[i]
        cols = pl.ds(lo, hi - lo)
        out = outs[t]
        if phase == 0:
            for copy in first[i]:
                copy.wait_recv()
            started.extend(first[i])
            if along_x:
                part, peer = out.at[y, x, :, core, :, cols], device(y, 1 - x, z, core)
            else:
                part, peer = out.at[y, x, :, core, :, cols], device(1 - y, x, z, core)
        else:
            held[i].wait_recv()
            started.append(held[i])
            if phase == 1:
                if along_x:
                    part, peer = out.at[y, :, :, core, :, cols], device(1 - y, x, z, core)
                else:
                    part, peer = out.at[:, x, :, core, :, cols], device(y, 1 - x, z, core)
            elif phase == 2:
                part, peer = out.at[:, :, :, core, :, cols], device(y, x, z, 1 - core)
            else:
                return
        at = depth - 1 + phase
        held[i] = remote(part, part, send.at[i, at], recv.at[i, at], peer)
        held[i].start()

    in_order(grouped(plan), 4, act)
    for copy in spread:
        copy.wait_recv()
    for copy in spread + started:
        copy.wait_send()


def run_gather(depth, ids, tensors):
    plan = []
    for t, a in enumerate(tensors):
        cols = a.shape[1]
        if a.dtype == F32:
            plan.append((t, 0, cols, True))
        else:
            plan.append((t, 0, cols // 2, True))
            plan.append((t, cols // 2, cols, False))
    any_spec = pl.BlockSpec(memory_space=pl.ANY)
    n = len(tensors)
    return pl.pallas_call(
        functools.partial(gather_kernel, plan, depth),
        in_specs=[any_spec] * (n + 1),
        out_specs=[any_spec] * (n + 1),
        out_shape=[jax.ShapeDtypeStruct(ids.shape, ids.dtype)]
        + [jax.ShapeDtypeStruct((2, 2, depth, 2) + a.shape, a.dtype) for a in tensors],
        scratch_shapes=[
            pltpu.SemaphoreType.DMA((n + 1,)),
            pltpu.SemaphoreType.DMA((2 * depth,)),
            pltpu.SemaphoreType.DMA((2 * depth,)),
            pltpu.SemaphoreType.DMA((len(plan), depth + 2)),
            pltpu.SemaphoreType.DMA((len(plan), depth + 2)),
        ],
        compiler_params=pltpu.CompilerParams(collective_id=0, has_side_effects=True),
        name="gather_weights",
    )(ids, *tensors)


def add_into(target, other):
    lead = target.shape[: len(target.shape) - 2]
    total = 1
    for d in lead:
        total *= d

    def one(i, _):
        index = []
        for d in reversed(lead):
            index.append(lax.rem(i, d))
            i = lax.div(i, d)
        index = tuple(reversed(index))
        target[index] = target[index] + other[index]
        return _

    lax.fori_loop(0, total, one, 0)


def halves(shapes, start=0):
    plan = []
    for t, shape in enumerate(shapes):
        cols = shape[-1]
        plan.append((t + start, 0, cols // 2, True))
        plan.append((t + start, cols // 2, cols, False))
    return plan


class Reduce:
    def __init__(self, plan, depth, sources, resident, outs, bufs, loads, send, recv, at):
        self.plan, self.depth, self.sources, self.resident = plan, depth, sources, resident
        self.outs, self.bufs, self.loads, self.send, self.recv = outs, bufs, loads, send, recv
        self.y, self.x, self.z, self.core = at

    def sizes(shape, lo, hi, depth, resident):
        piece = (shape[-2], hi - lo)
        whole = pltpu.VMEM((2, 2, depth) + piece, F32)
        own = [] if resident else [whole]
        return own + [whole, pltpu.VMEM((2, depth) + piece, F32), pltpu.VMEM((2, depth) + piece, F32)]

    def load(self, i):
        t, lo, hi, _ = self.plan[i]
        source = self.sources[t].at[:, :, :, self.core, :, pl.ds(lo, hi - lo)]
        return pltpu.make_async_copy(source, self.bufs[i][0], self.loads.at[i])

    def copies(self, i, phase):
        t, lo, hi, along_x = self.plan[i]
        y, x, z, core = self.y, self.x, self.z, self.core
        whole, half, quarter = self.bufs[i][-3:]
        by_x, by_y = device(y, 1 - x, z, core), device(1 - y, x, z, core)
        if phase == 0:
            source = self.sources[t].at[:, :, :, 1 - core, :, pl.ds(lo, hi - lo)]
            moves = [(source, whole, device(y, x, z, 1 - core))]
        elif phase == 1:
            moves = [(whole.at[1 - y], half, by_y) if along_x else (whole.at[:, 1 - x], half, by_x)]
        elif phase == 2:
            moves = [(half.at[1 - x], quarter.at[0], by_x) if along_x else (half.at[1 - y], quarter.at[0], by_y)]
        else:
            moves = []
            for dz in range(1, self.depth):
                pz = (z + dz) % self.depth
                moves.append((quarter.at[0, pz], quarter.at[1, dz], device(y, x, pz, core)))
        return [
            remote(src, dst, self.send.at[i, phase + n], self.recv.at[i, phase + n], peer)
            for n, (src, dst, peer) in enumerate(moves)
        ]

    def begin(self, i):
        for copy in self.copies(i, 0):
            copy.start()
        if not self.resident:
            self.load(i).start()

    def act(self, i, phase):
        t, lo, hi, along_x = self.plan[i]
        y, x, z, core = self.y, self.x, self.z, self.core
        whole, half, quarter = self.bufs[i][-3:]
        for copy in self.copies(i, phase):
            copy.wait_recv()
        if phase == 0:
            if self.resident:
                add_into(whole, self.sources[t].at[:, :, :, core, :, pl.ds(lo, hi - lo)])
            else:
                self.load(i).wait()
                add_into(whole, self.bufs[i][0])
        elif phase == 1:
            add_into(half, whole.at[y] if along_x else whole.at[:, x])
        elif phase == 2:
            add_into(quarter.at[0], half.at[x] if along_x else half.at[y])
        else:
            total = quarter[0, z]
            for dz in range(1, self.depth):
                total = total + quarter[1, dz]
            self.outs[t][:, lo:hi] = total
            return
        for copy in self.copies(i, phase + 1):
            copy.start()

    def finish(self):
        for i in range(len(self.plan)):
            for phase in range(4):
                for copy in self.copies(i, phase):
                    copy.wait_send()


def everywhere(value, slots, sends, recvs, depth, at):
    y, x, z, core = at
    slots[0] = value
    peers = (device(y, x, z, 1 - core), device(y, 1 - x, z, core), device(1 - y, x, z, core))
    for n, peer in enumerate(peers):
        copy = remote(slots.at[2 * n], slots.at[2 * n + 1], sends.at[n], recvs.at[n], peer)
        copy.start()
        copy.wait()
        slots[2 * n + 2] = slots[2 * n] + slots[2 * n + 1]
    copies = []
    for dz in range(1, depth):
        copy = remote(
            slots.at[6], slots.at[7 + z], sends.at[2 + dz], recvs.at[2 + dz], device(y, x, (z + dz) % depth, core)
        )
        copy.start()
        copies.append(copy)
    slots[7 + z] = slots[6]
    for copy in copies:
        copy.wait()
    total = slots[7]
    for dz in range(1, depth):
        total = total + slots[7 + dz]
    return total


SCHEDULE = {1: [(0, 0)], 2: [(1, 0)], 3: [(2, 0)], 4: [(0, 1)], 6: [(1, 1), (0, 2)], 7: [(2, 1)]}
LEFT_OVER = [(1, 2), (2, 2), (0, 3), (1, 3), (2, 3)]


def backward_kernel(
    depth, early, late, early_bufs, late_bufs, *refs
):
    ids, keep, p, q, ds, conv, queue, tab, gains, taps, w_in, g_tab_in, small_in = refs[:13]
    n_early, n_late = len(grouped(early)), len(grouped(late))
    sources = refs[13 : 13 + n_early]
    outs = refs[13 + n_early : 13 + 2 * n_early + n_late]
    small_o, squares_o = refs[13 + 2 * n_early + n_late : 15 + 2 * n_early + n_late]
    scratch = refs[15 + 2 * n_early + n_late :]
    small, g_in, g_tab, lam_s, reach_s, d_pre, ext, head_s, carry_s, hot_sum = scratch[:10]
    loads, early_send, early_recv, late_send, late_recv, slots, sq_slots, sends, recvs, sq_sends, sq_recvs = scratch[10:21]
    at = 21
    held = []
    for n in early_bufs + late_bufs:
        held.append(scratch[at : at + n])
        at += n
    spot = place()
    first_sums = Reduce(
        early, depth, sources, False, outs[:n_early], held[: len(early)], loads, early_send, early_recv, spot
    )
    last_sums = Reduce(
        late, depth, (g_in, g_tab), True, outs[n_early:], held[len(early) :], None, late_send, late_recv, spot
    )
    early_groups, late_groups = grouped(early), grouped(late)
    step = pl.program_id(0)
    rows, hidden = keep.shape
    vocab, width = tab.shape
    kernel = taps.shape[0]
    rim = (kernel - 1) * ROWS
    steps = rows // ROWS
    bias_rows = hidden // width

    @pl.when(step == 0)
    def _():
        greet(*spot, depth)
        for i in range(len(early)):
            first_sums.begin(i)
        g_in[...] = jnp.zeros_like(g_in)
        hot_sum[...] = jnp.zeros_like(hot_sum)
        small[...] = jnp.zeros_like(small)
        small[0:ROWS, :] = small_in[...]
        head_s[...] = jnp.zeros_like(head_s)
        carry_s[...] = jnp.zeros_like(carry_s)

    for when, acts in SCHEDULE.items():

        @pl.when(step == when)
        def _(acts=acts):
            for group, phase in acts:
                for i in early_groups[group]:
                    first_sums.act(i, phase)

    low_half = lax.broadcasted_iota(jnp.int32, (ROWS, hidden), 0) < ROWS // 2

    def scan_one(i, state):
        carry, reach = state
        at = pl.ds(pl.multiple_of((steps - 1 - i) * ROWS, ROWS), ROWS)
        lam = ds[at, :] + carry
        lam_s[at, :] = lam
        reach_s[at, :] = reach
        k = keep[at, :]
        return k * lam, k * reach

    first, _ = lax.fori_loop(
        0, steps, scan_one, (carry_s[...], jnp.where(low_half, 1.0, 0.0)), unroll=4
    )
    entry = jnp.where(low_half, swap_halves(first), 0.0)
    reach0 = keep[0:ROWS, :] * reach_s[0:ROWS, :]
    carry_s[...] = jnp.where(low_half, 0.0, swap_halves(first + reach0 * entry))

    def fix_one(pair, sums):
        gates, cands = [], []
        for half_step in range(2):
            at = pl.ds(pl.multiple_of(pair * 2 * ROWS + half_step * ROWS, ROWS), ROWS)
            lam = lam_s[at, :] + reach_s[at, :] * entry
            d_gate = lam * p[at, :]
            sums = sums + d_gate
            gates.append(d_gate)
            cands.append(lam * q[at, :])
        both = pl.ds(pl.multiple_of(pair * 2 * ROWS, 2 * ROWS), 2 * ROWS)
        d_pre[both, 0:hidden] = jnp.concatenate(gates, axis=0).astype(BF)
        d_pre[both, hidden : 2 * hidden] = jnp.concatenate(cands, axis=0).astype(BF)
        return sums

    sums = lax.fori_loop(
        0, steps // 2, fix_one, jnp.zeros((ROWS, hidden), F32), unroll=4
    )
    d_bias = column_sum(sums)
    base = ROWS + kernel
    for r in range(bias_rows):
        small[base + r : base + r + 1, :] += d_bias[:, r * width : (r + 1) * width]

    g_in[...] += tn(conv[...], d_pre[...]).reshape(g_in.shape)
    ext[0:rows, :] = nt(d_pre[...], w_in[...])
    half = lax.broadcasted_iota(jnp.int32, (rim, width), 0) % ROWS < ROWS // 2
    mine = ext[0:rim, :]
    ext[rows:, :] = jnp.where(
        half,
        swap_halves(mine.reshape(kernel - 1, ROWS, width)).reshape(rim, width),
        swap_halves(head_s[...].reshape(kernel - 1, ROWS, width)).reshape(rim, width),
    )
    head_s[...] = mine
    known = queue[...].astype(F32)
    d_queue = None
    for k in range(kernel):
        shift = (kernel - 1 - k) * ROWS
        part = ext[shift : shift + rows, :]
        term = taps[k : k + 1] * part
        d_queue = term if d_queue is None else d_queue + term
        small[ROWS + k : ROWS + k + 1, :] += column_sum(part * known)
    hot_t = one_hot_t(ids[0][0:1, :], vocab)
    hot_sum[...] += nn(hot_t, d_queue.astype(BF))

    @pl.when(step == pl.num_programs(0) - 1)
    def _():
        wide = tab[...].astype(BF).astype(F32)
        inverse = inv_rms(wide)
        total = hot_sum[...]
        small[0:1, :] = column_sum(total * (wide * inverse))
        g_tab[...] = (g_tab_in[...] + norm_back(wide, inverse, gains[0:1], total)).reshape(g_tab.shape)
        for i in range(len(late)):
            last_sums.begin(i)
        for group, phase in LEFT_OVER[:2]:
            for i in early_groups[group]:
                first_sums.act(i, phase)
        for phase in range(4):
            for group in late_groups:
                for i in group:
                    last_sums.act(i, phase)
            if phase == 0:
                for group, stage in LEFT_OVER[2:]:
                    for i in early_groups[group]:
                        first_sums.act(i, stage)
                small_o[...] = everywhere(small[...], slots, sends, recvs, depth, spot)
        square = jnp.zeros((1, 1), F32)
        for out in outs:
            value = out[...]
            square = square + jnp.sum(jnp.sum(value * value, axis=1, keepdims=True), axis=0, keepdims=True)
        squares_o[...] = everywhere(
            jnp.broadcast_to(square, (ROWS, LANES)), sq_slots, sq_sends, sq_recvs, depth, spot
        )
        first_sums.finish()
        last_sums.finish()


def run_backward(depth, ids, keep, p, q, ds, conv, queue, tab, gains, taps, w_in, g_tab, small, grads):
    blocks, _, rows = ids.shape
    vocab, width = tab.shape
    hidden = keep.shape[1]
    kernel = taps.shape[0]
    total = blocks * rows
    rim = (kernel - 1) * ROWS
    last = blocks - 1
    wide = pl.BlockSpec((rows, hidden), lambda i: (last - i, 0))
    thin = pl.BlockSpec((rows, width), lambda i: (last - i, 0))
    owners = (2, 2, depth, 2)
    early_shapes = [g.shape for g in grads]
    late_shapes = [owners + (width // (8 * depth), 2 * hidden), owners + (vocab // (8 * depth), width)]
    early, late = halves(early_shapes), halves(late_shapes)
    early_bufs = [Reduce.sizes(early_shapes[t], lo, hi, depth, False) for t, lo, hi, _ in early]
    late_bufs = [Reduce.sizes(late_shapes[t], lo, hi, depth, True) for t, lo, hi, _ in late]
    any_spec = pl.BlockSpec(memory_space=pl.ANY)
    out = [s[-2:] for s in early_shapes + late_shapes] + [(2 * ROWS, width), (ROWS, LANES)]
    flat = [b for group in early_bufs + late_bufs for b in group]
    dma = lambda *shape: pltpu.SemaphoreType.DMA(shape)
    return pl.pallas_call(
        functools.partial(
            backward_kernel, depth, early, late, [len(b) for b in early_bufs], [len(b) for b in late_bufs]
        ),
        grid=(blocks,),
        in_specs=[pl.BlockSpec((1, ROWS, rows), lambda i: (last - i, 0, 0)), wide, wide, wide, wide, thin, thin]
        + [whole(a.shape) for a in (tab, gains, taps, w_in, g_tab, small)]
        + [any_spec] * len(grads),
        out_specs=[whole(s) for s in out],
        out_shape=[jax.ShapeDtypeStruct(s, F32) for s in out],
        scratch_shapes=[
            pltpu.VMEM((2 * ROWS, width), F32),
            pltpu.VMEM(late_shapes[0], F32),
            pltpu.VMEM(late_shapes[1], F32),
            pltpu.VMEM((rows, hidden), F32),
            pltpu.VMEM((rows, hidden), F32),
            pltpu.VMEM((rows, 2 * hidden), BF),
            pltpu.VMEM((rim + rows, width), F32),
            pltpu.VMEM((rim, width), F32),
            pltpu.VMEM((ROWS, hidden), F32),
            pltpu.VMEM((vocab, width), F32),
            dma(len(early)),
            dma(len(early), depth + 2),
            dma(len(early), depth + 2),
            dma(len(late), depth + 2),
            dma(len(late), depth + 2),
            pltpu.VMEM((7 + depth, 2 * ROWS, width), F32),
            pltpu.VMEM((7 + depth, ROWS, LANES), F32),
            dma(depth + 2),
            dma(depth + 2),
            dma(depth + 2),
            dma(depth + 2),
        ]
        + flat,
        compiler_params=pltpu.CompilerParams(
            dimension_semantics=("arbitrary",), collective_id=1, has_side_effects=True, vmem_limit_bytes=62 * MIB
        ),
        cost_estimate=pl.CostEstimate(
            flops=2 * total * width * (4 * hidden + vocab), bytes_accessed=total * hidden * 16, transcendentals=0
        ),
        name="front_back_and_reduce",
    )(ids, keep, p, q, ds, conv, queue, tab, gains, taps, w_in, g_tab, small, *grads)


def adam_kernel(shapes, small, squares, count, *refs):
    mats = refs[:5]
    weights, firsts, seconds = refs[5:13], refs[13:21], refs[21:29]
    loss_o, count_o, norm_o = refs[29:32]
    new_w, new_m, new_v = refs[32:40], refs[40:48], refs[48:56]
    kernel, bias_rows = shapes
    width = small.shape[1]
    grads = [m[...] for m in mats]
    grads.append(small[0:3, :])
    grads.append(small[ROWS : ROWS + kernel, :])
    base = ROWS + kernel
    grads.append(
        jnp.concatenate([small[base + r : base + r + 1, :] for r in range(bias_rows)], axis=1)
    )
    square = squares[0:1, 0:1]
    for grad in grads[5:]:
        square = square + jnp.sum(jnp.sum(grad * grad, axis=1, keepdims=True), axis=0, keepdims=True)
    norm = jnp.sqrt(square)
    scale = jnp.minimum(1.0, CLIP / (norm + 1e-06))
    norm_o[...] = norm
    loss_o[...] = small[3:4, 0:1]
    count_o[...] = jnp.sum(count[:, 0:1, 0:1], axis=0)
    for i in range(8):
        rate = RATE_MATRIX if i < 5 else RATE_VECTOR
        decay = WEIGHT_DECAY if i < 5 else 0.0
        w, m, v = adam(weights[i][...], grads[i] * scale, firsts[i][...], seconds[i][...], rate, decay)
        new_w[i][...] = w
        new_m[i][...] = m
        new_v[i][...] = v


def run_adam(shapes, mats, small, squares, count, weights, firsts, seconds):
    one = jax.ShapeDtypeStruct((1, 1), F32)
    like = [jax.ShapeDtypeStruct(w.shape, F32) for w in weights]
    vmem = pl.BlockSpec(memory_space=pltpu.VMEM)
    args = (small, squares, count) + tuple(mats) + tuple(weights) + tuple(firsts) + tuple(seconds)
    return pl.pallas_call(
        functools.partial(adam_kernel, shapes),
        in_specs=[vmem] * len(args),
        out_specs=[vmem] * 27,
        out_shape=[one] * 3 + like * 3,
        compiler_params=pltpu.CompilerParams(vmem_limit_bytes=40 * MIB),
        name="adam_update",
    )(*args)


def spread_ids(tokens, targets, counted, depth):
    seqs, span = tokens.shape
    ways = 2 * depth

    def one(a):
        parts = a.reshape(ways, seqs // ways, 2, span // 2)
        return parts.transpose(0, 3, 2, 1).reshape(ways, 1, -1)

    rows = [one(tokens), one(targets), one(counted)]
    fill = jnp.zeros((ways, ROWS - 3, rows[0].shape[-1]), jnp.int32)
    return jnp.concatenate(rows + [fill], axis=1)


def body_moved(depth, *args):
    tokens, targets, counted = args[:3]
    weights, firsts, seconds = args[3:11], args[11:19], args[19:27]
    table, w_in, w_out, w_up, w_down, gains, conv_taps, gate_bias = weights
    ids = spread_ids(tokens, targets, counted, depth)
    share = jnp.sum(counted.astype(F32))
    first = jnp.concatenate([table, jnp.broadcast_to(share, (table.shape[0], LANES))], axis=1)
    mats = [w[0].astype(BF) for w in (w_in, w_out, w_up, w_down)]
    got = run_gather(depth, ids, [first, mats[0], mats[1], mats[2], mats[3]])
    ids = got[0]
    width = table.shape[1]
    tab = got[1][..., :width].reshape(-1, width)
    count = got[1][..., width:].reshape(-1, table.shape[0], LANES)
    full = [g.reshape(-1, g.shape[-1]) for g in got[2:]]
    taps = conv_taps[0]
    keep, p, q, ds, conv, queue, g_down, g_up, g_out, g_tab, small = run_forward(
        ids, tab, count, gains, taps, gate_bias, *full
    )
    grads = [g.reshape((2, 2, depth, 2, -1, g.shape[-1])) for g in (g_down, g_up, g_out)]
    r_down, r_up, r_out, r_in, r_tab, small, squares = run_backward(
        depth, ids, keep, p, q, ds, conv, queue, tab, gains, taps, full[0], g_tab, small, grads
    )
    mats = [r_tab, r_in, r_out, r_up, r_down]
    flat = lambda group: [group[0]] + [a[0] for a in group[1:5]] + [group[5], group[6][0], group[7]]
    out = run_adam(
        (conv_taps.shape[1], gate_bias.shape[1] // width),
        mats, small, squares, count, flat(weights), flat(firsts), flat(seconds),
    )
    shaped = [o.reshape(()) for o in out[:3]]
    for i, o in enumerate(out[3:]):
        shaped.append(o.reshape(weights[i % 8].shape))
    return tuple(shaped)


def choose(mesh, *args):
    ways = mesh.shape["seq"]
    seqs, span = args[0].shape
    if mesh.shape["dp"] == 4 and ways == 8 and seqs == 4 * ways and span == LANES:
        return body_moved(ways // 2, *args)
    return body(*args)


def solution(mesh):
    return jax.shard_map(
        functools.partial(choose, mesh),
        mesh=mesh,
        in_specs=(
            P("dp", "seq"),
            P("dp", "seq"),
            P("dp", "seq"),
            P(("dp", "seq"), None),
            P(None, ("dp", "seq"), None),
            P(None, ("dp", "seq"), None),
            P(None, ("dp", "seq"), None),
            P(None, ("dp", "seq"), None),
            P(),
            P(),
            P(),
            P(("dp", "seq"), None),
            P(None, ("dp", "seq"), None),
            P(None, ("dp", "seq"), None),
            P(None, ("dp", "seq"), None),
            P(None, ("dp", "seq"), None),
            P(),
            P(),
            P(),
            P(("dp", "seq"), None),
            P(None, ("dp", "seq"), None),
            P(None, ("dp", "seq"), None),
            P(None, ("dp", "seq"), None),
            P(None, ("dp", "seq"), None),
            P(),
            P(),
            P(),
        ),
        out_specs=(
            P(),
            P(),
            P(),
            P(("dp", "seq"), None),
            P(None, ("dp", "seq"), None),
            P(None, ("dp", "seq"), None),
            P(None, ("dp", "seq"), None),
            P(None, ("dp", "seq"), None),
            P(),
            P(),
            P(),
            P(("dp", "seq"), None),
            P(None, ("dp", "seq"), None),
            P(None, ("dp", "seq"), None),
            P(None, ("dp", "seq"), None),
            P(None, ("dp", "seq"), None),
            P(),
            P(),
            P(),
            P(("dp", "seq"), None),
            P(None, ("dp", "seq"), None),
            P(None, ("dp", "seq"), None),
            P(None, ("dp", "seq"), None),
            P(None, ("dp", "seq"), None),
            P(),
            P(),
            P(),
        ),
        check_vma=False,
    )
```

```python
import functools

import jax
import jax.numpy as jnp
from jax import lax
from jax.experimental import pallas as pl
from jax.experimental.pallas import tpu as pltpu
from jax.sharding import PartitionSpec as P

V = 256
MICRO = 2
STEP = 3


EPS = 1e-06
CLIP = 0.01
BETA_ONE = 0.5
BETA_TWO = 0.5
ADAM_EPS = 1e-08
RATE_MATRIX = 0.03
RATE_VECTOR = 0.3
WEIGHT_DECAY = 0.1


def from_behind(x, axis, by):
    devices = lax.axis_size(axis)
    pairs = [(i, i + by) for i in range(devices) if 0 <= i + by < devices]
    return lax.ppermute(x, axis, pairs)


def carried_in(part, axis, combine, identity, reverse):
    count = lax.axis_size(axis)
    place = lax.axis_index(axis)
    ahead = count - 1 - place if reverse else place
    gathered = jax.tree.map(lambda a: lax.all_gather(a, axis), part)
    state = jax.tree.map(lambda a, e: jnp.zeros_like(a) + jnp.asarray(e, a.dtype), part, identity)

    def one(lap, state):
        source = count - 1 - lap if reverse else lap
        return combine(
            state, jax.tree.map(lambda a: lax.dynamic_index_in_dim(a, source, 0, False), gathered)
        )

    return lax.fori_loop(0, ahead, one, state)


def matmul(left, right):
    return jnp.dot(left, right, preferred_element_type=jnp.float32)


def matmul_tn(left, right):
    return lax.dot_general(
        left, right, (((0,), (0,)), ((), ())), preferred_element_type=jnp.float32
    )


def matmul_nt(left, right):
    return lax.dot_general(
        left, right, (((1,), (1,)), ((), ())), preferred_element_type=jnp.float32
    )


def rms_norm(values, gain):
    return values * lax.rsqrt(jnp.mean(values * values, axis=-1, keepdims=True) + EPS) * gain


def combine(earlier, later):
    return (earlier[0] * later[0], later[0] * earlier[1] + later[1])


def gates(gate, cand):
    return (jax.nn.sigmoid(-gate), jax.nn.sigmoid(gate) * jax.nn.softplus(cand))


def conv_apply(padded, taps, length):
    total = taps[0] * padded[0:length].astype(jnp.float32)
    for k in range(1, taps.shape[0]):
        total = total + taps[k] * padded[k : k + length].astype(jnp.float32)
    return total


def adam(weight, grad, first, second, rate, decay):
    first = BETA_ONE * first + (1.0 - BETA_ONE) * grad
    second = BETA_TWO * second + (1.0 - BETA_TWO) * grad * grad
    fix_one = 1.0 - BETA_ONE**STEP
    fix_two = 1.0 - BETA_TWO**STEP
    update = first / fix_one / (jnp.sqrt(second / fix_two) + ADAM_EPS)
    return (weight - rate * (update + decay * weight), first, second)


def mixer_front(queue, rim, taps, bias, w_in):
    span, seqs, width = queue.shape
    padded = jnp.concatenate([rim, queue], axis=0)
    conv_low = conv_apply(padded, taps, span).astype(jnp.bfloat16)
    pre = matmul(conv_low.reshape(span * seqs, width), w_in).reshape(span, seqs, -1)
    hidden = bias.shape[0]
    keep, write = gates(pre[..., :hidden] + bias, pre[..., hidden:])
    return (padded, conv_low, pre, keep, write)


def block_tail(state, resid, gain_b, w_out, w_up, w_down):
    span, seqs, width = resid.shape
    state_low = state.astype(jnp.bfloat16).reshape(span * seqs, -1)
    mixed = resid + matmul(state_low, w_out).reshape(span, seqs, width)
    normed_low = rms_norm(mixed, gain_b).astype(jnp.bfloat16).reshape(span * seqs, width)
    lifted = matmul(normed_low, w_up)
    active_low = jax.nn.gelu(lifted).astype(jnp.bfloat16)
    result = mixed + matmul(active_low, w_down).reshape(span, seqs, width)
    return (result, (state_low, mixed, normed_low, lifted, active_low))


def layer_forward(resid, taps, gain_a, gain_b, bias, mats):
    span = resid.shape[0]
    kernel = taps.shape[0]
    queue = rms_norm(resid, gain_a).astype(jnp.bfloat16)
    rim = from_behind(queue[span - kernel + 1 :], "seq", 1)
    padded, conv_low, pre, keep, write = mixer_front(queue, rim, taps, bias, mats[0])
    decay, local = lax.associative_scan(combine, (keep, write), axis=0)
    ones = jnp.ones_like(local[0])
    carry_in = carried_in(
        (decay[-1], local[-1]), "seq", combine, (ones, jnp.zeros_like(ones)), False
    )[1]
    state = local + decay * carry_in[None]
    result, unused = block_tail(state, resid, gain_b, mats[1], mats[2], mats[3])
    return (result, rim, carry_in)


def layer_backward(grad, resid, rim, carry_in, taps, gain_a, gain_b, bias, mats):
    w_in, w_out, w_up, w_down = mats
    span, seqs, width = resid.shape
    kernel = taps.shape[0]
    hidden = bias.shape[0]
    normed_a, norm_back = jax.vjp(rms_norm, resid, gain_a)
    queue = normed_a.astype(jnp.bfloat16)
    padded, conv_low, pre, keep, write = mixer_front(queue, rim, taps, bias, w_in)
    decay, local = lax.associative_scan(combine, (keep, write), axis=0)
    state = local + decay * carry_in[None]
    result, (state_low, mixed, normed_low, lifted, active_low) = block_tail(
        state, resid, gain_b, w_out, w_up, w_down
    )
    grad_low = grad.astype(jnp.bfloat16).reshape(span * seqs, width)
    g_down = matmul_tn(active_low, grad_low)
    d_active = matmul_nt(grad_low, w_down)
    d_lifted_low = jax.vjp(jax.nn.gelu, lifted)[1](d_active)[0].astype(jnp.bfloat16)
    g_up = matmul_tn(normed_low, d_lifted_low)
    d_normed = matmul_nt(d_lifted_low, w_up).reshape(span, seqs, width)
    d_mixed, d_gain_b = jax.vjp(rms_norm, mixed, gain_b)[1](d_normed)
    d_mixed = grad + d_mixed
    mixed_low = d_mixed.astype(jnp.bfloat16).reshape(span * seqs, width)
    g_out = matmul_tn(state_low, mixed_low)
    d_state = matmul_nt(mixed_low, w_out).reshape(span, seqs, hidden)
    follow = jnp.concatenate([keep[1:], jnp.ones_like(keep[:1])], axis=0)
    reach, back_local = lax.associative_scan(combine, (follow, d_state), axis=0, reverse=True)
    ones = jnp.ones_like(keep[0])
    summary = (keep[0] * reach[0], keep[0] * back_local[0])
    carry_out = carried_in(summary, "seq", combine, (ones, jnp.zeros_like(ones)), True)[1]
    adjoint = back_local + reach * carry_out[None]
    before = jnp.concatenate([carry_in[None], state[:-1]], axis=0)
    d_gate, d_cand = jax.vjp(gates, pre[..., :hidden] + bias, pre[..., hidden:])[1](
        (adjoint * before, adjoint)
    )
    d_bias = jnp.sum(d_gate, axis=(0, 1))
    d_pre = (
        jnp.concatenate([d_gate, d_cand], axis=-1)
        .astype(jnp.bfloat16)
        .reshape(span * seqs, 2 * hidden)
    )
    g_in = matmul_tn(conv_low.reshape(span * seqs, width), d_pre)
    d_conv = matmul_nt(d_pre, w_in).reshape(span, seqs, width)
    beyond = from_behind(d_conv[: kernel - 1].astype(jnp.bfloat16), "seq", -1).astype(jnp.float32)
    extended = jnp.concatenate([d_conv, beyond], axis=0)
    d_queue = taps[0] * extended[kernel - 1 : kernel - 1 + span]
    tap_grads = [jnp.sum(d_conv * padded[0:span].astype(jnp.float32), axis=(0, 1))]
    for k in range(1, kernel):
        d_queue = d_queue + taps[k] * extended[kernel - 1 - k : kernel - 1 - k + span]
        tap_grads.append(jnp.sum(d_conv * padded[k : k + span].astype(jnp.float32), axis=(0, 1)))
    rounded = lax.optimization_barrier(d_queue.astype(jnp.bfloat16)).astype(jnp.float32)
    d_resid, d_gain_a = norm_back(rounded)
    return (
        d_mixed + d_resid,
        (g_in, g_out, g_up, g_down),
        (jnp.stack(tap_grads), d_gain_a, d_gain_b, d_bias),
    )


def body(
    tokens,
    targets,
    counted,
    table,
    w_in,
    w_out,
    w_up,
    w_down,
    gains,
    conv_taps,
    gate_bias,
    m_table,
    m_in,
    m_out,
    m_up,
    m_down,
    m_gains,
    m_taps,
    m_bias,
    v_table,
    v_in,
    v_out,
    v_up,
    v_down,
    v_gains,
    v_taps,
    v_bias,
):
    layers = w_in.shape[0]
    seq_dev, span = tokens.shape
    rows = seq_dev // MICRO
    width = table.shape[1]
    vocab = V
    mask = counted.astype(jnp.float32)
    count = lax.psum(jnp.sum(mask), ("dp", "seq"))
    shards = (
        w_in.astype(jnp.bfloat16),
        w_out.astype(jnp.bfloat16),
        w_up.astype(jnp.bfloat16),
        w_down.astype(jnp.bfloat16),
    )
    layer_gains = gains[: 2 * layers].reshape(layers, 2, width)
    columns = jnp.arange(vocab, dtype=jnp.int32)

    def forward_step(resid, inputs):
        pieces, taps, pair, bias = inputs
        mats = (
            lax.all_gather(pieces[0], ("dp", "seq"), axis=0, tiled=True),
            lax.all_gather(pieces[1], ("dp", "seq"), axis=0, tiled=True),
            lax.all_gather(pieces[2], ("dp", "seq"), axis=0, tiled=True),
            lax.all_gather(pieces[3], ("dp", "seq"), axis=0, tiled=True),
        )
        result, rim, carry_in = layer_forward(resid, taps, pair[0], pair[1], bias, mats)
        return (result, (resid, rim, carry_in))

    def backward_step(grad, inputs):
        saved, pieces, taps, pair, bias = inputs
        mats = (
            lax.all_gather(pieces[0], ("dp", "seq"), axis=0, tiled=True),
            lax.all_gather(pieces[1], ("dp", "seq"), axis=0, tiled=True),
            lax.all_gather(pieces[2], ("dp", "seq"), axis=0, tiled=True),
            lax.all_gather(pieces[3], ("dp", "seq"), axis=0, tiled=True),
        )
        grad, full, small = layer_backward(
            grad, saved[0], saved[1], saved[2], taps, pair[0], pair[1], bias, mats
        )
        full = (
            lax.psum_scatter(full[0], ("dp", "seq"), scatter_dimension=0, tiled=True),
            lax.psum_scatter(full[1], ("dp", "seq"), scatter_dimension=0, tiled=True),
            lax.psum_scatter(full[2], ("dp", "seq"), scatter_dimension=0, tiled=True),
            lax.psum_scatter(full[3], ("dp", "seq"), scatter_dimension=0, tiled=True),
        )
        return (grad, (full, small))

    loss = jnp.zeros((), jnp.float32)
    g_table = jnp.zeros((vocab, width), jnp.float32)
    acc_full = None
    acc_small = None
    for index in range(MICRO):
        tok = tokens[index * rows : (index + 1) * rows].T.reshape(-1)
        tgt = targets[index * rows : (index + 1) * rows].T.reshape(-1)
        weights = mask[index * rows : (index + 1) * rows].T.reshape(-1)
        tab = lax.all_gather(table.astype(jnp.bfloat16), ("dp", "seq"), axis=0, tiled=True)
        picks = tok[:, None] == columns[None, :]
        resid = matmul(picks.astype(jnp.bfloat16), tab).reshape(span, rows, width)
        final, saved = lax.scan(forward_step, resid, (shards, conv_taps, layer_gains, gate_bias))
        normed_f, final_back = jax.vjp(rms_norm, final, gains[2 * layers])
        normed_low = normed_f.astype(jnp.bfloat16).reshape(span * rows, width)
        logits = matmul_nt(normed_low, tab)
        top = jnp.max(logits, axis=-1, keepdims=True)
        lse = jnp.log(jnp.sum(jnp.exp(logits - top), axis=-1)) + top[:, 0]
        hits = (tgt[:, None] == columns[None, :]).astype(jnp.float32)
        picked = jnp.sum(hits * logits, axis=-1)
        loss = loss + jnp.sum(weights * (lse - picked))
        d_logits = ((jnp.exp(logits - lse[:, None]) - hits) * (weights / count)[:, None]).astype(
            jnp.bfloat16
        )
        g_table = g_table + matmul_tn(d_logits, normed_low)
        d_normed = matmul(d_logits, tab).reshape(span, rows, width)
        d_final, d_gain_f = final_back(d_normed)
        grad0, (full, small) = lax.scan(
            backward_step, d_final, (saved, shards, conv_taps, layer_gains, gate_bias), reverse=True
        )
        g_table = g_table + lax.dot_general(
            picks.astype(jnp.float32),
            grad0.reshape(span * rows, width),
            (((0,), (0,)), ((), ())),
            precision=lax.Precision.HIGHEST,
        )
        layer_gain_grads = jnp.stack([small[1], small[2]], axis=1).reshape(2 * layers, width)
        vectors = (jnp.concatenate([layer_gain_grads, d_gain_f[None]], axis=0), small[0], small[3])
        if index == 0:
            acc_full, acc_small = (full, vectors)
        else:
            acc_full = jax.tree.map(lambda a, b: a + b, acc_full, full)
            acc_small = jax.tree.map(lambda a, b: a + b, acc_small, vectors)
    table_shard = lax.psum_scatter(g_table, ("dp", "seq"), scatter_dimension=0, tiled=True)
    g_gains, g_taps, g_bias = lax.psum((acc_small[0], acc_small[1], acc_small[2]), ("dp", "seq"))
    matrices = (table_shard, acc_full[0], acc_full[1], acc_full[2], acc_full[3])
    squares = jnp.zeros((), jnp.float32)
    for grad in matrices:
        squares = squares + jnp.sum(grad * grad)
    squares_all, loss_all = lax.psum((squares, loss), ("dp", "seq"))
    small_squares = jnp.sum(g_gains * g_gains) + jnp.sum(g_taps * g_taps) + jnp.sum(g_bias * g_bias)
    norm = jnp.sqrt(squares_all + small_squares)
    scale = jnp.minimum(1.0, CLIP / (norm + 1e-06))
    params = (table, w_in, w_out, w_up, w_down, gains, conv_taps, gate_bias)
    grads = matrices + (g_gains, g_taps, g_bias)
    firsts = (m_table, m_in, m_out, m_up, m_down, m_gains, m_taps, m_bias)
    seconds = (v_table, v_in, v_out, v_up, v_down, v_gains, v_taps, v_bias)
    news, next_m, next_v = ([], [], [])
    for index in range(8):
        rate = RATE_MATRIX if index < 5 else RATE_VECTOR
        decay = WEIGHT_DECAY if index < 5 else 0.0
        weight, first, second = adam(
            params[index], grads[index] * scale, firsts[index], seconds[index], rate, decay
        )
        news.append(weight)
        next_m.append(first)
        next_v.append(second)
    return (
        loss_all,
        count,
        norm,
        news[0],
        news[1],
        news[2],
        news[3],
        news[4],
        news[5],
        news[6],
        news[7],
        next_m[0],
        next_m[1],
        next_m[2],
        next_m[3],
        next_m[4],
        next_m[5],
        next_m[6],
        next_m[7],
        next_v[0],
        next_v[1],
        next_v[2],
        next_v[3],
        next_v[4],
        next_v[5],
        next_v[6],
        next_v[7],
    )


BF = jnp.bfloat16
F32 = jnp.float32
MIB = 1 << 20
LANES = 128
ROWS = 8
GELU_A = 0.7978845608028654
GELU_B = 0.044715


def nn(left, right):
    return jnp.dot(left, right, preferred_element_type=F32)


def tn(left, right):
    return lax.dot_general(left, right, (((0,), (0,)), ((), ())), preferred_element_type=F32)


def nt(left, right):
    return lax.dot_general(left, right, (((1,), (1,)), ((), ())), preferred_element_type=F32)


def inv_rms(values):
    return lax.rsqrt(jnp.mean(values * values, axis=-1, keepdims=True) + EPS)


def norm_back(values, inverse, gain, grad):
    width = values.shape[-1]
    scaled = grad * gain
    dot = jnp.sum(scaled * values, axis=-1, keepdims=True)
    return inverse * scaled - values * (inverse * inverse * inverse * dot * (1.0 / width))


def column_sum(values):
    return jnp.sum(values, axis=0, keepdims=True)


def swap_halves(tile):
    return pltpu.roll(tile, ROWS // 2, tile.ndim - 2)


def one_hot(column, vocab):
    lane = lax.broadcasted_iota(jnp.int32, (column.shape[0], vocab), 1)
    return (column == lane).astype(F32).astype(BF)


def one_hot_t(row, vocab):
    place = lax.broadcasted_iota(jnp.int32, (vocab, row.shape[1]), 0)
    return (row == place).astype(F32).astype(BF)


def whole(shape):
    zeros = (0,) * len(shape)
    return pl.BlockSpec(shape, lambda i: zeros, pipeline_mode=pl.Buffered(1))


def place():
    dp = lax.axis_index("dp")
    seq = lax.axis_index("seq")
    return dp // 2, dp % 2, seq // 2, seq % 2


def device(y, x, z, core):
    return (y * 2 + x, z * 2 + core)


def greet(y, x, z, core, depth):
    barrier = pltpu.get_barrier_semaphore()
    peers = [device(1 - y, x, z, core), device(y, 1 - x, z, core), device(1 - y, 1 - x, z, core)]
    for dz in range(depth):
        for dc in range(2):
            if dz or dc:
                peers.append(device(y, x, (z + dz) % depth, (core + dc) % 2))
    for peer in peers:
        pl.semaphore_signal(barrier, inc=1, device_id=peer, device_id_type=pl.DeviceIdType.MESH)
    pl.semaphore_wait(barrier, len(peers))


def remote(src, dst, send, recv, peer):
    return pltpu.make_async_remote_copy(
        src_ref=src,
        dst_ref=dst,
        send_sem=send,
        recv_sem=recv,
        device_id=peer,
        device_id_type=pl.DeviceIdType.MESH,
    )


def in_order(groups, phases, act):
    for time in range(len(groups) + phases - 1):
        for phase in range(phases - 1, -1, -1):
            at = time - phase
            if 0 <= at < len(groups):
                for item in groups[at]:
                    act(item, phase)


def grouped(plan):
    return [[i, i + 1] for i in range(0, len(plan), 2)]


class Gather:
    def __init__(self, plan, depth, sources, outs, send, recv, at):
        self.plan, self.depth, self.sources, self.outs, self.send, self.recv = plan, depth, sources, outs, send, recv
        self.y, self.x, self.z, self.core = at

    def copies(self, i, phase):
        t, lo, hi, along_x = self.plan[i]
        cols = pl.ds(lo, hi - lo)
        y, x, z, core = self.y, self.x, self.z, self.core
        out = self.outs[t]
        by_x, by_y = device(y, 1 - x, z, core), device(1 - y, x, z, core)
        if phase == 0:
            mine = out.at[y, x, z, core, :, cols]
            source = mine if self.sources[t] is None else self.sources[t].at[:, cols]
            moves = [(source, mine, device(y, x, (z + dz) % self.depth, core)) for dz in range(1, self.depth)]
        elif phase == 1:
            part = out.at[y, x, :, core, :, cols]
            moves = [(part, part, by_x if along_x else by_y)]
        elif phase == 2:
            part = out.at[y, :, :, core, :, cols] if along_x else out.at[:, x, :, core, :, cols]
            moves = [(part, part, by_y if along_x else by_x)]
        else:
            part = out.at[:, :, :, core, :, cols]
            moves = [(part, part, device(y, x, z, 1 - core))]
        base = 0 if phase == 0 else self.depth - 2 + phase
        return [
            remote(src, dst, self.send.at[i, base + n], self.recv.at[i, base + n], peer)
            for n, (src, dst, peer) in enumerate(moves)
        ]

    def begin(self, i):
        for copy in self.copies(i, 0):
            copy.start()

    def act(self, i, phase):
        for copy in self.copies(i, phase):
            copy.wait_recv()
        if phase < 3:
            for copy in self.copies(i, phase + 1):
                copy.start()

    def finish(self):
        for i in range(len(self.plan)):
            for phase in range(4):
                for copy in self.copies(i, phase):
                    copy.wait_send()


def add_into(target, other):
    lead = target.shape[: len(target.shape) - 2]
    total = 1
    for d in lead:
        total *= d

    def one(i, _):
        index = []
        for d in reversed(lead):
            index.append(lax.rem(i, d))
            i = lax.div(i, d)
        index = tuple(reversed(index))
        target[index] = target[index] + other[index]
        return _

    lax.fori_loop(0, total, one, 0)


def halves(shapes, cuts=None):
    plan = []
    for t, shape in enumerate(shapes):
        pieces = 2 * (cuts[t] if cuts else 1)
        wide = shape[-1] // pieces
        for n in range(pieces):
            plan.append((t, n * wide, (n + 1) * wide, n % 2 == 0))
    return plan


class Reduce:
    def __init__(self, plan, depth, sources, resident, outs, bufs, loads, send, recv, at):
        self.plan, self.depth, self.sources, self.resident = plan, depth, sources, resident
        self.outs, self.bufs, self.loads, self.send, self.recv = outs, bufs, loads, send, recv
        self.y, self.x, self.z, self.core = at

    def sizes(shape, lo, hi, depth, resident):
        piece = (shape[-2], hi - lo)
        whole = pltpu.VMEM((2, 2, depth) + piece, F32)
        own = [] if resident else [whole]
        return own + [whole, pltpu.VMEM((2, depth) + piece, F32), pltpu.VMEM((2, depth) + piece, F32)]

    def load(self, i):
        t, lo, hi, _ = self.plan[i]
        source = self.sources[t].at[:, :, :, self.core, :, pl.ds(lo, hi - lo)]
        return pltpu.make_async_copy(source, self.bufs[i][0], self.loads.at[i])

    def copies(self, i, phase):
        t, lo, hi, along_x = self.plan[i]
        y, x, z, core = self.y, self.x, self.z, self.core
        whole, half, quarter = self.bufs[i][-3:]
        by_x, by_y = device(y, 1 - x, z, core), device(1 - y, x, z, core)
        if phase == 0:
            source = self.sources[t].at[:, :, :, 1 - core, :, pl.ds(lo, hi - lo)]
            moves = [(source, whole, device(y, x, z, 1 - core))]
        elif phase == 1:
            moves = [(whole.at[1 - y], half, by_y) if along_x else (whole.at[:, 1 - x], half, by_x)]
        elif phase == 2:
            moves = [(half.at[1 - x], quarter.at[0], by_x) if along_x else (half.at[1 - y], quarter.at[0], by_y)]
        else:
            moves = []
            for dz in range(1, self.depth):
                pz = (z + dz) % self.depth
                moves.append((quarter.at[0, pz], quarter.at[1, dz], device(y, x, pz, core)))
        return [
            remote(src, dst, self.send.at[i, phase + n], self.recv.at[i, phase + n], peer)
            for n, (src, dst, peer) in enumerate(moves)
        ]

    def begin(self, i):
        for copy in self.copies(i, 0):
            copy.start()
        if not self.resident:
            self.load(i).start()

    def act(self, i, phase):
        t, lo, hi, along_x = self.plan[i]
        y, x, z, core = self.y, self.x, self.z, self.core
        whole, half, quarter = self.bufs[i][-3:]
        for copy in self.copies(i, phase):
            copy.wait_recv()
        if phase == 0:
            if self.resident:
                add_into(whole, self.sources[t].at[:, :, :, core, :, pl.ds(lo, hi - lo)])
            else:
                self.load(i).wait()
                add_into(whole, self.bufs[i][0])
        elif phase == 1:
            add_into(half, whole.at[y] if along_x else whole.at[:, x])
        elif phase == 2:
            add_into(quarter.at[0], half.at[x] if along_x else half.at[y])
        else:
            total = quarter[0, z]
            for dz in range(1, self.depth):
                total = total + quarter[1, dz]
            self.outs[t][:, lo:hi] = total
            return
        for copy in self.copies(i, phase + 1):
            copy.start()

    def finish(self):
        for i in range(len(self.plan)):
            for phase in range(4):
                for copy in self.copies(i, phase):
                    copy.wait_send()


class Everywhere:
    def __init__(self, slots, sends, recvs, depth, at):
        y, x, z, core = at
        self.slots, self.ways = slots, 2 * depth
        self.me, self.other = z * 2 + core, self.ways + y * 2 + x
        self.near, self.far = [], []
        mine = slots.at[self.me]
        for dz in range(depth):
            for dc in range(2):
                if dz or dc:
                    n = dz * 2 + dc
                    peer = device(y, x, (z + dz) % depth, (core + dc) % 2)
                    self.near.append(remote(mine, mine, sends.at[n], recvs.at[n], peer))
        mine = slots.at[self.other]
        for n, (dy, dx) in enumerate(((0, 1), (1, 0), (1, 1))):
            n += self.ways
            peer = device((y + dy) % 2, (x + dx) % 2, z, core)
            self.far.append(remote(mine, mine, sends.at[n], recvs.at[n], peer))

    def total(self, lo, hi):
        value = self.slots[lo]
        for n in range(lo + 1, hi):
            value = value + self.slots[n]
        return value

    def begin(self, value):
        self.slots[self.me] = value
        for copy in self.near:
            copy.start()

    def middle(self):
        for copy in self.near:
            copy.wait()
        self.slots[self.other] = self.total(0, self.ways)
        for copy in self.far:
            copy.start()

    def end(self):
        for copy in self.far:
            copy.wait()
        return self.total(self.ways, self.ways + 4)


SCHEDULE = {
    2: [(True, 0, 0), (True, 1, 0)], 3: [(True, 2, 0)], 4: [(True, 0, 1)], 6: [(True, 1, 1)],
    9: [(True, 2, 1), (False, 0, 0), (False, 1, 0), (True, 0, 2)], 10: [(True, 1, 2)], 12: [(True, 2, 2)], 14: [(False, 0, 1)],
}
LEFT_OVER = [
    (False, 2, 0), (None, 0, 0), (False, 1, 1), (False, 0, 2), (False, 2, 1), (True, 0, 3), (True, 1, 3), (True, 2, 3),
    (False, 1, 2), (False, 2, 2), (False, 0, 3), (False, 1, 3), (False, 2, 3),
]


def backward_kernel(depth, early, late, sizes, *refs):
    ids, keep, p, q, ds, conv, queue, tab, gains, taps, w_in, g_tab_a, g_tab_b, small_in, r_down = refs[:15]
    sources = refs[15:17]
    outs = tuple(refs[17:21])
    small_o, squares_o = refs[21:23]
    small, g_in, g_tab, d_pre, ext, head_s, carry_s, hot_sum = refs[23:31]
    loads, early_send, early_recv, late_send, late_recv, slots, sq_slots, sends, recvs, sq_sends, sq_recvs = refs[31:42]
    at = 42
    held = []
    for n in sizes:
        held.append(refs[at : at + n])
        at += n
    spot = place()
    first_sums = Reduce(
        early, depth, sources, False, outs[:2], held[: len(early)], loads, early_send, early_recv, spot
    )
    last_sums = Reduce(
        late, depth, (g_in, g_tab), True, outs[2:], held[len(early) :], None, late_send, late_recv, spot
    )
    smalls = Everywhere(slots, sends, recvs, depth, spot)
    squares = Everywhere(sq_slots, sq_sends, sq_recvs, depth, spot)
    early_groups, late_groups = grouped(early), grouped(late)
    step = pl.program_id(0)
    blocks = pl.num_programs(0) // 2
    rows, hidden = keep.shape
    vocab, width = tab.shape
    kernel = taps.shape[0]
    rim = (kernel - 1) * ROWS
    steps = rows // ROWS
    bias_rows = hidden // width
    base = ROWS + kernel

    def run(acts):
        for is_early, group, phase in acts:
            if is_early is None:
                smalls.middle()
                continue
            sums, groups = (first_sums, early_groups) if is_early else (last_sums, late_groups)
            for i in groups[group]:
                sums.act(i, phase)

    @pl.when(step == 0)
    def _():
        greet(*spot, depth)
        for i in range(len(early)):
            first_sums.begin(i)
        g_in[...] = jnp.zeros_like(g_in)
        hot_sum[...] = jnp.zeros_like(hot_sum)
        small[...] = jnp.zeros_like(small)
        small[0:ROWS, :] = small_in[...]
        head_s[...] = jnp.zeros_like(head_s)
        carry_s[...] = jnp.zeros_like(carry_s)

    for when, acts in SCHEDULE.items():

        @pl.when(step == when)
        def _(acts=acts):
            run(acts)

    @pl.when(step < blocks)
    def _():
        low_half = lax.broadcasted_iota(jnp.int32, (ROWS, hidden), 0) < ROWS // 2
        carry = carry_s[...]
        block = blocks - 1 - step

        def scan_one(i, reached):
            at = pl.ds(pl.multiple_of((steps - 1 - i) * ROWS, ROWS), ROWS)
            return keep[at, :] * (ds[at, :] + reached)

        first = lax.fori_loop(0, steps, scan_one, carry, unroll=8)

        def scan_two(i, state):
            reached, total = state
            pair = steps // 2 - 1 - i
            gates, cands = [None, None], [None, None]
            for half_step in (1, 0):
                at = pl.ds(pl.multiple_of(pair * 2 * ROWS + half_step * ROWS, ROWS), ROWS)
                lam = ds[at, :] + reached
                reached = keep[at, :] * lam
                gates[half_step] = lam * p[at, :]
                cands[half_step] = lam * q[at, :]
                total = total + gates[half_step]
            both = pl.ds(pl.multiple_of(pair * 2 * ROWS, 2 * ROWS), 2 * ROWS)
            d_pre[block, both, 0:hidden] = jnp.concatenate(gates, axis=0).astype(BF)
            d_pre[block, both, hidden : 2 * hidden] = jnp.concatenate(cands, axis=0).astype(BF)
            return reached, total

        entry = jnp.where(low_half, swap_halves(first), carry)
        last, total = lax.fori_loop(
            0, steps // 2, scan_two, (entry, jnp.zeros((ROWS, hidden), F32)), unroll=4
        )
        carry_s[...] = jnp.where(low_half, 0.0, swap_halves(last))
        d_bias = column_sum(total)
        for r in range(bias_rows):
            small[base + r : base + r + 1, :] += d_bias[:, r * width : (r + 1) * width]
        g_in[...] += tn(conv[...], d_pre[block]).reshape(g_in.shape)

    @pl.when(step == blocks - 1)
    def _():
        for group in late_groups[:2]:
            for i in group:
                last_sums.begin(i)

    @pl.when(step >= blocks)
    def _():
        block = 2 * blocks - 1 - step
        ext[0:rows, :] = nt(d_pre[block], w_in[...])
        half = lax.broadcasted_iota(jnp.int32, (rim, width), 0) % ROWS < ROWS // 2
        mine = ext[0:rim, :]
        ext[rows:, :] = jnp.where(
            half,
            swap_halves(mine.reshape(kernel - 1, ROWS, width)).reshape(rim, width),
            swap_halves(head_s[...].reshape(kernel - 1, ROWS, width)).reshape(rim, width),
        )
        head_s[...] = mine
        known = queue[...].astype(F32)
        d_queue = None
        for k in range(kernel):
            shift = (kernel - 1 - k) * ROWS
            part = ext[shift : shift + rows, :]
            term = taps[k : k + 1] * part
            d_queue = term if d_queue is None else d_queue + term
            small[ROWS + k : ROWS + k + 1, :] += column_sum(part * known)
        hot_t = one_hot_t(ids[0][0:1, :], vocab)
        hot_sum[...] += nn(hot_t, d_queue.astype(BF))

    @pl.when(step == 2 * blocks - 1)
    def _():
        wide = tab[...].astype(BF).astype(F32)
        inverse = inv_rms(wide)
        total = hot_sum[...]
        small[0:1, :] = column_sum(total * (wide * inverse))
        smalls.begin(small[...])
        g_tab[...] = (
            g_tab_a[...] + g_tab_b[...] + norm_back(wide, inverse, gains[0:1], total)
        ).reshape(g_tab.shape)
        for i in late_groups[2]:
            last_sums.begin(i)
        run(LEFT_OVER)
        small_o[...] = smalls.end()
        square = jnp.zeros((1, 1), F32)
        for out in outs + (r_down,):
            value = out[...]
            square = square + jnp.sum(jnp.sum(value * value, axis=1, keepdims=True), axis=0, keepdims=True)
        squares.begin(jnp.broadcast_to(square, (ROWS, LANES)))
        squares.middle()
        squares_o[...] = squares.end()
        first_sums.finish()
        last_sums.finish()


def run_backward(depth, ids, keep, p, q, ds, conv, queue, tab, gains, taps, w_in, g_tabs, small, r_down, grads):
    blocks, _, rows = ids.shape
    vocab, width = tab.shape
    hidden = keep.shape[1]
    kernel = taps.shape[0]
    rim = (kernel - 1) * ROWS
    last = blocks - 1
    wide = pl.BlockSpec((rows, hidden), lambda i: (jnp.maximum(last - i, 0), 0))
    front = pl.BlockSpec((rows, width), lambda i: (jnp.maximum(last - i, 0), 0))
    back = pl.BlockSpec((rows, width), lambda i: (jnp.minimum(2 * blocks - 1 - i, last), 0))
    back_ids = pl.BlockSpec((1, ROWS, rows), lambda i: (jnp.minimum(2 * blocks - 1 - i, last), 0, 0))
    owners = (2, 2, depth, 2)
    early_shapes = [g.shape for g in grads]
    late_shapes = [owners + (width // (8 * depth), 2 * hidden), owners + (vocab // (8 * depth), width)]
    early, late = halves(early_shapes, (2, 1)), halves(late_shapes, (2, 1))
    bufs = [Reduce.sizes(early_shapes[t], lo, hi, depth, False) for t, lo, hi, _ in early]
    bufs += [Reduce.sizes(late_shapes[t], lo, hi, depth, True) for t, lo, hi, _ in late]
    any_spec = pl.BlockSpec(memory_space=pl.ANY)
    out = [s[-2:] for s in early_shapes + late_shapes] + [(2 * ROWS, width), (ROWS, LANES)]
    dma = lambda *shape: pltpu.SemaphoreType.DMA(shape)
    fixed = (tab, gains, taps, w_in) + tuple(g_tabs) + (small, r_down)
    return pl.pallas_call(
        functools.partial(backward_kernel, depth, early, late, [len(b) for b in bufs]),
        grid=(2 * blocks,),
        in_specs=[back_ids, wide, wide, wide, wide, front, back]
        + [whole(a.shape) for a in fixed]
        + [any_spec] * len(grads),
        out_specs=[whole(s) for s in out],
        out_shape=[jax.ShapeDtypeStruct(s, F32) for s in out],
        scratch_shapes=[
            pltpu.VMEM((2 * ROWS, width), F32),
            pltpu.VMEM(late_shapes[0], F32),
            pltpu.VMEM(late_shapes[1], F32),
            pltpu.VMEM((blocks, rows, 2 * hidden), BF),
            pltpu.VMEM((rim + rows, width), F32),
            pltpu.VMEM((rim, width), F32),
            pltpu.VMEM((ROWS, hidden), F32),
            pltpu.VMEM((vocab, width), F32),
            dma(len(early)),
            dma(len(early), depth + 2),
            dma(len(early), depth + 2),
            dma(len(late), depth + 2),
            dma(len(late), depth + 2),
            pltpu.VMEM((2 * depth + 4, 2 * ROWS, width), F32),
            pltpu.VMEM((2 * depth + 4, ROWS, LANES), F32),
            dma(2 * depth + 4),
            dma(2 * depth + 4),
            dma(2 * depth + 4),
            dma(2 * depth + 4),
        ]
        + [b for group in bufs for b in group],
        compiler_params=pltpu.CompilerParams(
            dimension_semantics=("arbitrary",), collective_id=1, has_side_effects=True, vmem_limit_bytes=63 * MIB
        ),
        name="front_back_and_reduce",
    )(ids, keep, p, q, ds, conv, queue, *fixed, *grads)


def front_block(ids, qtab, taps, bias, w_in, keep_o, p_o, q_o, conv_o, queue_o, state_o, padq, tail_s, carry_s, big):
    rows, hidden = keep_o.shape
    vocab, width = qtab.shape
    kernel = taps.shape[0]
    rim = (kernel - 1) * ROWS
    steps = rows // ROWS
    chunk = 256
    hot = one_hot(ids.T[:, 0:1], vocab)
    queue = nn(hot, qtab[...])
    queue_o[...] = queue.astype(BF)
    padq[rim:, :] = queue
    half = lax.broadcasted_iota(jnp.int32, (rim, width), 0) % ROWS < ROWS // 2
    before = tail_s[...].reshape(kernel - 1, ROWS, width)
    latest = padq[rows:, :].reshape(kernel - 1, ROWS, width)
    padq[0:rim, :] = jnp.where(
        half, swap_halves(before).reshape(rim, width), swap_halves(latest).reshape(rim, width)
    )
    tail_s[...] = padq[rows:, :]
    conv = taps[0:1] * padq[0:rows, :]
    for k in range(1, kernel):
        conv = conv + taps[k : k + 1] * padq[k * ROWS : k * ROWS + rows, :]
    conv_o[...] = conv.astype(BF)

    for j in range(hidden // chunk):
        cols = slice(j * chunk, (j + 1) * chunk)
        gate = nn(conv_o[...], w_in[:, j * chunk : (j + 1) * chunk]) + bias[0:1, cols]
        cand = nn(conv_o[...], w_in[:, hidden + j * chunk : hidden + (j + 1) * chunk])
        eg = jnp.exp(-jnp.abs(gate))
        rg = pl.reciprocal(1.0 + eg)
        sg = eg * rg
        up = gate >= 0
        write_gate = jnp.where(up, rg, sg)
        keep_o[:, cols] = jnp.where(up, sg, rg)
        ec = jnp.exp(-jnp.abs(cand))
        rc = pl.reciprocal(1.0 + ec)
        slope = jnp.where(cand >= 0, rc, ec * rc)
        soft = jnp.maximum(cand, 0.0) + jnp.where(
            ec < 1e-3, ec * (1.0 - 0.5 * ec), jnp.log(1.0 + ec)
        )
        p_o[:, cols] = write_gate
        q_o[:, cols] = write_gate * slope
        big[:, cols] = write_gate * soft

    low_half = lax.broadcasted_iota(jnp.int32, (ROWS, hidden), 0) < ROWS // 2
    carry = carry_s[...]

    def scan_one(tau, state):
        at = pl.ds(pl.multiple_of(tau * ROWS, ROWS), ROWS)
        return keep_o[at, :] * state + big[at, :]

    end = lax.fori_loop(0, steps, scan_one, carry, unroll=8)

    def scan_two(pair, state):
        lows = []
        for half_step in range(2):
            at = pl.ds(pl.multiple_of(pair * 2 * ROWS + half_step * ROWS, ROWS), ROWS)
            keep, write = keep_o[at, :], big[at, :]
            p_o[at, :] = keep * (write - p_o[at, :] * state)
            state = keep * state + write
            lows.append(state)
        both = pl.ds(pl.multiple_of(pair * 2 * ROWS, 2 * ROWS), 2 * ROWS)
        state_o[both, :] = jnp.concatenate(lows, axis=0).astype(BF)
        return state

    last = lax.fori_loop(0, steps // 2, scan_two, jnp.where(low_half, carry, swap_halves(end)), unroll=4)
    carry_s[...] = jnp.where(low_half, swap_halves(last), 0.0)


GATHER_SCHEDULE = {1: [(0, 0), (1, 0)], 2: [(2, 0), (0, 1)], 3: [(1, 1)], 4: [(2, 1), (0, 2)], 5: [(1, 2)], 6: [(2, 2)]}
GATHER_LAST = [(0, 3), (1, 3), (2, 3)]


def front_kernel(
    depth, now, later,
    ids, table, w_in, w_out, w_up, w_down, gains, taps, bias,
    keep_o, p_o, q_o, conv_o, queue_o, state_o, ids_o, tab_o, count_o, w_in_o, w_out_o, w_up_o, w_down_o,
    ids_s, tab_s, count_s, in_s, out_s, up_s, down_s, qtab, padq, tail_s, carry_s, big,
    ids_send, ids_recv, now_send, now_recv, later_send, later_recv, own_sem, in_sem,
):
    step = pl.program_id(0)
    spot = place()
    y, x, z, core = spot
    me = z * 2 + core
    wait_in = pltpu.make_async_copy(in_s, w_in_o, in_sem)
    first = Gather(now, depth, [None] * 3, [tab_s, count_s, in_s], now_send, now_recv, spot)
    rest = Gather(later, depth, [out_s, up_s, down_s], [w_out_o, w_up_o, w_down_o], later_send, later_recv, spot)
    later_groups = grouped(later)
    own = [
        pltpu.make_async_copy(src, dst.at[y, x, z, core], own_sem.at[n])
        for n, (src, dst) in enumerate(((out_s, w_out_o), (up_s, w_up_o), (down_s, w_down_o)))
    ]
    spread = []
    for dz in range(depth):
        for dc in range(2):
            if dz or dc:
                pz, pc = (z + dz) % depth, (core + dc) % 2
                n = dz * 2 + dc
                spread.append(
                    remote(ids.at[pz * 2 + pc], ids_s.at[me], ids_send.at[n], ids_recv.at[n], device(y, x, pz, pc))
                )

    @pl.when(step == 0)
    def _():
        tab_s[y, x, z, core] = table[...]
        share = jnp.zeros((1, ids.shape[2]), F32)
        for n in range(ids.shape[0]):
            share = share + ids[n, 2:3, :].astype(F32)
        count_s[y, x, z, core] = jnp.broadcast_to(jnp.sum(share, axis=1, keepdims=True), count_o.shape)
        in_s[y, x, z, core] = w_in[...].astype(BF)
        greet(*spot, depth)
        for i in range(len(now)):
            first.begin(i)
        for copy in spread:
            copy.start()
        out_s[...] = w_out[...].astype(BF)
        up_s[...] = w_up[...].astype(BF)
        down_s[...] = w_down[...].astype(BF)
        for copy in own:
            copy.start()
        ids_s[me] = ids[me]
        for i in range(len(now)):
            first.act(i, 0)
        for i in range(len(later)):
            rest.begin(i)
        for phase in range(1, 4):
            for i in range(len(now)):
                first.act(i, phase)
        wait_in.start()
        for copy in spread:
            copy.wait_recv()
        tab = tab_s[...].reshape(tab_o.shape)
        tab_o[...] = tab
        wide = tab.astype(BF).astype(F32)
        qtab[...] = (wide * inv_rms(wide) * gains[0:1]).astype(BF)
        total = jnp.zeros(count_o.shape, F32)
        for n in range(8 * depth):
            total = total + count_s[n // (4 * depth), n // (2 * depth) % 2, n // 2 % depth, n % 2]
        count_o[...] = total
        tail_s[...] = jnp.zeros_like(tail_s)
        carry_s[...] = jnp.zeros_like(carry_s)
        for copy in own:
            copy.wait()

    for when, acts in GATHER_SCHEDULE.items():

        @pl.when(step == when)
        def _(acts=acts):
            for group, phase in acts:
                for i in later_groups[group]:
                    rest.act(i, phase)

    here = ids_s[step]
    ids_o[0] = here
    front_block(
        here, qtab, taps, bias, FlatRows(in_s), keep_o, p_o, q_o, conv_o, queue_o, state_o, padq, tail_s, carry_s, big
    )

    @pl.when(step == pl.num_programs(0) - 1)
    def _():
        for group, phase in GATHER_LAST:
            for i in later_groups[group]:
                rest.act(i, phase)
        wait_in.wait()
        for copy in spread:
            copy.wait_send()
        first.finish()
        rest.finish()


class FlatRows:
    def __init__(self, ref):
        self.ref = ref

    def __getitem__(self, index):
        cols = index[1]
        part = self.ref[:, :, :, :, :, cols]
        return part.reshape(-1, part.shape[-1])


def run_front(depth, ids, table, mats, gains, taps, bias):
    blocks, _, rows = ids.shape
    w_in, w_out, w_up, w_down = mats
    width = table.shape[1]
    hidden = bias.shape[1]
    kernel = taps.shape[0]
    total = blocks * rows
    rim = (kernel - 1) * ROWS
    owners = (2, 2, depth, 2)
    devices = 8 * depth
    vocab = devices * table.shape[0]
    cols = w_in.shape[1]
    now = [(0, 0, width, True), (1, 0, LANES, False)]
    for n in range(4):
        now.append((2, n * cols // 4, (n + 1) * cols // 4, n % 2 == 0))
    later = halves([a.shape for a in (w_out, w_up, w_down)])
    wide = pl.BlockSpec((rows, hidden), lambda i: (i, 0))
    thin = pl.BlockSpec((rows, width), lambda i: (i, 0))
    any_spec = pl.BlockSpec(memory_space=pl.ANY)
    dma = lambda *shape: pltpu.SemaphoreType.DMA(shape)
    args = (ids, table, w_in, w_out, w_up, w_down, gains, taps, bias)
    struct = jax.ShapeDtypeStruct
    return pl.pallas_call(
        functools.partial(front_kernel, depth, now, later),
        grid=(blocks,),
        in_specs=[whole(a.shape) for a in args],
        out_specs=[wide] * 3 + [thin, thin, wide]
        + [pl.BlockSpec((1, ROWS, rows), lambda i: (i, 0, 0)), whole((vocab, width)), whole((ROWS, LANES))]
        + [any_spec] * 4,
        out_shape=[struct((total, hidden), F32)] * 3
        + [struct((total, width), BF)] * 2
        + [struct((total, hidden), BF), struct(ids.shape, jnp.int32), struct((vocab, width), F32), struct((ROWS, LANES), F32)]
        + [struct(owners + a.shape, BF) for a in mats],
        scratch_shapes=[
            pltpu.VMEM(ids.shape, jnp.int32),
            pltpu.VMEM(owners + table.shape, F32),
            pltpu.VMEM(owners + (ROWS, LANES), F32),
            pltpu.VMEM(owners + w_in.shape, BF),
            pltpu.VMEM(w_out.shape, BF),
            pltpu.VMEM(w_up.shape, BF),
            pltpu.VMEM(w_down.shape, BF),
            pltpu.VMEM((vocab, width), BF),
            pltpu.VMEM((rim + rows, width), F32),
            pltpu.VMEM((rim, width), F32),
            pltpu.VMEM((ROWS, hidden), F32),
            pltpu.VMEM((rows, hidden), F32),
            dma(2 * depth),
            dma(2 * depth),
            dma(len(now), depth + 2),
            dma(len(now), depth + 2),
            dma(len(later), depth + 2),
            dma(len(later), depth + 2),
            dma(3),
            pltpu.SemaphoreType.DMA,
        ],
        compiler_params=pltpu.CompilerParams(
            dimension_semantics=("arbitrary",), collective_id=0, has_side_effects=True, vmem_limit_bytes=60 * MIB
        ),
        name="gather_and_front",
    )(*args)


def tail_kernel(
    ids, state_low, tab, count, gains, w_out, w_up, w_down,
    mixed_o, normed_o, final_o, lifted_o, g_down, g_tab, small_o,
    tab_low, slope_s, active,
):
    step = pl.program_id(0)
    rows = state_low.shape[0]
    vocab, width = tab.shape
    ff = w_up.shape[1]
    chunk = 256

    @pl.when(step == 0)
    def _():
        tab_low[...] = tab[...].astype(BF)
        g_down[...] = jnp.zeros_like(g_down)
        g_tab[...] = jnp.zeros_like(g_tab)
        small_o[...] = jnp.zeros_like(small_o)

    columns = jnp.concatenate([ids[n].T for n in range(ids.shape[0])], axis=0)
    hot = one_hot(columns[:, 0:1], vocab)
    mixed = nn(hot, tab_low[...]) + nn(state_low[...], w_out[...])
    mixed_o[...] = mixed
    inverse_b = inv_rms(mixed)
    normed_o[...] = (mixed * inverse_b * gains[1:2]).astype(BF)
    for j in range(ff // chunk):
        cols = slice(j * chunk, (j + 1) * chunk)
        lifted = nn(normed_o[...], w_up[:, cols])
        square = lifted * lifted
        curve = jnp.tanh(lifted * (GELU_A + (GELU_A * GELU_B) * square))
        cdf = 0.5 + 0.5 * curve
        active[:, cols] = (lifted * cdf).astype(BF)
        slope_s[:, cols] = cdf + (0.5 * lifted) * (1.0 - curve * curve) * (
            GELU_A + (3.0 * GELU_A * GELU_B) * square
        )
    result = mixed_o[...] + nn(active[...], w_down[...])
    inverse_f = inv_rms(result)
    unit_f = result * inverse_f
    normed_f = (unit_f * gains[2:3]).astype(BF)

    logits = nt(normed_f, tab_low[...])
    top = jnp.max(logits, axis=-1, keepdims=True)
    powers = jnp.exp(logits - top)
    total = jnp.sum(powers, axis=-1, keepdims=True)
    lse = jnp.log(total) + top
    target = columns[:, 1:2] == lax.broadcasted_iota(jnp.int32, (rows, vocab), 1)
    picked = jnp.sum(jnp.where(target, logits, 0.0), axis=-1, keepdims=True)
    weight = columns[:, 2:3].astype(F32)
    loss = column_sum(weight * (lse - picked))
    share = weight * (1.0 / count[0:1, 0:1])
    d_logits = ((powers * (1.0 / total) - jnp.where(target, 1.0, 0.0)) * share).astype(BF)
    g_tab[...] += tn(d_logits, normed_f)
    d_normed_f = nn(d_logits, tab_low[...])
    small_o[2:3, :] += column_sum(d_normed_f * unit_f)
    small_o[3:4, :] += jnp.broadcast_to(loss, (1, width))
    d_final = norm_back(result, inverse_f, gains[2:3], d_normed_f)
    final_o[...] = d_final
    grad_low = d_final.astype(BF)
    for j in range(ff // chunk):
        cols = slice(j * chunk, (j + 1) * chunk)
        d_active = nt(grad_low, w_down[cols, :])
        g_down[cols, :] += tn(active[:, cols], grad_low)
        lifted_o[:, cols] = (d_active * slope_s[:, cols]).astype(BF)


def run_tail(join, ids, state_low, tab, count, gains, w_out, w_up, w_down):
    blocks, _, rows = ids.shape
    rows, blocks = rows * join, blocks // join
    vocab, width = tab.shape
    hidden = w_out.shape[0]
    ff = w_up.shape[1]
    total = blocks * rows
    block = lambda cols: pl.BlockSpec((rows, cols), lambda i: (i, 0))
    sums = ((ff, width), (vocab, width), (ROWS, width))
    struct = jax.ShapeDtypeStruct
    return pl.pallas_call(
        tail_kernel,
        grid=(blocks,),
        in_specs=[pl.BlockSpec((join, ROWS, rows // join), lambda i: (i, 0, 0)), block(hidden)]
        + [whole(a.shape) for a in (tab, count, gains, w_out, w_up, w_down)],
        out_specs=[block(width), block(width), block(width), block(ff)] + [whole(s) for s in sums],
        out_shape=[struct((total, width), F32), struct((total, width), BF), struct((total, width), F32), struct((total, ff), BF)]
        + [struct(s, F32) for s in sums],
        scratch_shapes=[
            pltpu.VMEM((vocab, width), BF),
            pltpu.VMEM((rows, ff), F32),
            pltpu.VMEM((rows, ff), BF),
        ],
        compiler_params=pltpu.CompilerParams(
            dimension_semantics=("arbitrary",), vmem_limit_bytes=62 * MIB
        ),
        name="tail_and_head",
    )(ids, state_low, tab, count, gains, w_out, w_up, w_down)


DOWN_SCHEDULE = {1: [(0, 0), (1, 0)], 3: [(0, 1)], 4: [(1, 1)], 5: [(0, 2)], 6: [(1, 2)]}


def mid_kernel(depth, plan, sizes, *refs):
    ids, state_low, mixed, normed, final, lifted, gains, w_out, w_up, small_in, g_down = refs[:11]
    ds_o, g_up, g_out, g_emb, small_o, r_down = refs[11:17]
    loads, send, recv = refs[17:20]
    bufs, at = [], 20
    for n in sizes:
        bufs.append(refs[at : at + n])
        at += n
    step = pl.program_id(0)
    last = pl.num_programs(0) - 1
    spot = place()
    sums = Reduce(plan, depth, (g_down,), False, (r_down,), bufs, loads, send, recv, spot)
    groups = grouped(plan)
    vocab = g_emb.shape[0]

    @pl.when(step == 0)
    def _():
        greet(*spot, depth)
        for i in range(len(plan)):
            sums.begin(i)
        g_up[...] = jnp.zeros_like(g_up)
        g_out[...] = jnp.zeros_like(g_out)
        g_emb[...] = jnp.zeros_like(g_emb)
        small_o[...] = small_in[...]

    for when, acts in DOWN_SCHEDULE.items():

        @pl.when(step == when)
        def _(acts=acts):
            for group, phase in acts:
                for i in groups[group]:
                    sums.act(i, phase)

    d_normed = nt(lifted[...], w_up[...])
    g_up[...] += tn(normed[...], lifted[...])
    value = mixed[...]
    inverse = inv_rms(value)
    small_o[1:2, :] += column_sum(d_normed * (value * inverse))
    d_mixed = final[...] + norm_back(value, inverse, gains[1:2], d_normed)
    mixed_low = d_mixed.astype(BF)
    rest = (d_mixed - mixed_low.astype(F32)).astype(BF)
    ds_o[...] = nt(mixed_low, w_out[...])
    g_out[...] += tn(state_low[...], mixed_low)
    row = jnp.concatenate([ids[n, 0:1, :] for n in range(ids.shape[0])], axis=1)
    hot_t = one_hot_t(row, vocab)
    g_emb[...] += nn(hot_t, mixed_low) + nn(hot_t, rest)

    @pl.when(step == last)
    def _():
        for group in groups:
            for i in group:
                sums.act(i, 3)
        sums.finish()


def run_mid(depth, ids, state_low, mixed, normed, final, lifted, gains, w_out, w_up, small, g_down, vocab):
    blocks, _, rows = ids.shape
    width, ff = w_up.shape
    hidden = w_out.shape[0]
    total = blocks * rows
    block = lambda cols: pl.BlockSpec((rows, cols), lambda i: (i, 0))
    plan = halves([g_down.shape], (2,))
    bufs = [Reduce.sizes(g_down.shape, lo, hi, depth, False) for _, lo, hi, _ in plan]
    dma = lambda *shape: pltpu.SemaphoreType.DMA(shape)
    sums = ((width, ff), (hidden, width), (vocab, width), (ROWS, width), g_down.shape[-2:])
    return pl.pallas_call(
        functools.partial(mid_kernel, depth, plan, [len(b) for b in bufs]),
        grid=(blocks,),
        in_specs=[pl.BlockSpec((1, ROWS, rows), lambda i: (i, 0, 0)), block(hidden)]
        + [block(width)] * 3 + [block(ff)]
        + [whole(a.shape) for a in (gains, w_out, w_up, small)]
        + [pl.BlockSpec(memory_space=pl.ANY)],
        out_specs=[block(hidden)] + [whole(s) for s in sums],
        out_shape=[jax.ShapeDtypeStruct((total, hidden), F32)] + [jax.ShapeDtypeStruct(s, F32) for s in sums],
        scratch_shapes=[dma(len(plan)), dma(len(plan), depth + 2), dma(len(plan), depth + 2)]
        + [b for group in bufs for b in group],
        compiler_params=pltpu.CompilerParams(
            dimension_semantics=("arbitrary",), collective_id=2, has_side_effects=True, vmem_limit_bytes=62 * MIB
        ),
        name="mid_back_and_reduce",
    )(ids, state_low, mixed, normed, final, lifted, gains, w_out, w_up, small, g_down)


def adam_kernel(shapes, small, squares, count, *refs):
    mats = refs[:5]
    weights, firsts, seconds = refs[5:13], refs[13:21], refs[21:29]
    loss_o, count_o, norm_o = refs[29:32]
    new_w, new_m, new_v = refs[32:40], refs[40:48], refs[48:56]
    kernel, bias_rows = shapes
    width = small.shape[1]
    grads = [m[...] for m in mats]
    grads.append(small[0:3, :])
    grads.append(small[ROWS : ROWS + kernel, :])
    base = ROWS + kernel
    grads.append(
        jnp.concatenate([small[base + r : base + r + 1, :] for r in range(bias_rows)], axis=1)
    )
    square = squares[0:1, 0:1]
    for grad in grads[5:]:
        square = square + jnp.sum(jnp.sum(grad * grad, axis=1, keepdims=True), axis=0, keepdims=True)
    norm = jnp.sqrt(square)
    scale = jnp.minimum(1.0, CLIP / (norm + 1e-06))
    norm_o[...] = norm
    loss_o[...] = small[3:4, 0:1]
    count_o[...] = count[0:1, 0:1]
    for i in range(8):
        rate = RATE_MATRIX if i < 5 else RATE_VECTOR
        decay = WEIGHT_DECAY if i < 5 else 0.0
        w, m, v = adam(weights[i][...], grads[i] * scale, firsts[i][...], seconds[i][...], rate, decay)
        new_w[i][...] = w
        new_m[i][...] = m
        new_v[i][...] = v


def run_adam(shapes, mats, small, squares, count, weights, firsts, seconds):
    one = jax.ShapeDtypeStruct((1, 1), F32)
    like = [jax.ShapeDtypeStruct(w.shape, F32) for w in weights]
    args = (small, squares, count) + tuple(mats) + tuple(weights) + tuple(firsts) + tuple(seconds)
    return pl.pallas_call(
        functools.partial(adam_kernel, shapes),
        grid=(1,),
        in_specs=[whole(a.shape) for a in args],
        out_specs=[whole(a.shape) for a in [one] * 3 + like * 3],
        out_shape=[one] * 3 + like * 3,
        compiler_params=pltpu.CompilerParams(vmem_limit_bytes=60 * MIB),
        name="adam_update",
    )(*args)


def spread_ids(tokens, targets, counted, depth):
    seqs, span = tokens.shape
    ways = 2 * depth
    three = jnp.stack([tokens, targets, counted]).reshape(3, ways, seqs // ways, 2, span // 2)
    rows = three.transpose(1, 0, 4, 3, 2).reshape(ways, 3, -1)
    return jnp.pad(rows, ((0, 0), (0, ROWS - 3), (0, 0)))


def body_moved(depth, *args):
    tokens, targets, counted = args[:3]
    weights, firsts, seconds = args[3:11], args[11:19], args[19:27]
    table, w_in, w_out, w_up, w_down, gains, conv_taps, gate_bias = weights
    width = table.shape[1]
    taps = conv_taps[0]
    ids = spread_ids(tokens, targets, counted, depth)
    keep, p, q, conv, queue, state_low, ids, tab, count, *full = run_front(
        depth, ids, table, (w_in[0], w_out[0], w_up[0], w_down[0]), gains, taps, gate_bias
    )
    full = [a.reshape(-1, a.shape[-1]) for a in full]
    mixed, normed, final, lifted, g_down, g_head, small = run_tail(1, ids, state_low, tab, count, gains, *full[1:])
    owned = lambda g: g.reshape((2, 2, depth, 2, -1, g.shape[-1]))
    ds, g_up, g_out, g_emb, small, r_down = run_mid(
        depth, ids, state_low, mixed, normed, final, lifted, gains, full[1], full[2], small, owned(g_down), tab.shape[0]
    )
    r_up, r_out, r_in, r_tab, small, squares = run_backward(
        depth, ids, keep, p, q, ds, conv, queue, tab, gains, taps, full[0], (g_head, g_emb), small, r_down,
        (owned(g_up), owned(g_out)),
    )
    mats = [r_tab, r_in, r_out, r_up, r_down]
    flat = lambda group: [group[0]] + [a[0] for a in group[1:5]] + [group[5], group[6][0], group[7]]
    out = run_adam(
        (conv_taps.shape[1], gate_bias.shape[1] // width),
        mats, small, squares, count, flat(weights), flat(firsts), flat(seconds),
    )
    shaped = [o.reshape(()) for o in out[:3]]
    for i, o in enumerate(out[3:]):
        shaped.append(o.reshape(weights[i % 8].shape))
    return tuple(shaped)


def choose(mesh, *args):
    ways = mesh.shape["seq"]
    seqs, span = args[0].shape
    if mesh.shape["dp"] == 4 and ways == 8 and seqs == 4 * ways and span == LANES:
        return body_moved(ways // 2, *args)
    return body(*args)


def solution(mesh):
    return jax.shard_map(
        functools.partial(choose, mesh),
        mesh=mesh,
        in_specs=(
            P("dp", "seq"),
            P("dp", "seq"),
            P("dp", "seq"),
            P(("dp", "seq"), None),
            P(None, ("dp", "seq"), None),
            P(None, ("dp", "seq"), None),
            P(None, ("dp", "seq"), None),
            P(None, ("dp", "seq"), None),
            P(),
            P(),
            P(),
            P(("dp", "seq"), None),
            P(None, ("dp", "seq"), None),
            P(None, ("dp", "seq"), None),
            P(None, ("dp", "seq"), None),
            P(None, ("dp", "seq"), None),
            P(),
            P(),
            P(),
            P(("dp", "seq"), None),
            P(None, ("dp", "seq"), None),
            P(None, ("dp", "seq"), None),
            P(None, ("dp", "seq"), None),
            P(None, ("dp", "seq"), None),
            P(),
            P(),
            P(),
        ),
        out_specs=(
            P(),
            P(),
            P(),
            P(("dp", "seq"), None),
            P(None, ("dp", "seq"), None),
            P(None, ("dp", "seq"), None),
            P(None, ("dp", "seq"), None),
            P(None, ("dp", "seq"), None),
            P(),
            P(),
            P(),
            P(("dp", "seq"), None),
            P(None, ("dp", "seq"), None),
            P(None, ("dp", "seq"), None),
            P(None, ("dp", "seq"), None),
            P(None, ("dp", "seq"), None),
            P(),
            P(),
            P(),
            P(("dp", "seq"), None),
            P(None, ("dp", "seq"), None),
            P(None, ("dp", "seq"), None),
            P(None, ("dp", "seq"), None),
            P(None, ("dp", "seq"), None),
            P(),
            P(),
            P(),
        ),
        check_vma=False,
    )
```

```python
import functools

import jax
import jax.numpy as jnp
from jax import lax
from jax.experimental import pallas as pl
from jax.experimental.pallas import tpu as pltpu
from jax.sharding import PartitionSpec as P

V = 256
MICRO = 2
STEP = 3


EPS = 1e-06
CLIP = 0.01
BETA_ONE = 0.5
BETA_TWO = 0.5
ADAM_EPS = 1e-08
RATE_MATRIX = 0.03
RATE_VECTOR = 0.3
WEIGHT_DECAY = 0.1


def from_behind(x, axis, by):
    devices = lax.axis_size(axis)
    pairs = [(i, i + by) for i in range(devices) if 0 <= i + by < devices]
    return lax.ppermute(x, axis, pairs)


def carried_in(part, axis, combine, identity, reverse):
    count = lax.axis_size(axis)
    place = lax.axis_index(axis)
    ahead = count - 1 - place if reverse else place
    gathered = jax.tree.map(lambda a: lax.all_gather(a, axis), part)
    state = jax.tree.map(lambda a, e: jnp.zeros_like(a) + jnp.asarray(e, a.dtype), part, identity)

    def one(lap, state):
        source = count - 1 - lap if reverse else lap
        return combine(
            state, jax.tree.map(lambda a: lax.dynamic_index_in_dim(a, source, 0, False), gathered)
        )

    return lax.fori_loop(0, ahead, one, state)


def matmul(left, right):
    return jnp.dot(left, right, preferred_element_type=jnp.float32)


def matmul_tn(left, right):
    return lax.dot_general(
        left, right, (((0,), (0,)), ((), ())), preferred_element_type=jnp.float32
    )


def matmul_nt(left, right):
    return lax.dot_general(
        left, right, (((1,), (1,)), ((), ())), preferred_element_type=jnp.float32
    )


def rms_norm(values, gain):
    return values * lax.rsqrt(jnp.mean(values * values, axis=-1, keepdims=True) + EPS) * gain


def combine(earlier, later):
    return (earlier[0] * later[0], later[0] * earlier[1] + later[1])


def gates(gate, cand):
    return (jax.nn.sigmoid(-gate), jax.nn.sigmoid(gate) * jax.nn.softplus(cand))


def conv_apply(padded, taps, length):
    total = taps[0] * padded[0:length].astype(jnp.float32)
    for k in range(1, taps.shape[0]):
        total = total + taps[k] * padded[k : k + length].astype(jnp.float32)
    return total


def adam(weight, grad, first, second, rate, decay):
    first = BETA_ONE * first + (1.0 - BETA_ONE) * grad
    second = BETA_TWO * second + (1.0 - BETA_TWO) * grad * grad
    fix_one = 1.0 - BETA_ONE**STEP
    fix_two = 1.0 - BETA_TWO**STEP
    update = first / fix_one / (jnp.sqrt(second / fix_two) + ADAM_EPS)
    return (weight - rate * (update + decay * weight), first, second)


def mixer_front(queue, rim, taps, bias, w_in):
    span, seqs, width = queue.shape
    padded = jnp.concatenate([rim, queue], axis=0)
    conv_low = conv_apply(padded, taps, span).astype(jnp.bfloat16)
    pre = matmul(conv_low.reshape(span * seqs, width), w_in).reshape(span, seqs, -1)
    hidden = bias.shape[0]
    keep, write = gates(pre[..., :hidden] + bias, pre[..., hidden:])
    return (padded, conv_low, pre, keep, write)


def block_tail(state, resid, gain_b, w_out, w_up, w_down):
    span, seqs, width = resid.shape
    state_low = state.astype(jnp.bfloat16).reshape(span * seqs, -1)
    mixed = resid + matmul(state_low, w_out).reshape(span, seqs, width)
    normed_low = rms_norm(mixed, gain_b).astype(jnp.bfloat16).reshape(span * seqs, width)
    lifted = matmul(normed_low, w_up)
    active_low = jax.nn.gelu(lifted).astype(jnp.bfloat16)
    result = mixed + matmul(active_low, w_down).reshape(span, seqs, width)
    return (result, (state_low, mixed, normed_low, lifted, active_low))


def layer_forward(resid, taps, gain_a, gain_b, bias, mats):
    span = resid.shape[0]
    kernel = taps.shape[0]
    queue = rms_norm(resid, gain_a).astype(jnp.bfloat16)
    rim = from_behind(queue[span - kernel + 1 :], "seq", 1)
    padded, conv_low, pre, keep, write = mixer_front(queue, rim, taps, bias, mats[0])
    decay, local = lax.associative_scan(combine, (keep, write), axis=0)
    ones = jnp.ones_like(local[0])
    carry_in = carried_in(
        (decay[-1], local[-1]), "seq", combine, (ones, jnp.zeros_like(ones)), False
    )[1]
    state = local + decay * carry_in[None]
    result, unused = block_tail(state, resid, gain_b, mats[1], mats[2], mats[3])
    return (result, rim, carry_in)


def layer_backward(grad, resid, rim, carry_in, taps, gain_a, gain_b, bias, mats):
    w_in, w_out, w_up, w_down = mats
    span, seqs, width = resid.shape
    kernel = taps.shape[0]
    hidden = bias.shape[0]
    normed_a, norm_back = jax.vjp(rms_norm, resid, gain_a)
    queue = normed_a.astype(jnp.bfloat16)
    padded, conv_low, pre, keep, write = mixer_front(queue, rim, taps, bias, w_in)
    decay, local = lax.associative_scan(combine, (keep, write), axis=0)
    state = local + decay * carry_in[None]
    result, (state_low, mixed, normed_low, lifted, active_low) = block_tail(
        state, resid, gain_b, w_out, w_up, w_down
    )
    grad_low = grad.astype(jnp.bfloat16).reshape(span * seqs, width)
    g_down = matmul_tn(active_low, grad_low)
    d_active = matmul_nt(grad_low, w_down)
    d_lifted_low = jax.vjp(jax.nn.gelu, lifted)[1](d_active)[0].astype(jnp.bfloat16)
    g_up = matmul_tn(normed_low, d_lifted_low)
    d_normed = matmul_nt(d_lifted_low, w_up).reshape(span, seqs, width)
    d_mixed, d_gain_b = jax.vjp(rms_norm, mixed, gain_b)[1](d_normed)
    d_mixed = grad + d_mixed
    mixed_low = d_mixed.astype(jnp.bfloat16).reshape(span * seqs, width)
    g_out = matmul_tn(state_low, mixed_low)
    d_state = matmul_nt(mixed_low, w_out).reshape(span, seqs, hidden)
    follow = jnp.concatenate([keep[1:], jnp.ones_like(keep[:1])], axis=0)
    reach, back_local = lax.associative_scan(combine, (follow, d_state), axis=0, reverse=True)
    ones = jnp.ones_like(keep[0])
    summary = (keep[0] * reach[0], keep[0] * back_local[0])
    carry_out = carried_in(summary, "seq", combine, (ones, jnp.zeros_like(ones)), True)[1]
    adjoint = back_local + reach * carry_out[None]
    before = jnp.concatenate([carry_in[None], state[:-1]], axis=0)
    d_gate, d_cand = jax.vjp(gates, pre[..., :hidden] + bias, pre[..., hidden:])[1](
        (adjoint * before, adjoint)
    )
    d_bias = jnp.sum(d_gate, axis=(0, 1))
    d_pre = (
        jnp.concatenate([d_gate, d_cand], axis=-1)
        .astype(jnp.bfloat16)
        .reshape(span * seqs, 2 * hidden)
    )
    g_in = matmul_tn(conv_low.reshape(span * seqs, width), d_pre)
    d_conv = matmul_nt(d_pre, w_in).reshape(span, seqs, width)
    beyond = from_behind(d_conv[: kernel - 1].astype(jnp.bfloat16), "seq", -1).astype(jnp.float32)
    extended = jnp.concatenate([d_conv, beyond], axis=0)
    d_queue = taps[0] * extended[kernel - 1 : kernel - 1 + span]
    tap_grads = [jnp.sum(d_conv * padded[0:span].astype(jnp.float32), axis=(0, 1))]
    for k in range(1, kernel):
        d_queue = d_queue + taps[k] * extended[kernel - 1 - k : kernel - 1 - k + span]
        tap_grads.append(jnp.sum(d_conv * padded[k : k + span].astype(jnp.float32), axis=(0, 1)))
    rounded = lax.optimization_barrier(d_queue.astype(jnp.bfloat16)).astype(jnp.float32)
    d_resid, d_gain_a = norm_back(rounded)
    return (
        d_mixed + d_resid,
        (g_in, g_out, g_up, g_down),
        (jnp.stack(tap_grads), d_gain_a, d_gain_b, d_bias),
    )


def body(
    tokens,
    targets,
    counted,
    table,
    w_in,
    w_out,
    w_up,
    w_down,
    gains,
    conv_taps,
    gate_bias,
    m_table,
    m_in,
    m_out,
    m_up,
    m_down,
    m_gains,
    m_taps,
    m_bias,
    v_table,
    v_in,
    v_out,
    v_up,
    v_down,
    v_gains,
    v_taps,
    v_bias,
):
    layers = w_in.shape[0]
    seq_dev, span = tokens.shape
    rows = seq_dev // MICRO
    width = table.shape[1]
    vocab = V
    mask = counted.astype(jnp.float32)
    count = lax.psum(jnp.sum(mask), ("dp", "seq"))
    shards = (
        w_in.astype(jnp.bfloat16),
        w_out.astype(jnp.bfloat16),
        w_up.astype(jnp.bfloat16),
        w_down.astype(jnp.bfloat16),
    )
    layer_gains = gains[: 2 * layers].reshape(layers, 2, width)
    columns = jnp.arange(vocab, dtype=jnp.int32)

    def forward_step(resid, inputs):
        pieces, taps, pair, bias = inputs
        mats = (
            lax.all_gather(pieces[0], ("dp", "seq"), axis=0, tiled=True),
            lax.all_gather(pieces[1], ("dp", "seq"), axis=0, tiled=True),
            lax.all_gather(pieces[2], ("dp", "seq"), axis=0, tiled=True),
            lax.all_gather(pieces[3], ("dp", "seq"), axis=0, tiled=True),
        )
        result, rim, carry_in = layer_forward(resid, taps, pair[0], pair[1], bias, mats)
        return (result, (resid, rim, carry_in))

    def backward_step(grad, inputs):
        saved, pieces, taps, pair, bias = inputs
        mats = (
            lax.all_gather(pieces[0], ("dp", "seq"), axis=0, tiled=True),
            lax.all_gather(pieces[1], ("dp", "seq"), axis=0, tiled=True),
            lax.all_gather(pieces[2], ("dp", "seq"), axis=0, tiled=True),
            lax.all_gather(pieces[3], ("dp", "seq"), axis=0, tiled=True),
        )
        grad, full, small = layer_backward(
            grad, saved[0], saved[1], saved[2], taps, pair[0], pair[1], bias, mats
        )
        full = (
            lax.psum_scatter(full[0], ("dp", "seq"), scatter_dimension=0, tiled=True),
            lax.psum_scatter(full[1], ("dp", "seq"), scatter_dimension=0, tiled=True),
            lax.psum_scatter(full[2], ("dp", "seq"), scatter_dimension=0, tiled=True),
            lax.psum_scatter(full[3], ("dp", "seq"), scatter_dimension=0, tiled=True),
        )
        return (grad, (full, small))

    loss = jnp.zeros((), jnp.float32)
    g_table = jnp.zeros((vocab, width), jnp.float32)
    acc_full = None
    acc_small = None
    for index in range(MICRO):
        tok = tokens[index * rows : (index + 1) * rows].T.reshape(-1)
        tgt = targets[index * rows : (index + 1) * rows].T.reshape(-1)
        weights = mask[index * rows : (index + 1) * rows].T.reshape(-1)
        tab = lax.all_gather(table.astype(jnp.bfloat16), ("dp", "seq"), axis=0, tiled=True)
        picks = tok[:, None] == columns[None, :]
        resid = matmul(picks.astype(jnp.bfloat16), tab).reshape(span, rows, width)
        final, saved = lax.scan(forward_step, resid, (shards, conv_taps, layer_gains, gate_bias))
        normed_f, final_back = jax.vjp(rms_norm, final, gains[2 * layers])
        normed_low = normed_f.astype(jnp.bfloat16).reshape(span * rows, width)
        logits = matmul_nt(normed_low, tab)
        top = jnp.max(logits, axis=-1, keepdims=True)
        lse = jnp.log(jnp.sum(jnp.exp(logits - top), axis=-1)) + top[:, 0]
        hits = (tgt[:, None] == columns[None, :]).astype(jnp.float32)
        picked = jnp.sum(hits * logits, axis=-1)
        loss = loss + jnp.sum(weights * (lse - picked))
        d_logits = ((jnp.exp(logits - lse[:, None]) - hits) * (weights / count)[:, None]).astype(
            jnp.bfloat16
        )
        g_table = g_table + matmul_tn(d_logits, normed_low)
        d_normed = matmul(d_logits, tab).reshape(span, rows, width)
        d_final, d_gain_f = final_back(d_normed)
        grad0, (full, small) = lax.scan(
            backward_step, d_final, (saved, shards, conv_taps, layer_gains, gate_bias), reverse=True
        )
        g_table = g_table + lax.dot_general(
            picks.astype(jnp.float32),
            grad0.reshape(span * rows, width),
            (((0,), (0,)), ((), ())),
            precision=lax.Precision.HIGHEST,
        )
        layer_gain_grads = jnp.stack([small[1], small[2]], axis=1).reshape(2 * layers, width)
        vectors = (jnp.concatenate([layer_gain_grads, d_gain_f[None]], axis=0), small[0], small[3])
        if index == 0:
            acc_full, acc_small = (full, vectors)
        else:
            acc_full = jax.tree.map(lambda a, b: a + b, acc_full, full)
            acc_small = jax.tree.map(lambda a, b: a + b, acc_small, vectors)
    table_shard = lax.psum_scatter(g_table, ("dp", "seq"), scatter_dimension=0, tiled=True)
    g_gains, g_taps, g_bias = lax.psum((acc_small[0], acc_small[1], acc_small[2]), ("dp", "seq"))
    matrices = (table_shard, acc_full[0], acc_full[1], acc_full[2], acc_full[3])
    squares = jnp.zeros((), jnp.float32)
    for grad in matrices:
        squares = squares + jnp.sum(grad * grad)
    squares_all, loss_all = lax.psum((squares, loss), ("dp", "seq"))
    small_squares = jnp.sum(g_gains * g_gains) + jnp.sum(g_taps * g_taps) + jnp.sum(g_bias * g_bias)
    norm = jnp.sqrt(squares_all + small_squares)
    scale = jnp.minimum(1.0, CLIP / (norm + 1e-06))
    params = (table, w_in, w_out, w_up, w_down, gains, conv_taps, gate_bias)
    grads = matrices + (g_gains, g_taps, g_bias)
    firsts = (m_table, m_in, m_out, m_up, m_down, m_gains, m_taps, m_bias)
    seconds = (v_table, v_in, v_out, v_up, v_down, v_gains, v_taps, v_bias)
    news, next_m, next_v = ([], [], [])
    for index in range(8):
        rate = RATE_MATRIX if index < 5 else RATE_VECTOR
        decay = WEIGHT_DECAY if index < 5 else 0.0
        weight, first, second = adam(
            params[index], grads[index] * scale, firsts[index], seconds[index], rate, decay
        )
        news.append(weight)
        next_m.append(first)
        next_v.append(second)
    return (
        loss_all,
        count,
        norm,
        news[0],
        news[1],
        news[2],
        news[3],
        news[4],
        news[5],
        news[6],
        news[7],
        next_m[0],
        next_m[1],
        next_m[2],
        next_m[3],
        next_m[4],
        next_m[5],
        next_m[6],
        next_m[7],
        next_v[0],
        next_v[1],
        next_v[2],
        next_v[3],
        next_v[4],
        next_v[5],
        next_v[6],
        next_v[7],
    )


BF = jnp.bfloat16
F32 = jnp.float32
MIB = 1 << 20
LANES = 128
ROWS = 8
GELU_A = 0.7978845608028654
GELU_B = 0.044715
LOG2E = 1.4426950408889634


def nn(left, right):
    return jnp.dot(left, right, preferred_element_type=F32)


def tn(left, right):
    return lax.dot_general(left, right, (((0,), (0,)), ((), ())), preferred_element_type=F32)


def nt(left, right):
    return lax.dot_general(left, right, (((1,), (1,)), ((), ())), preferred_element_type=F32)


def inv_rms(values):
    return lax.rsqrt(jnp.mean(values * values, axis=-1, keepdims=True) + EPS)


def norm_back(values, inverse, gain, grad):
    width = values.shape[-1]
    scaled = grad * gain
    dot = jnp.sum(scaled * values, axis=-1, keepdims=True)
    return inverse * scaled - values * (inverse * inverse * inverse * dot * (1.0 / width))


def column_sum(values):
    return jnp.sum(values, axis=0, keepdims=True)


def swap_halves(tile):
    return pltpu.roll(tile, ROWS // 2, tile.ndim - 2)


def one_hot(column, vocab):
    lane = lax.broadcasted_iota(jnp.int32, (column.shape[0], vocab), 1)
    return (column == lane).astype(F32).astype(BF)


def one_hot_t(row, vocab):
    place = lax.broadcasted_iota(jnp.int32, (vocab, row.shape[1]), 0)
    return (row == place).astype(F32).astype(BF)


def whole(shape):
    zeros = (0,) * len(shape)
    return pl.BlockSpec(shape, lambda i: zeros, pipeline_mode=pl.Buffered(1))


def place():
    dp = lax.axis_index("dp")
    seq = lax.axis_index("seq")
    return dp // 2, dp % 2, seq // 2, seq % 2


def device(y, x, z, core):
    return (y * 2 + x, z * 2 + core)


def greet(y, x, z, core, depth):
    barrier = pltpu.get_barrier_semaphore()
    peers = [device(1 - y, x, z, core), device(y, 1 - x, z, core), device(1 - y, 1 - x, z, core)]
    for dz in range(depth):
        for dc in range(2):
            if dz or dc:
                peers.append(device(y, x, (z + dz) % depth, (core + dc) % 2))
    for peer in peers:
        pl.semaphore_signal(barrier, inc=1, device_id=peer, device_id_type=pl.DeviceIdType.MESH)
    pl.semaphore_wait(barrier, len(peers))


def remote(src, dst, send, recv, peer):
    return pltpu.make_async_remote_copy(
        src_ref=src,
        dst_ref=dst,
        send_sem=send,
        recv_sem=recv,
        device_id=peer,
        device_id_type=pl.DeviceIdType.MESH,
    )


def in_order(groups, phases, act):
    for time in range(len(groups) + phases - 1):
        for phase in range(phases - 1, -1, -1):
            at = time - phase
            if 0 <= at < len(groups):
                for item in groups[at]:
                    act(item, phase)


def grouped(plan):
    return [[i, i + 1] for i in range(0, len(plan), 2)]


class Gather:
    def __init__(self, plan, depth, sources, outs, send, recv, at):
        self.plan, self.depth, self.sources, self.outs, self.send, self.recv = plan, depth, sources, outs, send, recv
        self.y, self.x, self.z, self.core = at

    def copies(self, i, phase):
        t, lo, hi, along_x = self.plan[i]
        cols = pl.ds(lo, hi - lo)
        y, x, z, core = self.y, self.x, self.z, self.core
        out = self.outs[t]
        by_x, by_y = device(y, 1 - x, z, core), device(1 - y, x, z, core)
        if phase == 0:
            mine = out.at[y, x, z, core, :, cols]
            source = mine if self.sources[t] is None else self.sources[t].at[:, cols]
            moves = [(source, mine, device(y, x, (z + dz) % self.depth, core)) for dz in range(1, self.depth)]
        elif phase == 1:
            part = out.at[y, x, :, core, :, cols]
            moves = [(part, part, by_x if along_x else by_y)]
        elif phase == 2:
            part = out.at[y, :, :, core, :, cols] if along_x else out.at[:, x, :, core, :, cols]
            moves = [(part, part, by_y if along_x else by_x)]
        else:
            part = out.at[:, :, :, core, :, cols]
            moves = [(part, part, device(y, x, z, 1 - core))]
        base = 0 if phase == 0 else self.depth - 2 + phase
        return [
            remote(src, dst, self.send.at[i, base + n], self.recv.at[i, base + n], peer)
            for n, (src, dst, peer) in enumerate(moves)
        ]

    def begin(self, i):
        for copy in self.copies(i, 0):
            copy.start()

    def act(self, i, phase):
        for copy in self.copies(i, phase):
            copy.wait_recv()
        if phase < 3:
            for copy in self.copies(i, phase + 1):
                copy.start()

    def finish(self):
        for i in range(len(self.plan)):
            for phase in range(4):
                for copy in self.copies(i, phase):
                    copy.wait_send()


def add_into(target, other):
    lead = target.shape[: len(target.shape) - 2]
    total = 1
    for d in lead:
        total *= d

    def one(i, _):
        index = []
        for d in reversed(lead):
            index.append(lax.rem(i, d))
            i = lax.div(i, d)
        index = tuple(reversed(index))
        target[index] = target[index] + other[index]
        return _

    lax.fori_loop(0, total, one, 0)


def halves(shapes, cuts=None):
    plan = []
    for t, shape in enumerate(shapes):
        pieces = 2 * (cuts[t] if cuts else 1)
        wide = shape[-1] // pieces
        for n in range(pieces):
            plan.append((t, n * wide, (n + 1) * wide, n % 2 == 0))
    return plan


class Reduce:
    def __init__(self, plan, depth, source, resident, out, refs, at):
        self.plan, self.depth, self.source, self.resident, self.out = plan, depth, source, resident, out
        self.send, self.recv = refs[:2]
        if not resident:
            self.loads, self.own = refs[2:4]
        first = 2 if resident else 4
        self.bufs = [refs[first + 3 * i : first + 3 * i + 3] for i in range(len(plan))]
        self.y, self.x, self.z, self.core = at

    def scratch(shape, plan, depth, resident):
        piece = (shape[-2], plan[0][2] - plan[0][1])
        dma = lambda *n: pltpu.SemaphoreType.DMA(n)
        own = [] if resident else [dma(len(plan)), pltpu.VMEM((2, 2, depth) + piece, F32)]
        each = [
            pltpu.VMEM((2, 2, depth) + piece, F32), pltpu.VMEM((2, depth) + piece, F32), pltpu.VMEM((2, depth) + piece, F32)
        ]
        return [dma(len(plan), depth + 2), dma(len(plan), depth + 2)] + own + each * len(plan)

    def load(self, i):
        t, lo, hi, _ = self.plan[i]
        source = self.source.at[:, :, :, self.core, :, pl.ds(lo, hi - lo)]
        return pltpu.make_async_copy(source, self.own, self.loads.at[i])

    def copies(self, i, phase):
        t, lo, hi, along_x = self.plan[i]
        y, x, z, core = self.y, self.x, self.z, self.core
        whole, half, quarter = self.bufs[i]
        by_x, by_y = device(y, 1 - x, z, core), device(1 - y, x, z, core)
        if phase == 0:
            source = self.source.at[:, :, :, 1 - core, :, pl.ds(lo, hi - lo)]
            moves = [(source, whole, device(y, x, z, 1 - core))]
        elif phase == 1:
            moves = [(whole.at[1 - y], half, by_y) if along_x else (whole.at[:, 1 - x], half, by_x)]
        elif phase == 2:
            moves = [(half.at[1 - x], quarter.at[0], by_x) if along_x else (half.at[1 - y], quarter.at[0], by_y)]
        else:
            moves = []
            for dz in range(1, self.depth):
                pz = (z + dz) % self.depth
                moves.append((quarter.at[0, pz], quarter.at[1, dz], device(y, x, pz, core)))
        return [
            remote(src, dst, self.send.at[i, phase + n], self.recv.at[i, phase + n], peer)
            for n, (src, dst, peer) in enumerate(moves)
        ]

    def begin(self):
        for i in range(len(self.plan)):
            for copy in self.copies(i, 0):
                copy.start()
        if not self.resident:
            self.load(0).start()

    def pair(self, n, phase):
        for i in (2 * n, 2 * n + 1):
            self.act(i, phase)

    def act(self, i, phase):
        t, lo, hi, along_x = self.plan[i]
        y, x, z, core = self.y, self.x, self.z, self.core
        whole, half, quarter = self.bufs[i]
        for copy in self.copies(i, phase):
            copy.wait_recv()
        if phase == 0:
            if self.resident:
                add_into(whole, self.source.at[:, :, :, core, :, pl.ds(lo, hi - lo)])
            else:
                self.load(i).wait()
                add_into(whole, self.own)
                if i + 1 < len(self.plan):
                    self.load(i + 1).start()
        elif phase == 1:
            add_into(half, whole.at[y] if along_x else whole.at[:, x])
        elif phase == 2:
            add_into(quarter.at[0], half.at[x] if along_x else half.at[y])
        else:
            total = quarter[0, z]
            for dz in range(1, self.depth):
                total = total + quarter[1, dz]
            self.out[:, lo:hi] = total
            return
        for copy in self.copies(i, phase + 1):
            copy.start()

    def finish(self):
        for i in range(len(self.plan)):
            for phase in range(4):
                for copy in self.copies(i, phase):
                    copy.wait_send()


class Everywhere:
    def __init__(self, slots, sends, recvs, depth, at):
        y, x, z, core = at
        self.slots, self.ways = slots, 2 * depth
        self.me, self.other = z * 2 + core, self.ways + y * 2 + x
        self.near, self.far = [], []
        mine = slots.at[self.me]
        for dz in range(depth):
            for dc in range(2):
                if dz or dc:
                    n = dz * 2 + dc
                    peer = device(y, x, (z + dz) % depth, (core + dc) % 2)
                    self.near.append(remote(mine, mine, sends.at[n], recvs.at[n], peer))
        mine = slots.at[self.other]
        for n, (dy, dx) in enumerate(((0, 1), (1, 0), (1, 1))):
            n += self.ways
            peer = device((y + dy) % 2, (x + dx) % 2, z, core)
            self.far.append(remote(mine, mine, sends.at[n], recvs.at[n], peer))

    def total(self, lo, hi):
        value = self.slots[lo]
        for n in range(lo + 1, hi):
            value = value + self.slots[n]
        return value

    def begin(self, value):
        self.slots[self.me] = value
        for copy in self.near:
            copy.start()

    def middle(self):
        for copy in self.near:
            copy.wait()
        self.slots[self.other] = self.total(0, self.ways)
        for copy in self.far:
            copy.start()

    def end(self):
        for copy in self.far:
            copy.wait()
        return self.total(self.ways, self.ways + 4)


class EverywhereHalved:
    def __init__(self, whole, parts, sends, recvs, depth, at):
        y, x, z, core = at
        self.whole, self.parts, self.depth, self.core = whole, parts, depth, core
        other = device(y, x, z, 1 - core)
        self.first = remote(whole.at[0], whole.at[1], sends.at[0], recvs.at[0], other)
        self.spot = (z, depth + y * 2 + x)
        self.along, self.plane = [], []
        mine = parts.at[z]
        for dz in range(1, depth):
            peer = device(y, x, (z + dz) % depth, core)
            self.along.append(remote(mine, mine, sends.at[dz], recvs.at[dz], peer))
        mine = parts.at[self.spot[1]]
        for n, (dy, dx) in enumerate(((0, 1), (1, 0), (1, 1))):
            peer = device((y + dy) % 2, (x + dx) % 2, z, core)
            self.plane.append(remote(mine, mine, sends.at[depth + n], recvs.at[depth + n], peer))
        mine = whole.at[2, core]
        self.last = remote(mine, mine, sends.at[depth + 3], recvs.at[depth + 3], other)

    def total(self, lo, hi):
        value = self.parts[lo]
        for n in range(lo + 1, hi):
            value = value + self.parts[n]
        return value

    def step(self, n, value=None):
        if n == 0:
            self.whole[0] = value.reshape(self.whole.shape[1:])
            self.first.start()
        elif n == 1:
            self.first.wait()
            lower = self.whole[self.core, self.core] + self.whole[1 - self.core, self.core]
            self.parts[self.spot[0]] = lower
            for copy in self.along:
                copy.start()
        elif n == 2:
            for copy in self.along:
                copy.wait()
            self.parts[self.spot[1]] = self.total(0, self.depth)
            for copy in self.plane:
                copy.start()
        elif n == 3:
            for copy in self.plane:
                copy.wait()
            self.whole[2, self.core] = self.total(self.depth, self.depth + 4)
            self.last.start()
        else:
            self.last.wait()
            return self.whole[2].reshape(-1, self.whole.shape[-1])


SCHEDULE = {
    1: [(0, 0, 0)], 3: [(0, 1, 0)], 5: [(0, 2, 0)], 7: [(0, 0, 1)], 8: [(0, 3, 0), (0, 1, 1)], 9: [(1, 0, 0)],
    10: [(0, 0, 2), (0, 2, 1)], 11: [(0, 1, 2), (0, 3, 1)], 13: [(0, 2, 2)], 14: [(0, 3, 2), (1, 0, 1)],
}
LEFT_OVER = [
    (2, 0, 0), (3, 0, 1), (1, 0, 2), (2, 0, 1), (3, 0, 2), (2, 0, 2), (3, 0, 3), (0, 0, 3), (0, 1, 3), (0, 2, 3), (0, 3, 3),
    (1, 0, 3), (2, 0, 3),
]


def last_kernel(depth, plans, counts, *refs):
    ids, d_pre, state_low, mixed_low, tab, gains, taps, w_in, g_tab_a, g_tab_b, small_in, r_down, r_up, g_in = refs[:14]
    r_in, r_out, r_tab, small_o, squares_o = refs[14:19]
    small, g_out, g_tab, qtab, ext, head_s, hot_sum = refs[19:26]
    whole_s, part_s, sq_slots, sends, recvs, sq_sends, sq_recvs = refs[26:33]
    spot = place()
    sums, at = [], 33
    for n, (source, out) in enumerate(((g_in, r_in), (g_out, r_out), (g_tab, r_tab))):
        sums.append(Reduce(plans[n], depth, source, n > 0, out, refs[at : at + counts[n]], spot))
        at += counts[n]
    smalls = EverywhereHalved(whole_s, part_s, sends, recvs, depth, spot)
    squares = Everywhere(sq_slots, sq_sends, sq_recvs, depth, spot)
    step = pl.program_id(0)
    blocks = pl.num_programs(0) // 2
    rows = d_pre.shape[0]
    vocab, width = tab.shape
    kernel = taps.shape[0]
    rim = (kernel - 1) * ROWS

    def run(acts):
        for n, pair, phase in acts:
            if n == 3:
                smalls.step(phase)
            else:
                sums[n].pair(pair, phase)

    @pl.when(step == 0)
    def _():
        greet(*spot, depth)
        sums[0].begin()
        wide = tab[...].astype(BF).astype(F32)
        qtab[...] = (wide * inv_rms(wide) * gains[0:1]).astype(BF)
        g_out[...] = jnp.zeros_like(g_out)
        hot_sum[...] = jnp.zeros_like(hot_sum)
        small[...] = jnp.zeros_like(small)
        small[0:ROWS, :] = small_in[...]
        head_s[...] = jnp.zeros_like(head_s)

    for when, acts in SCHEDULE.items():

        @pl.when(step == when)
        def _(acts=acts):
            run(acts)

    @pl.when(step < blocks)
    def _():
        g_out[...] += tn(state_low[...], mixed_low[...]).reshape(g_out.shape)

    @pl.when(step == blocks - 1)
    def _():
        sums[1].begin()

    @pl.when(step >= blocks)
    def _():
        ext[0:rows, :] = nt(d_pre[...], w_in[...])
        half = lax.broadcasted_iota(jnp.int32, (rim, width), 0) % ROWS < ROWS // 2
        mine = ext[0:rim, :]
        ext[rows:, :] = jnp.where(
            half,
            swap_halves(mine.reshape(kernel - 1, ROWS, width)).reshape(rim, width),
            swap_halves(head_s[...].reshape(kernel - 1, ROWS, width)).reshape(rim, width),
        )
        head_s[...] = mine
        here = ids[0]
        known = nn(one_hot(here.T[:, 0:1], vocab), qtab[...])
        d_queue = None
        for k in range(kernel):
            shift = (kernel - 1 - k) * ROWS
            part = ext[shift : shift + rows, :]
            term = taps[k : k + 1] * part
            d_queue = term if d_queue is None else d_queue + term
            small[ROWS + k : ROWS + k + 1, :] += column_sum(part * known)
        hot_t = one_hot_t(here[0:1, :], vocab)
        hot_sum[...] += nn(hot_t, d_queue.astype(BF))

    @pl.when(step == 2 * blocks - 1)
    def _():
        wide = tab[...].astype(BF).astype(F32)
        inverse = inv_rms(wide)
        total = hot_sum[...]
        g_tab[...] = (
            g_tab_a[...] + g_tab_b[...] + norm_back(wide, inverse, gains[0:1], total)
        ).reshape(g_tab.shape)
        sums[2].begin()
        small[0:1, :] = column_sum(total * (wide * inverse))
        smalls.step(0, small[...])
        run(LEFT_OVER)
        square = jnp.zeros((1, 1), F32)
        for out in (r_in, r_out, r_tab, r_down, r_up):
            value = out[...]
            square = square + jnp.sum(jnp.sum(value * value, axis=1, keepdims=True), axis=0, keepdims=True)
        squares.begin(jnp.broadcast_to(square, (ROWS, LANES)))
        small_o[...] = smalls.step(4)
        squares.middle()
        squares_o[...] = squares.end()
        for one in sums:
            one.finish()


def run_last(depth, ids, d_pre, state_low, mixed_low, tab, gains, taps, w_in, g_tabs, small, done, g_in):
    blocks, _, rows = ids.shape
    vocab, width = tab.shape
    kernel = taps.shape[0]
    rim = (kernel - 1) * ROWS
    last = blocks - 1
    owners = (2, 2, depth, 2)
    hidden = state_low.shape[1]
    shapes = (g_in.shape, owners + (hidden // (8 * depth), width), owners + (vocab // (8 * depth), width))
    plans = [halves([shape], (cuts,)) for shape, cuts in zip(shapes, (4, 1, 1))]
    back = lambda i: jnp.minimum(2 * blocks - 1 - i, last)
    once = lambda cols: pl.BlockSpec((rows, cols), lambda i: (jnp.minimum(i, last), 0))
    moving = [Reduce.scratch(shape, plan, depth, n > 0) for n, (shape, plan) in enumerate(zip(shapes, plans))]
    out = [s[-2:] for s in shapes] + [(2 * ROWS, width), (ROWS, LANES)]
    dma = lambda *shape: pltpu.SemaphoreType.DMA(shape)
    fixed = (tab, gains, taps, w_in) + tuple(g_tabs) + (small,) + tuple(done)
    return pl.pallas_call(
        functools.partial(last_kernel, depth, plans, [len(m) for m in moving]),
        grid=(2 * blocks,),
        in_specs=[
            pl.BlockSpec((1, ROWS, rows), lambda i: (back(i), 0, 0)),
            pl.BlockSpec((rows, d_pre.shape[1]), lambda i: (back(i), 0)),
            once(hidden),
            once(width),
        ]
        + [whole(a.shape) for a in fixed]
        + [pl.BlockSpec(memory_space=pl.ANY)],
        out_specs=[whole(s) for s in out],
        out_shape=[jax.ShapeDtypeStruct(s, F32) for s in out],
        scratch_shapes=[
            pltpu.VMEM((2 * ROWS, width), F32),
            pltpu.VMEM(shapes[1], F32),
            pltpu.VMEM(shapes[2], F32),
            pltpu.VMEM((vocab, width), BF),
            pltpu.VMEM((rim + rows, width), F32),
            pltpu.VMEM((rim, width), F32),
            pltpu.VMEM((vocab, width), F32),
            pltpu.VMEM((3, 2, ROWS, width), F32),
            pltpu.VMEM((depth + 4, ROWS, width), F32),
            pltpu.VMEM((2 * depth + 4, ROWS, LANES), F32),
            dma(depth + 4),
            dma(depth + 4),
            dma(2 * depth + 4),
            dma(2 * depth + 4),
        ]
        + [piece for group in moving for piece in group],
        compiler_params=pltpu.CompilerParams(
            dimension_semantics=("arbitrary",), collective_id=1, has_side_effects=True, vmem_limit_bytes=62 * MIB
        ),
        name="last_back_and_reduce",
    )(ids, d_pre, state_low, mixed_low, *fixed, g_in)


def conv_block(block, ids_s, qtab, taps, conv_s, padq, tail_s):
    _, rows, width = conv_s.shape
    vocab = qtab.shape[0]
    kernel = taps.shape[0]
    rim = (kernel - 1) * ROWS
    queue = nn(one_hot(id_column(ids_s[block], 0), vocab), qtab[...])
    padq[rim:, :] = queue
    half = lax.broadcasted_iota(jnp.int32, (rim, width), 0) % ROWS < ROWS // 2
    before = tail_s[...].reshape(kernel - 1, ROWS, width)
    latest = padq[rows:, :].reshape(kernel - 1, ROWS, width)
    padq[0:rim, :] = jnp.where(
        half, swap_halves(before).reshape(rim, width), swap_halves(latest).reshape(rim, width)
    )
    tail_s[...] = padq[rows:, :]
    conv = taps[0:1] * padq[0:rows, :]
    for k in range(1, kernel):
        conv = conv + taps[k : k + 1] * padq[k * ROWS : k * ROWS + rows, :]
    conv_s[block] = conv.astype(BF)


def id_column(ids, which):
    turned = ids.T
    return jnp.concatenate([turned[:, 2 * which : 2 * which + 1], turned[:, 2 * which + 1 : 2 * which + 2]], axis=0)


def front_block(conv, bias, w_in, keep_o, p_o, q_o, state_o, carry_s, big):
    rows, hidden = keep_o.shape
    steps = rows // ROWS
    chunk = 256
    low_half = lax.broadcasted_iota(jnp.int32, (ROWS, chunk), 0) < ROWS // 2
    for j in range(hidden // chunk):
        cols = slice(j * chunk, (j + 1) * chunk)
        gate = nn(conv[...], w_in[:, j * chunk : (j + 1) * chunk]) + bias[0:1, cols]
        cand = nn(conv[...], w_in[:, hidden + j * chunk : hidden + (j + 1) * chunk])
        grown = jnp.exp2(jnp.minimum(gate * -LOG2E, 120.0))
        write_gate = pl.reciprocal(1.0 + grown)
        keep_o[:, cols] = grown * write_gate
        small = jnp.exp2(jnp.abs(cand) * -LOG2E)
        one_more = 1.0 + small
        soft = jnp.maximum(cand, 0.0) + (jnp.log(one_more) + (small - (one_more - 1.0)))
        p_o[:, cols] = write_gate
        q_o[:, cols] = write_gate * jnp.exp2((cand - soft) * LOG2E)
        big[:, cols] = write_gate * soft

        carry = carry_s[:, cols]
        end = carry
        for tau in range(steps):
            at = slice(tau * ROWS, (tau + 1) * ROWS)
            end = keep_o[at, cols] * end + big[at, cols]
        state = jnp.where(low_half, carry, swap_halves(end))
        for tau in range(steps):
            at = slice(tau * ROWS, (tau + 1) * ROWS)
            change = big[at, cols] - p_o[at, cols] * state
            p_o[at, cols] = keep_o[at, cols] * change
            state = state + change
            big[at, cols] = state
        state_o[:, cols] = big[:, cols].astype(BF)
        carry_s[:, cols] = jnp.where(low_half, swap_halves(state), 0.0)


GATHER_SCHEDULE = {1: [(2, 0), (0, 1)], 2: [(1, 1), (3, 0), (4, 0)], 3: [(2, 1), (0, 2)], 4: [(3, 1), (1, 2)], 5: [(4, 1), (2, 2)], 6: [(3, 2)], 7: [(4, 2)]}
GATHER_LAST = [(0, 3), (1, 3), (2, 3), (3, 3), (4, 3)]


def front_kernel(
    depth, now, later,
    ids, table, w_in, w_out, w_up, w_down, gains, taps, bias,
    keep_o, p_o, q_o, state_o, ids_o, tab_o, count_o, conv_o, w_in_o, w_out_o, w_up_o, w_down_o,
    ids_s, tab_s, count_s, in_s, out_s, up_s, down_s, qtab, conv_s, padq, tail_s, carry_s, big,
    ids_send, ids_recv, now_send, now_recv, later_send, later_recv, own_sem, in_sem,
):
    step = pl.program_id(0)
    blocks = pl.num_programs(0)
    spot = place()
    y, x, z, core = spot
    me = z * 2 + core
    onward = [
        pltpu.make_async_copy(in_s, w_in_o, in_sem.at[0]),
        pltpu.make_async_copy(conv_s, conv_o, in_sem.at[1]),
    ]
    first = Gather(now, depth, [None] * 3, [tab_s, count_s, in_s], now_send, now_recv, spot)
    rest = Gather(later, depth, [out_s, up_s, down_s], [w_out_o, w_up_o, w_down_o], later_send, later_recv, spot)
    later_groups = grouped(later)
    own = [
        pltpu.make_async_copy(src, dst.at[y, x, z, core], own_sem.at[n])
        for n, (src, dst) in enumerate(((out_s, w_out_o), (up_s, w_up_o), (down_s, w_down_o)))
    ]
    spread = []
    for dz in range(depth):
        for dc in range(2):
            if dz or dc:
                pz, pc = (z + dz) % depth, (core + dc) % 2
                n = dz * 2 + dc
                spread.append(
                    remote(ids.at[pz * 2 + pc], ids_s.at[me], ids_send.at[n], ids_recv.at[n], device(y, x, pz, pc))
                )

    @pl.when(step == 0)
    def _():
        half = table.shape[1] // 2
        tab_s[y, x, z, core] = jnp.concatenate([table[:, 0:half], table[:, half:]], axis=0).astype(BF)
        share = jnp.zeros((2, ids.shape[2]), F32)
        for n in range(ids.shape[0]):
            share = share + ids[n, 4:6, :].astype(F32)
        share = jnp.sum(jnp.sum(share, axis=1, keepdims=True), axis=0, keepdims=True)
        count_s[y, x, z, core] = jnp.broadcast_to(share, count_o.shape)
        in_s[y, x, z, core] = w_in[...].astype(BF)
        ids_s[me] = ids[me]
        greet(*spot, depth)
        pairs = [(i, i + 1) for i in range(0, len(now), 2)]

        def act(pair, phase):
            for i in pairs[pair]:
                first.act(i, phase)

        def begin(pair):
            for i in pairs[pair]:
                first.begin(i)

        begin(0)
        for copy in spread:
            copy.start()
        begin(1)
        begin(2)
        act(0, 0)
        out_s[...] = w_out[...].astype(BF)
        up_s[...] = w_up[...].astype(BF)
        down_s[...] = w_down[...].astype(BF)
        for copy in own:
            copy.start()
        act(1, 0)
        begin(3)
        act(0, 1)
        act(2, 0)
        begin(4)
        act(1, 1)
        act(0, 2)
        act(3, 0)
        act(2, 1)
        act(4, 0)
        for i in range(len(later)):
            rest.begin(i)
        act(1, 2)
        act(0, 3)
        act(3, 1)
        for copy in spread:
            copy.wait_recv()
        wide = tab_s[...].astype(F32).reshape(-1, 2 * ROWS, half)
        tab = jnp.concatenate([wide[:, 0:ROWS], wide[:, ROWS:]], axis=-1).reshape(tab_o.shape)
        tab_o[...] = tab
        qtab[...] = (tab * inv_rms(tab) * gains[0:1]).astype(BF)
        tail_s[...] = jnp.zeros_like(tail_s)
        carry_s[...] = jnp.zeros_like(carry_s)

        def convolve(lo, hi):
            def one(block, _):
                conv_block(block, ids_s, qtab, taps, conv_s, padq, tail_s)
                return _

            lax.fori_loop(lo, hi, one, 0)

        for copy in own:
            copy.wait()
        convolve(0, 2)
        act(2, 2)
        act(4, 1)
        convolve(2, 4)
        for i in later_groups[0]:
            rest.act(i, 0)
        act(1, 3)
        act(3, 2)
        convolve(4, 6)
        act(4, 2)
        act(2, 3)
        convolve(6, 8)
        for i in later_groups[1]:
            rest.act(i, 0)
        onward[1].start()
        total = jnp.zeros(count_o.shape, F32)
        for n in range(8 * depth):
            total = total + count_s[n // (4 * depth), n // (2 * depth) % 2, n // 2 % depth, n % 2]
        count_o[...] = total
        act(3, 3)
        act(4, 3)
        onward[0].start()

    for when, acts in GATHER_SCHEDULE.items():

        @pl.when(step == when)
        def _(acts=acts):
            for group, phase in acts:
                for i in later_groups[group]:
                    rest.act(i, phase)

    here = ids_s[step]
    for n in range(3):
        ids_o[0, n : n + 1, :] = jnp.concatenate([here[2 * n : 2 * n + 1, :], here[2 * n + 1 : 2 * n + 2, :]], axis=1)
    ids_o[0, 3:, :] = jnp.zeros((ROWS - 3, ids_o.shape[2]), jnp.int32)
    front_block(conv_s.at[step], bias, FlatRows(in_s), keep_o, p_o, q_o, state_o, carry_s, big)

    @pl.when(step == blocks - 1)
    def _():
        for group, phase in GATHER_LAST:
            for i in later_groups[group]:
                rest.act(i, phase)
        for copy in onward:
            copy.wait()
        for copy in spread:
            copy.wait_send()
        first.finish()
        rest.finish()


class FlatRows:
    def __init__(self, ref):
        self.ref = ref

    def __getitem__(self, index):
        cols = index[1]
        part = self.ref[:, :, :, :, :, cols]
        return part.reshape(-1, part.shape[-1])


def run_front(depth, ids, table, mats, gains, taps, bias):
    blocks, _, half = ids.shape
    rows = 2 * half
    w_in, w_out, w_up, w_down = mats
    width = table.shape[1]
    hidden = bias.shape[1]
    kernel = taps.shape[0]
    total = blocks * rows
    rim = (kernel - 1) * ROWS
    owners = (2, 2, depth, 2)
    devices = 8 * depth
    vocab = devices * table.shape[0]
    cols = w_in.shape[1]
    now = [(0, 0, width // 2, True), (1, 0, LANES, False)]
    for n in range(8):
        now.append((2, n * cols // 8, (n + 1) * cols // 8, n % 2 == 0))
    later = halves([a.shape for a in (w_out, w_up, w_down)], (1, 2, 2))
    wide = pl.BlockSpec((rows, hidden), lambda i: (i, 0))
    any_spec = pl.BlockSpec(memory_space=pl.ANY)
    dma = lambda *shape: pltpu.SemaphoreType.DMA(shape)
    args = (ids, table, w_in, w_out, w_up, w_down, gains, taps, bias)
    struct = jax.ShapeDtypeStruct
    return pl.pallas_call(
        functools.partial(front_kernel, depth, now, later),
        grid=(blocks,),
        in_specs=[whole(a.shape) for a in args],
        out_specs=[wide] * 4
        + [pl.BlockSpec((1, ROWS, rows), lambda i: (i, 0, 0)), whole((vocab, width)), whole((ROWS, LANES))]
        + [any_spec] * 5,
        out_shape=[struct((total, hidden), F32)] * 3
        + [struct((total, hidden), BF), struct((blocks, ROWS, rows), jnp.int32), struct((vocab, width), F32)]
        + [struct((ROWS, LANES), F32), struct((blocks, rows, width), BF)]
        + [struct(owners + a.shape, BF) for a in mats],
        scratch_shapes=[
            pltpu.VMEM(ids.shape, jnp.int32),
            pltpu.VMEM(owners + (2 * ROWS, width // 2), BF),
            pltpu.VMEM(owners + (ROWS, LANES), F32),
            pltpu.VMEM(owners + w_in.shape, BF),
            pltpu.VMEM(w_out.shape, BF),
            pltpu.VMEM(w_up.shape, BF),
            pltpu.VMEM(w_down.shape, BF),
            pltpu.VMEM((vocab, width), BF),
            pltpu.VMEM((blocks, rows, width), BF),
            pltpu.VMEM((rim + rows, width), F32),
            pltpu.VMEM((rim, width), F32),
            pltpu.VMEM((ROWS, hidden), F32),
            pltpu.VMEM((rows, hidden), F32),
            dma(2 * depth),
            dma(2 * depth),
            dma(len(now), depth + 2),
            dma(len(now), depth + 2),
            dma(len(later), depth + 2),
            dma(len(later), depth + 2),
            dma(3),
            dma(2),
        ],
        compiler_params=pltpu.CompilerParams(
            dimension_semantics=("arbitrary",), collective_id=0, has_side_effects=True, vmem_limit_bytes=60 * MIB
        ),
        name="gather_and_front",
    )(*args)


def tail_kernel(
    ids, state_low, tab, count, gains, w_out, w_up, w_down,
    mixed_o, normed_o, final_o, lifted_o, g_down, g_tab, small_o,
    tab_low, slope_s, active,
):
    step = pl.program_id(0)
    rows = state_low.shape[0]
    vocab, width = tab.shape
    ff = w_up.shape[1]
    chunk = 256

    @pl.when(step == 0)
    def _():
        tab_low[...] = tab[...].astype(BF)
        g_down[...] = jnp.zeros_like(g_down)
        g_tab[...] = jnp.zeros_like(g_tab)
        small_o[...] = jnp.zeros_like(small_o)

    columns = jnp.concatenate([ids[n].T for n in range(ids.shape[0])], axis=0)
    hot = one_hot(columns[:, 0:1], vocab)
    mixed = nn(hot, tab_low[...]) + nn(state_low[...], w_out[...])
    mixed_o[...] = mixed
    inverse_b = inv_rms(mixed)
    normed_o[...] = (mixed * inverse_b * gains[1:2]).astype(BF)
    for j in range(ff // chunk):
        cols = slice(j * chunk, (j + 1) * chunk)
        lifted = nn(normed_o[...], w_up[:, cols])
        square = lifted * lifted
        curve = jnp.tanh(lifted * (GELU_A + (GELU_A * GELU_B) * square))
        cdf = 0.5 + 0.5 * curve
        active[:, cols] = (lifted * cdf).astype(BF)
        slope_s[:, cols] = cdf + (0.5 * lifted) * (1.0 - curve * curve) * (
            GELU_A + (3.0 * GELU_A * GELU_B) * square
        )
    result = mixed_o[...] + nn(active[...], w_down[...])
    inverse_f = inv_rms(result)
    unit_f = result * inverse_f
    normed_f = (unit_f * gains[2:3]).astype(BF)

    logits = nt(normed_f, tab_low[...])
    top = jnp.max(logits, axis=-1, keepdims=True)
    powers = jnp.exp(logits - top)
    total = jnp.sum(powers, axis=-1, keepdims=True)
    lse = jnp.log(total) + top
    target = columns[:, 1:2] == lax.broadcasted_iota(jnp.int32, (rows, vocab), 1)
    picked = jnp.sum(jnp.where(target, logits, 0.0), axis=-1, keepdims=True)
    weight = columns[:, 2:3].astype(F32)
    loss = column_sum(weight * (lse - picked))
    share = weight * (1.0 / count[0:1, 0:1])
    d_logits = ((powers * (1.0 / total) - jnp.where(target, 1.0, 0.0)) * share).astype(BF)
    g_tab[...] += tn(d_logits, normed_f)
    d_normed_f = nn(d_logits, tab_low[...])
    small_o[2:3, :] += column_sum(d_normed_f * unit_f)
    small_o[3:4, :] += jnp.broadcast_to(loss, (1, width))
    d_final = norm_back(result, inverse_f, gains[2:3], d_normed_f)
    final_o[...] = d_final
    grad_low = d_final.astype(BF)
    for j in range(ff // chunk):
        cols = slice(j * chunk, (j + 1) * chunk)
        d_active = nt(grad_low, w_down[cols, :])
        g_down[cols, :] += tn(active[:, cols], grad_low)
        lifted_o[:, cols] = (d_active * slope_s[:, cols]).astype(BF)


def run_tail(join, ids, state_low, tab, count, gains, w_out, w_up, w_down):
    blocks, _, rows = ids.shape
    rows, blocks = rows * join, blocks // join
    vocab, width = tab.shape
    hidden = w_out.shape[0]
    ff = w_up.shape[1]
    total = blocks * rows
    block = lambda cols: pl.BlockSpec((rows, cols), lambda i: (i, 0))
    sums = ((ff, width), (vocab, width), (ROWS, width))
    struct = jax.ShapeDtypeStruct
    return pl.pallas_call(
        tail_kernel,
        grid=(blocks,),
        in_specs=[pl.BlockSpec((join, ROWS, rows // join), lambda i: (i, 0, 0)), block(hidden)]
        + [whole(a.shape) for a in (tab, count, gains, w_out, w_up, w_down)],
        out_specs=[block(width), block(width), block(width), block(ff)] + [whole(s) for s in sums],
        out_shape=[struct((total, width), F32), struct((total, width), BF), struct((total, width), F32), struct((total, ff), BF)]
        + [struct(s, F32) for s in sums],
        scratch_shapes=[
            pltpu.VMEM((vocab, width), BF),
            pltpu.VMEM((rows, ff), F32),
            pltpu.VMEM((rows, ff), BF),
        ],
        compiler_params=pltpu.CompilerParams(
            dimension_semantics=("arbitrary",), vmem_limit_bytes=62 * MIB
        ),
        name="tail_and_head",
    )(ids, state_low, tab, count, gains, w_out, w_up, w_down)


MID_SCHEDULE = {
    3: [(0, 0, 0), (0, 1, 0)], 8: [(0, 0, 1)], 9: [(0, 1, 1), (1, 0, 0), (1, 1, 0), (0, 0, 2)],
    10: [(0, 1, 2)], 11: [(1, 0, 1)], 12: [(1, 1, 1)], 13: [(1, 0, 2), (1, 1, 2)],
}
MID_LAST = [(0, 0, 3), (0, 1, 3), (1, 0, 3), (1, 1, 3)]


def mid_kernel(depth, plans, counts, *refs):
    ids, mixed, normed, final, lifted, keep, p, q, conv, gains, w_out, w_up, small_in, g_down = refs[:14]
    d_pre, mixed_o, g_in, g_emb, small_o, r_down, r_up = refs[14:21]
    g_up, ds, cand, carry_s = refs[21:25]
    step = pl.program_id(0)
    blocks = pl.num_programs(0) // 2
    spot = place()
    sums, at = [], 25
    for n, (source, out) in enumerate(((g_down, r_down), (g_up, r_up))):
        sums.append(Reduce(plans[n], depth, source, n > 0, out, refs[at : at + counts[n]], spot))
        at += counts[n]
    vocab, width = g_emb.shape
    rows, hidden = keep.shape
    steps = rows // ROWS
    chunk = 256

    def run(acts):
        for n, pair, phase in acts:
            sums[n].pair(pair, phase)

    @pl.when(step == 0)
    def _():
        greet(*spot, depth)
        sums[0].begin()
        g_up[...] = jnp.zeros_like(g_up)
        g_in[...] = jnp.zeros_like(g_in)
        g_emb[...] = jnp.zeros_like(g_emb)
        small_o[...] = small_in[...]
        carry_s[...] = jnp.zeros_like(carry_s)

    for when, acts in MID_SCHEDULE.items():

        @pl.when(step == when)
        def _(acts=acts):
            run(acts)

    @pl.when(step < blocks)
    def _():
        g_up[...] += tn(normed[...], lifted[...]).reshape(g_up.shape)

    @pl.when(step == blocks - 1)
    def _():
        sums[1].begin()

    @pl.when(step >= blocks)
    def _():
        d_normed = nt(lifted[...], w_up[...])
        value = mixed[...]
        inverse = inv_rms(value)
        small_o[1:2, :] += column_sum(d_normed * (value * inverse))
        d_mixed = final[...] + norm_back(value, inverse, gains[1:2], d_normed)
        mixed_low = d_mixed.astype(BF)
        rest = (d_mixed - mixed_low.astype(F32)).astype(BF)
        ds[...] = nt(mixed_low, w_out[...])
        hot_t = one_hot_t(ids[0][0:1, :], vocab)
        g_emb[...] += nn(hot_t, mixed_low) + nn(hot_t, rest)
        mixed_o[...] = mixed_low

        low_half = lax.broadcasted_iota(jnp.int32, (ROWS, chunk), 0) < ROWS // 2
        for j in range(hidden // chunk):
            cols = slice(j * chunk, (j + 1) * chunk)
            carry = carry_s[:, cols]
            first = carry
            for tau in reversed(range(steps)):
                at = slice(tau * ROWS, (tau + 1) * ROWS)
                first = keep[at, cols] * (ds[at, cols] + first)
            reached = jnp.where(low_half, swap_halves(first), carry)
            total = jnp.zeros((ROWS, chunk), F32)
            for tau in reversed(range(steps)):
                at = slice(tau * ROWS, (tau + 1) * ROWS)
                lam = ds[at, cols] + reached
                reached = keep[at, cols] * lam
                d_gate = lam * p[at, cols]
                ds[at, cols] = d_gate
                cand[at, :] = lam * q[at, cols]
                total = total + d_gate
            d_pre[:, j * chunk : (j + 1) * chunk] = ds[:, cols].astype(BF)
            d_pre[:, hidden + j * chunk : hidden + (j + 1) * chunk] = cand[...].astype(BF)
            carry_s[:, cols] = jnp.where(low_half, 0.0, swap_halves(reached))
            at = j * chunk
            row = 4 + at // width
            small_o[row : row + 1, at % width : at % width + chunk] += column_sum(total)
            for start in (at, hidden + at):
                g_in[:, start : start + chunk] += tn(conv[...], d_pre[:, start : start + chunk])

    @pl.when(step == 2 * blocks - 1)
    def _():
        run(MID_LAST)
        for one in sums:
            one.finish()


def run_mid(depth, ids, mixed, normed, final, lifted, keep, p, q, conv, gains, w_out, w_up, small, g_down, vocab):
    blocks, _, rows = ids.shape
    width, ff = w_up.shape
    hidden = w_out.shape[0]
    total = blocks * rows
    last = blocks - 1
    owners = (2, 2, depth, 2)
    back = lambda cols: pl.BlockSpec((rows, cols), lambda i: (jnp.minimum(2 * blocks - 1 - i, last), 0))
    once = pl.BlockSpec((rows, width), lambda i: (jnp.minimum(i, last), 0))
    both = pl.BlockSpec((rows, ff), lambda i: (jnp.minimum(i, 2 * blocks - 1 - i), 0))
    up_shape = owners + (width // (8 * depth), ff)
    shapes = (g_down.shape, up_shape)
    plans = [halves([shape], (2,)) for shape in shapes]
    moving = [Reduce.scratch(shape, plan, depth, n > 0) for n, (shape, plan) in enumerate(zip(shapes, plans))]
    sums = ((width, 2 * hidden), (vocab, width), small.shape, g_down.shape[-2:], up_shape[-2:])
    return pl.pallas_call(
        functools.partial(mid_kernel, depth, plans, [len(m) for m in moving]),
        grid=(2 * blocks,),
        in_specs=[
            pl.BlockSpec((1, ROWS, rows), lambda i: (jnp.minimum(2 * blocks - 1 - i, last), 0, 0)),
            back(width), once, back(width), both, back(hidden), back(hidden), back(hidden), back(width),
        ]
        + [whole(a.shape) for a in (gains, w_out, w_up, small)]
        + [pl.BlockSpec(memory_space=pl.ANY)],
        out_specs=[back(2 * hidden), back(width)] + [whole(s) for s in sums],
        out_shape=[jax.ShapeDtypeStruct((total, 2 * hidden), BF), jax.ShapeDtypeStruct((total, width), BF)] + [jax.ShapeDtypeStruct(s, F32) for s in sums],
        scratch_shapes=[
            pltpu.VMEM(up_shape, F32),
            pltpu.VMEM((rows, hidden), F32),
            pltpu.VMEM((rows, 256), F32),
            pltpu.VMEM((ROWS, hidden), F32),
        ]
        + [piece for group in moving for piece in group],
        compiler_params=pltpu.CompilerParams(
            dimension_semantics=("arbitrary",), collective_id=2, has_side_effects=True, vmem_limit_bytes=63 * MIB
        ),
        name="mid_back_and_reduce",
    )(ids, mixed, normed, final, lifted, keep, p, q, conv, gains, w_out, w_up, small, g_down)


def adam_kernel(shapes, small, squares, count, *refs):
    mats = refs[:5]
    weights, firsts, seconds = refs[5:13], refs[13:21], refs[21:29]
    loss_o, count_o, norm_o = refs[29:32]
    new_w, new_m, new_v = refs[32:40], refs[40:48], refs[48:56]
    kernel, bias_rows = shapes
    grads = [m[...] for m in mats]
    grads.append(small[0:3, :])
    grads.append(small[ROWS : ROWS + kernel, :])
    grads.append(jnp.concatenate([small[4 + r : 5 + r, :] for r in range(bias_rows)], axis=1))
    square = squares[0:1, 0:1]
    for grad in grads[5:]:
        square = square + jnp.sum(jnp.sum(grad * grad, axis=1, keepdims=True), axis=0, keepdims=True)
    norm = jnp.sqrt(square)
    scale = jnp.minimum(1.0, CLIP / (norm + 1e-06))
    norm_o[...] = norm
    loss_o[...] = small[3:4, 0:1]
    count_o[...] = count[0:1, 0:1]
    for i in range(8):
        rate = RATE_MATRIX if i < 5 else RATE_VECTOR
        decay = WEIGHT_DECAY if i < 5 else 0.0
        w, m, v = adam(weights[i][...], grads[i] * scale, firsts[i][...], seconds[i][...], rate, decay)
        new_w[i][...] = w
        new_m[i][...] = m
        new_v[i][...] = v


def run_adam(shapes, mats, small, squares, count, weights, firsts, seconds):
    one = jax.ShapeDtypeStruct((1, 1), F32)
    like = [jax.ShapeDtypeStruct(w.shape, F32) for w in weights]
    args = (small, squares, count) + tuple(mats) + tuple(weights) + tuple(firsts) + tuple(seconds)
    return pl.pallas_call(
        functools.partial(adam_kernel, shapes),
        grid=(1,),
        in_specs=[whole(a.shape) for a in args],
        out_specs=[whole(a.shape) for a in [one] * 3 + like * 3],
        out_shape=[one] * 3 + like * 3,
        compiler_params=pltpu.CompilerParams(vmem_limit_bytes=60 * MIB),
        name="adam_update",
    )(*args)


def spread_ids(tokens, targets, counted, depth):
    seqs, span = tokens.shape
    ways = 2 * depth
    three = jnp.stack([tokens, targets, counted]).reshape(3, ways, seqs // ways, 2, span // 2)
    rows = three.transpose(1, 0, 4, 3, 2).reshape(ways, 6, -1)
    return jnp.pad(rows, ((0, 0), (0, ROWS - 6), (0, 0)))


def body_moved(depth, *args):
    tokens, targets, counted = args[:3]
    weights, firsts, seconds = args[3:11], args[11:19], args[19:27]
    table, w_in, w_out, w_up, w_down, gains, conv_taps, gate_bias = weights
    width = table.shape[1]
    taps = conv_taps[0]
    ids = spread_ids(tokens, targets, counted, depth)
    keep, p, q, state_low, ids, tab, count, conv, *full = run_front(
        depth, ids, table, (w_in[0], w_out[0], w_up[0], w_down[0]), gains, taps, gate_bias
    )
    conv = conv.reshape(-1, width)
    full = [a.reshape(-1, a.shape[-1]) for a in full]
    mixed, normed, final, lifted, g_down, g_head, small = run_tail(1, ids, state_low, tab, count, gains, *full[1:])
    owned = lambda g: g.reshape((2, 2, depth, 2, -1, g.shape[-1]))
    d_pre, mixed_low, g_in, g_emb, small, r_down, r_up = run_mid(
        depth, ids, mixed, normed, final, lifted, keep, p, q, conv, gains, full[1], full[2], small, owned(g_down),
        tab.shape[0],
    )
    r_in, r_out, r_tab, small, squares = run_last(
        depth, ids, d_pre, state_low, mixed_low, tab, gains, taps, full[0], (g_head, g_emb), small, (r_down, r_up), owned(g_in)
    )
    mats = [r_tab, r_in, r_out, r_up, r_down]
    flat = lambda group: [group[0]] + [a[0] for a in group[1:5]] + [group[5], group[6][0], group[7]]
    out = run_adam(
        (conv_taps.shape[1], gate_bias.shape[1] // width),
        mats, small, squares, count, flat(weights), flat(firsts), flat(seconds),
    )
    shaped = [o.reshape(()) for o in out[:3]]
    for i, o in enumerate(out[3:]):
        shaped.append(o.reshape(weights[i % 8].shape))
    return tuple(shaped)


def choose(mesh, *args):
    ways = mesh.shape["seq"]
    seqs, span = args[0].shape
    if mesh.shape["dp"] == 4 and ways == 8 and seqs == 4 * ways and span == LANES:
        return body_moved(ways // 2, *args)
    return body(*args)


def solution(mesh):
    return jax.shard_map(
        functools.partial(choose, mesh),
        mesh=mesh,
        in_specs=(
            P("dp", "seq"),
            P("dp", "seq"),
            P("dp", "seq"),
            P(("dp", "seq"), None),
            P(None, ("dp", "seq"), None),
            P(None, ("dp", "seq"), None),
            P(None, ("dp", "seq"), None),
            P(None, ("dp", "seq"), None),
            P(),
            P(),
            P(),
            P(("dp", "seq"), None),
            P(None, ("dp", "seq"), None),
            P(None, ("dp", "seq"), None),
            P(None, ("dp", "seq"), None),
            P(None, ("dp", "seq"), None),
            P(),
            P(),
            P(),
            P(("dp", "seq"), None),
            P(None, ("dp", "seq"), None),
            P(None, ("dp", "seq"), None),
            P(None, ("dp", "seq"), None),
            P(None, ("dp", "seq"), None),
            P(),
            P(),
            P(),
        ),
        out_specs=(
            P(),
            P(),
            P(),
            P(("dp", "seq"), None),
            P(None, ("dp", "seq"), None),
            P(None, ("dp", "seq"), None),
            P(None, ("dp", "seq"), None),
            P(None, ("dp", "seq"), None),
            P(),
            P(),
            P(),
            P(("dp", "seq"), None),
            P(None, ("dp", "seq"), None),
            P(None, ("dp", "seq"), None),
            P(None, ("dp", "seq"), None),
            P(None, ("dp", "seq"), None),
            P(),
            P(),
            P(),
            P(("dp", "seq"), None),
            P(None, ("dp", "seq"), None),
            P(None, ("dp", "seq"), None),
            P(None, ("dp", "seq"), None),
            P(None, ("dp", "seq"), None),
            P(),
            P(),
            P(),
        ),
        check_vma=False,
    )
```

```python
import functools

import jax
import jax.numpy as jnp
from jax import lax
from jax.experimental import pallas as pl
from jax.experimental.pallas import tpu as pltpu
from jax.sharding import PartitionSpec as P

V = 256
MICRO = 2
STEP = 3


EPS = 1e-06
CLIP = 0.01
BETA_ONE = 0.5
BETA_TWO = 0.5
ADAM_EPS = 1e-08
RATE_MATRIX = 0.03
RATE_VECTOR = 0.3
WEIGHT_DECAY = 0.1


def from_behind(x, axis, by):
    devices = lax.axis_size(axis)
    pairs = [(i, i + by) for i in range(devices) if 0 <= i + by < devices]
    return lax.ppermute(x, axis, pairs)


def carried_in(part, axis, combine, identity, reverse):
    count = lax.axis_size(axis)
    place = lax.axis_index(axis)
    ahead = count - 1 - place if reverse else place
    gathered = jax.tree.map(lambda a: lax.all_gather(a, axis), part)
    state = jax.tree.map(lambda a, e: jnp.zeros_like(a) + jnp.asarray(e, a.dtype), part, identity)

    def one(lap, state):
        source = count - 1 - lap if reverse else lap
        return combine(
            state, jax.tree.map(lambda a: lax.dynamic_index_in_dim(a, source, 0, False), gathered)
        )

    return lax.fori_loop(0, ahead, one, state)


def matmul(left, right):
    return jnp.dot(left, right, preferred_element_type=jnp.float32)


def matmul_tn(left, right):
    return lax.dot_general(
        left, right, (((0,), (0,)), ((), ())), preferred_element_type=jnp.float32
    )


def matmul_nt(left, right):
    return lax.dot_general(
        left, right, (((1,), (1,)), ((), ())), preferred_element_type=jnp.float32
    )


def rms_norm(values, gain):
    return values * lax.rsqrt(jnp.mean(values * values, axis=-1, keepdims=True) + EPS) * gain


def combine(earlier, later):
    return (earlier[0] * later[0], later[0] * earlier[1] + later[1])


def gates(gate, cand):
    return (jax.nn.sigmoid(-gate), jax.nn.sigmoid(gate) * jax.nn.softplus(cand))


def conv_apply(padded, taps, length):
    total = taps[0] * padded[0:length].astype(jnp.float32)
    for k in range(1, taps.shape[0]):
        total = total + taps[k] * padded[k : k + length].astype(jnp.float32)
    return total


def adam(weight, grad, first, second, rate, decay):
    first = BETA_ONE * first + (1.0 - BETA_ONE) * grad
    second = BETA_TWO * second + (1.0 - BETA_TWO) * grad * grad
    fix_one = 1.0 - BETA_ONE**STEP
    fix_two = 1.0 - BETA_TWO**STEP
    update = first / fix_one / (jnp.sqrt(second / fix_two) + ADAM_EPS)
    return (weight - rate * (update + decay * weight), first, second)


def mixer_front(queue, rim, taps, bias, w_in):
    span, seqs, width = queue.shape
    padded = jnp.concatenate([rim, queue], axis=0)
    conv_low = conv_apply(padded, taps, span).astype(jnp.bfloat16)
    pre = matmul(conv_low.reshape(span * seqs, width), w_in).reshape(span, seqs, -1)
    hidden = bias.shape[0]
    keep, write = gates(pre[..., :hidden] + bias, pre[..., hidden:])
    return (padded, conv_low, pre, keep, write)


def block_tail(state, resid, gain_b, w_out, w_up, w_down):
    span, seqs, width = resid.shape
    state_low = state.astype(jnp.bfloat16).reshape(span * seqs, -1)
    mixed = resid + matmul(state_low, w_out).reshape(span, seqs, width)
    normed_low = rms_norm(mixed, gain_b).astype(jnp.bfloat16).reshape(span * seqs, width)
    lifted = matmul(normed_low, w_up)
    active_low = jax.nn.gelu(lifted).astype(jnp.bfloat16)
    result = mixed + matmul(active_low, w_down).reshape(span, seqs, width)
    return (result, (state_low, mixed, normed_low, lifted, active_low))


def layer_forward(resid, taps, gain_a, gain_b, bias, mats):
    span = resid.shape[0]
    kernel = taps.shape[0]
    queue = rms_norm(resid, gain_a).astype(jnp.bfloat16)
    rim = from_behind(queue[span - kernel + 1 :], "seq", 1)
    padded, conv_low, pre, keep, write = mixer_front(queue, rim, taps, bias, mats[0])
    decay, local = lax.associative_scan(combine, (keep, write), axis=0)
    ones = jnp.ones_like(local[0])
    carry_in = carried_in(
        (decay[-1], local[-1]), "seq", combine, (ones, jnp.zeros_like(ones)), False
    )[1]
    state = local + decay * carry_in[None]
    result, unused = block_tail(state, resid, gain_b, mats[1], mats[2], mats[3])
    return (result, rim, carry_in)


def layer_backward(grad, resid, rim, carry_in, taps, gain_a, gain_b, bias, mats):
    w_in, w_out, w_up, w_down = mats
    span, seqs, width = resid.shape
    kernel = taps.shape[0]
    hidden = bias.shape[0]
    normed_a, norm_back = jax.vjp(rms_norm, resid, gain_a)
    queue = normed_a.astype(jnp.bfloat16)
    padded, conv_low, pre, keep, write = mixer_front(queue, rim, taps, bias, w_in)
    decay, local = lax.associative_scan(combine, (keep, write), axis=0)
    state = local + decay * carry_in[None]
    result, (state_low, mixed, normed_low, lifted, active_low) = block_tail(
        state, resid, gain_b, w_out, w_up, w_down
    )
    grad_low = grad.astype(jnp.bfloat16).reshape(span * seqs, width)
    g_down = matmul_tn(active_low, grad_low)
    d_active = matmul_nt(grad_low, w_down)
    d_lifted_low = jax.vjp(jax.nn.gelu, lifted)[1](d_active)[0].astype(jnp.bfloat16)
    g_up = matmul_tn(normed_low, d_lifted_low)
    d_normed = matmul_nt(d_lifted_low, w_up).reshape(span, seqs, width)
    d_mixed, d_gain_b = jax.vjp(rms_norm, mixed, gain_b)[1](d_normed)
    d_mixed = grad + d_mixed
    mixed_low = d_mixed.astype(jnp.bfloat16).reshape(span * seqs, width)
    g_out = matmul_tn(state_low, mixed_low)
    d_state = matmul_nt(mixed_low, w_out).reshape(span, seqs, hidden)
    follow = jnp.concatenate([keep[1:], jnp.ones_like(keep[:1])], axis=0)
    reach, back_local = lax.associative_scan(combine, (follow, d_state), axis=0, reverse=True)
    ones = jnp.ones_like(keep[0])
    summary = (keep[0] * reach[0], keep[0] * back_local[0])
    carry_out = carried_in(summary, "seq", combine, (ones, jnp.zeros_like(ones)), True)[1]
    adjoint = back_local + reach * carry_out[None]
    before = jnp.concatenate([carry_in[None], state[:-1]], axis=0)
    d_gate, d_cand = jax.vjp(gates, pre[..., :hidden] + bias, pre[..., hidden:])[1](
        (adjoint * before, adjoint)
    )
    d_bias = jnp.sum(d_gate, axis=(0, 1))
    d_pre = (
        jnp.concatenate([d_gate, d_cand], axis=-1)
        .astype(jnp.bfloat16)
        .reshape(span * seqs, 2 * hidden)
    )
    g_in = matmul_tn(conv_low.reshape(span * seqs, width), d_pre)
    d_conv = matmul_nt(d_pre, w_in).reshape(span, seqs, width)
    beyond = from_behind(d_conv[: kernel - 1].astype(jnp.bfloat16), "seq", -1).astype(jnp.float32)
    extended = jnp.concatenate([d_conv, beyond], axis=0)
    d_queue = taps[0] * extended[kernel - 1 : kernel - 1 + span]
    tap_grads = [jnp.sum(d_conv * padded[0:span].astype(jnp.float32), axis=(0, 1))]
    for k in range(1, kernel):
        d_queue = d_queue + taps[k] * extended[kernel - 1 - k : kernel - 1 - k + span]
        tap_grads.append(jnp.sum(d_conv * padded[k : k + span].astype(jnp.float32), axis=(0, 1)))
    rounded = lax.optimization_barrier(d_queue.astype(jnp.bfloat16)).astype(jnp.float32)
    d_resid, d_gain_a = norm_back(rounded)
    return (
        d_mixed + d_resid,
        (g_in, g_out, g_up, g_down),
        (jnp.stack(tap_grads), d_gain_a, d_gain_b, d_bias),
    )


def body(
    tokens,
    targets,
    counted,
    table,
    w_in,
    w_out,
    w_up,
    w_down,
    gains,
    conv_taps,
    gate_bias,
    m_table,
    m_in,
    m_out,
    m_up,
    m_down,
    m_gains,
    m_taps,
    m_bias,
    v_table,
    v_in,
    v_out,
    v_up,
    v_down,
    v_gains,
    v_taps,
    v_bias,
):
    layers = w_in.shape[0]
    seq_dev, span = tokens.shape
    rows = seq_dev // MICRO
    width = table.shape[1]
    vocab = V
    mask = counted.astype(jnp.float32)
    count = lax.psum(jnp.sum(mask), ("dp", "seq"))
    shards = (
        w_in.astype(jnp.bfloat16),
        w_out.astype(jnp.bfloat16),
        w_up.astype(jnp.bfloat16),
        w_down.astype(jnp.bfloat16),
    )
    layer_gains = gains[: 2 * layers].reshape(layers, 2, width)
    columns = jnp.arange(vocab, dtype=jnp.int32)

    def forward_step(resid, inputs):
        pieces, taps, pair, bias = inputs
        mats = (
            lax.all_gather(pieces[0], ("dp", "seq"), axis=0, tiled=True),
            lax.all_gather(pieces[1], ("dp", "seq"), axis=0, tiled=True),
            lax.all_gather(pieces[2], ("dp", "seq"), axis=0, tiled=True),
            lax.all_gather(pieces[3], ("dp", "seq"), axis=0, tiled=True),
        )
        result, rim, carry_in = layer_forward(resid, taps, pair[0], pair[1], bias, mats)
        return (result, (resid, rim, carry_in))

    def backward_step(grad, inputs):
        saved, pieces, taps, pair, bias = inputs
        mats = (
            lax.all_gather(pieces[0], ("dp", "seq"), axis=0, tiled=True),
            lax.all_gather(pieces[1], ("dp", "seq"), axis=0, tiled=True),
            lax.all_gather(pieces[2], ("dp", "seq"), axis=0, tiled=True),
            lax.all_gather(pieces[3], ("dp", "seq"), axis=0, tiled=True),
        )
        grad, full, small = layer_backward(
            grad, saved[0], saved[1], saved[2], taps, pair[0], pair[1], bias, mats
        )
        full = (
            lax.psum_scatter(full[0], ("dp", "seq"), scatter_dimension=0, tiled=True),
            lax.psum_scatter(full[1], ("dp", "seq"), scatter_dimension=0, tiled=True),
            lax.psum_scatter(full[2], ("dp", "seq"), scatter_dimension=0, tiled=True),
            lax.psum_scatter(full[3], ("dp", "seq"), scatter_dimension=0, tiled=True),
        )
        return (grad, (full, small))

    loss = jnp.zeros((), jnp.float32)
    g_table = jnp.zeros((vocab, width), jnp.float32)
    acc_full = None
    acc_small = None
    for index in range(MICRO):
        tok = tokens[index * rows : (index + 1) * rows].T.reshape(-1)
        tgt = targets[index * rows : (index + 1) * rows].T.reshape(-1)
        weights = mask[index * rows : (index + 1) * rows].T.reshape(-1)
        tab = lax.all_gather(table.astype(jnp.bfloat16), ("dp", "seq"), axis=0, tiled=True)
        picks = tok[:, None] == columns[None, :]
        resid = matmul(picks.astype(jnp.bfloat16), tab).reshape(span, rows, width)
        final, saved = lax.scan(forward_step, resid, (shards, conv_taps, layer_gains, gate_bias))
        normed_f, final_back = jax.vjp(rms_norm, final, gains[2 * layers])
        normed_low = normed_f.astype(jnp.bfloat16).reshape(span * rows, width)
        logits = matmul_nt(normed_low, tab)
        top = jnp.max(logits, axis=-1, keepdims=True)
        lse = jnp.log(jnp.sum(jnp.exp(logits - top), axis=-1)) + top[:, 0]
        hits = (tgt[:, None] == columns[None, :]).astype(jnp.float32)
        picked = jnp.sum(hits * logits, axis=-1)
        loss = loss + jnp.sum(weights * (lse - picked))
        d_logits = ((jnp.exp(logits - lse[:, None]) - hits) * (weights / count)[:, None]).astype(
            jnp.bfloat16
        )
        g_table = g_table + matmul_tn(d_logits, normed_low)
        d_normed = matmul(d_logits, tab).reshape(span, rows, width)
        d_final, d_gain_f = final_back(d_normed)
        grad0, (full, small) = lax.scan(
            backward_step, d_final, (saved, shards, conv_taps, layer_gains, gate_bias), reverse=True
        )
        g_table = g_table + lax.dot_general(
            picks.astype(jnp.float32),
            grad0.reshape(span * rows, width),
            (((0,), (0,)), ((), ())),
            precision=lax.Precision.HIGHEST,
        )
        layer_gain_grads = jnp.stack([small[1], small[2]], axis=1).reshape(2 * layers, width)
        vectors = (jnp.concatenate([layer_gain_grads, d_gain_f[None]], axis=0), small[0], small[3])
        if index == 0:
            acc_full, acc_small = (full, vectors)
        else:
            acc_full = jax.tree.map(lambda a, b: a + b, acc_full, full)
            acc_small = jax.tree.map(lambda a, b: a + b, acc_small, vectors)
    table_shard = lax.psum_scatter(g_table, ("dp", "seq"), scatter_dimension=0, tiled=True)
    g_gains, g_taps, g_bias = lax.psum((acc_small[0], acc_small[1], acc_small[2]), ("dp", "seq"))
    matrices = (table_shard, acc_full[0], acc_full[1], acc_full[2], acc_full[3])
    squares = jnp.zeros((), jnp.float32)
    for grad in matrices:
        squares = squares + jnp.sum(grad * grad)
    squares_all, loss_all = lax.psum((squares, loss), ("dp", "seq"))
    small_squares = jnp.sum(g_gains * g_gains) + jnp.sum(g_taps * g_taps) + jnp.sum(g_bias * g_bias)
    norm = jnp.sqrt(squares_all + small_squares)
    scale = jnp.minimum(1.0, CLIP / (norm + 1e-06))
    params = (table, w_in, w_out, w_up, w_down, gains, conv_taps, gate_bias)
    grads = matrices + (g_gains, g_taps, g_bias)
    firsts = (m_table, m_in, m_out, m_up, m_down, m_gains, m_taps, m_bias)
    seconds = (v_table, v_in, v_out, v_up, v_down, v_gains, v_taps, v_bias)
    news, next_m, next_v = ([], [], [])
    for index in range(8):
        rate = RATE_MATRIX if index < 5 else RATE_VECTOR
        decay = WEIGHT_DECAY if index < 5 else 0.0
        weight, first, second = adam(
            params[index], grads[index] * scale, firsts[index], seconds[index], rate, decay
        )
        news.append(weight)
        next_m.append(first)
        next_v.append(second)
    return (
        loss_all,
        count,
        norm,
        news[0],
        news[1],
        news[2],
        news[3],
        news[4],
        news[5],
        news[6],
        news[7],
        next_m[0],
        next_m[1],
        next_m[2],
        next_m[3],
        next_m[4],
        next_m[5],
        next_m[6],
        next_m[7],
        next_v[0],
        next_v[1],
        next_v[2],
        next_v[3],
        next_v[4],
        next_v[5],
        next_v[6],
        next_v[7],
    )


BF = jnp.bfloat16
F32 = jnp.float32
MIB = 1 << 20
LANES = 128
ROWS = 8
GELU_A = 0.7978845608028654
GELU_B = 0.044715
LOG2E = 1.4426950408889634


def nn(left, right):
    return jnp.dot(left, right, preferred_element_type=F32)


def tn(left, right):
    return lax.dot_general(left, right, (((0,), (0,)), ((), ())), preferred_element_type=F32)


def nt(left, right):
    return lax.dot_general(left, right, (((1,), (1,)), ((), ())), preferred_element_type=F32)


def inv_rms(values):
    return lax.rsqrt(jnp.mean(values * values, axis=-1, keepdims=True) + EPS)


def norm_back(values, inverse, gain, grad):
    width = values.shape[-1]
    scaled = grad * gain
    dot = jnp.sum(scaled * values, axis=-1, keepdims=True)
    return inverse * scaled - values * (inverse * inverse * inverse * dot * (1.0 / width))


def column_sum(values):
    return jnp.sum(values, axis=0, keepdims=True)


def swap_halves(tile):
    return pltpu.roll(tile, ROWS // 2, tile.ndim - 2)


def spread_steps(tile, row, start, cols):
    parts = []
    for tau in range(LANES // 2):
        piece = tile[row : row + ROWS, start + tau : start + tau + 1]
        parts.append(jnp.broadcast_to(piece, (ROWS, cols)))
    return jnp.concatenate(parts, axis=0)


def hits(tile, start, vocab):
    lane = lax.broadcasted_iota(jnp.int32, (ROWS, vocab), 1)
    parts = []
    for tau in range(LANES // 2):
        piece = tile[0:ROWS, start + tau : start + tau + 1]
        parts.append((piece == lane).astype(F32))
    return jnp.concatenate(parts, axis=0)


def one_hot(tile, vocab):
    return hits(tile, 0, vocab).astype(BF)


def whole(shape):
    zeros = (0,) * len(shape)
    return pl.BlockSpec(shape, lambda i: zeros, pipeline_mode=pl.Buffered(1))


def place():
    dp = lax.axis_index("dp")
    seq = lax.axis_index("seq")
    return dp // 2, dp % 2, seq // 2, seq % 2


def device(y, x, z, core):
    return (y * 2 + x, z * 2 + core)


def greet(y, x, z, core, depth):
    barrier = pltpu.get_barrier_semaphore()
    peers = [device(1 - y, x, z, core), device(y, 1 - x, z, core), device(1 - y, 1 - x, z, core)]
    for dz in range(depth):
        for dc in range(2):
            if dz or dc:
                peers.append(device(y, x, (z + dz) % depth, (core + dc) % 2))
    for peer in peers:
        pl.semaphore_signal(barrier, inc=1, device_id=peer, device_id_type=pl.DeviceIdType.MESH)
    pl.semaphore_wait(barrier, len(peers))


def remote(src, dst, send, recv, peer):
    return pltpu.make_async_remote_copy(
        src_ref=src,
        dst_ref=dst,
        send_sem=send,
        recv_sem=recv,
        device_id=peer,
        device_id_type=pl.DeviceIdType.MESH,
    )


def in_order(groups, phases, act):
    for time in range(len(groups) + phases - 1):
        for phase in range(phases - 1, -1, -1):
            at = time - phase
            if 0 <= at < len(groups):
                for item in groups[at]:
                    act(item, phase)


def grouped(plan):
    return [[i, i + 1] for i in range(0, len(plan), 2)]


class Gather:
    def __init__(self, plan, depth, sources, outs, send, recv, at):
        self.plan, self.depth, self.sources, self.outs, self.send, self.recv = plan, depth, sources, outs, send, recv
        self.y, self.x, self.z, self.core = at

    def copies(self, i, phase):
        t, lo, hi, along_x = self.plan[i]
        cols = pl.ds(lo, hi - lo)
        y, x, z, core = self.y, self.x, self.z, self.core
        out = self.outs[t]
        by_x, by_y = device(y, 1 - x, z, core), device(1 - y, x, z, core)
        if phase == 0:
            mine = out.at[y, x, z, core, :, cols]
            source = mine if self.sources[t] is None else self.sources[t].at[:, cols]
            moves = [(source, mine, device(y, x, (z + dz) % self.depth, core)) for dz in range(1, self.depth)]
        elif phase == 1:
            part = out.at[y, x, :, core, :, cols]
            moves = [(part, part, by_x if along_x else by_y)]
        elif phase == 2:
            part = out.at[y, :, :, core, :, cols] if along_x else out.at[:, x, :, core, :, cols]
            moves = [(part, part, by_y if along_x else by_x)]
        else:
            part = out.at[:, :, :, core, :, cols]
            moves = [(part, part, device(y, x, z, 1 - core))]
        base = 0 if phase == 0 else self.depth - 2 + phase
        return [
            remote(src, dst, self.send.at[i, base + n], self.recv.at[i, base + n], peer)
            for n, (src, dst, peer) in enumerate(moves)
        ]

    def begin(self, i):
        for copy in self.copies(i, 0):
            copy.start()

    def act(self, i, phase):
        for copy in self.copies(i, phase):
            copy.wait_recv()
        if phase < 3:
            for copy in self.copies(i, phase + 1):
                copy.start()

    def finish(self):
        for i in range(len(self.plan)):
            for phase in range(4):
                for copy in self.copies(i, phase):
                    copy.wait_send()


def add_into(target, other):
    lead = [()]
    for d in target.shape[: len(target.shape) - 2]:
        lead = [index + (n,) for index in lead for n in range(d)]
    for index in lead:
        target[index] = target[index] + other[index]


def halves(shapes, cuts=None):
    plan = []
    for t, shape in enumerate(shapes):
        pieces = 2 * (cuts[t] if cuts else 1)
        wide = shape[-1] // pieces
        for n in range(pieces):
            plan.append((t, n * wide, (n + 1) * wide, n % 2 == 0))
    return plan


class Reduce:
    def __init__(self, plan, depth, source, resident, out, refs, at):
        self.plan, self.depth, self.source, self.resident, self.out = plan, depth, source, resident, out
        self.send, self.recv = refs[:2]
        if not resident:
            self.loads, self.own = refs[2:4]
        first = 2 if resident else 4
        self.bufs = [refs[first + 3 * i : first + 3 * i + 3] for i in range(len(plan))]
        self.y, self.x, self.z, self.core = at

    def scratch(shape, plan, depth, resident):
        piece = (shape[-2], plan[0][2] - plan[0][1])
        dma = lambda *n: pltpu.SemaphoreType.DMA(n)
        own = [] if resident else [dma(len(plan)), pltpu.VMEM((len(plan), 2, 2, depth) + piece, F32)]
        each = [
            pltpu.VMEM((2, 2, depth) + piece, F32), pltpu.VMEM((2, depth) + piece, F32), pltpu.VMEM((2, depth) + piece, F32)
        ]
        return [dma(len(plan), depth + 2), dma(len(plan), depth + 2)] + own + each * len(plan)

    def load(self, i):
        t, lo, hi, _ = self.plan[i]
        source = self.source.at[:, :, :, self.core, :, pl.ds(lo, hi - lo)]
        return pltpu.make_async_copy(source, self.own.at[i], self.loads.at[i])

    def copies(self, i, phase):
        t, lo, hi, along_x = self.plan[i]
        y, x, z, core = self.y, self.x, self.z, self.core
        whole, half, quarter = self.bufs[i]
        by_x, by_y = device(y, 1 - x, z, core), device(1 - y, x, z, core)
        if phase == 0:
            source = self.source.at[:, :, :, 1 - core, :, pl.ds(lo, hi - lo)]
            moves = [(source, whole, device(y, x, z, 1 - core))]
        elif phase == 1:
            moves = [(whole.at[1 - y], half, by_y) if along_x else (whole.at[:, 1 - x], half, by_x)]
        elif phase == 2:
            moves = [(half.at[1 - x], quarter.at[0], by_x) if along_x else (half.at[1 - y], quarter.at[0], by_y)]
        else:
            moves = []
            for dz in range(1, self.depth):
                pz = (z + dz) % self.depth
                moves.append((quarter.at[0, pz], quarter.at[1, dz], device(y, x, pz, core)))
        return [
            remote(src, dst, self.send.at[i, phase + n], self.recv.at[i, phase + n], peer)
            for n, (src, dst, peer) in enumerate(moves)
        ]

    def begin(self):
        for i in range(len(self.plan)):
            for copy in self.copies(i, 0):
                copy.start()
            if not self.resident:
                self.load(i).start()

    def pair(self, n, phase):
        for i in (2 * n, 2 * n + 1):
            self.act(i, phase)

    def act(self, i, phase):
        t, lo, hi, along_x = self.plan[i]
        y, x, z, core = self.y, self.x, self.z, self.core
        whole, half, quarter = self.bufs[i]
        for copy in self.copies(i, phase):
            copy.wait_recv()
        if phase == 0:
            if self.resident:
                add_into(whole, self.source.at[:, :, :, core, :, pl.ds(lo, hi - lo)])
            else:
                self.load(i).wait()
                add_into(whole, self.own.at[i])
        elif phase == 1:
            add_into(half, whole.at[y] if along_x else whole.at[:, x])
        elif phase == 2:
            add_into(quarter.at[0], half.at[x] if along_x else half.at[y])
        else:
            total = quarter[0, z]
            for dz in range(1, self.depth):
                total = total + quarter[1, dz]
            self.out[:, lo:hi] = total
            return
        for copy in self.copies(i, phase + 1):
            copy.start()

    def finish(self):
        for i in range(len(self.plan)):
            for phase in range(4):
                for copy in self.copies(i, phase):
                    copy.wait_send()


class Everywhere:
    def __init__(self, slots, sends, recvs, depth, at):
        y, x, z, core = at
        self.slots, self.ways = slots, 2 * depth
        self.me, self.other = z * 2 + core, self.ways + y * 2 + x
        self.near, self.far = [], []
        mine = slots.at[self.me]
        for dz in range(depth):
            for dc in range(2):
                if dz or dc:
                    n = dz * 2 + dc
                    peer = device(y, x, (z + dz) % depth, (core + dc) % 2)
                    self.near.append(remote(mine, mine, sends.at[n], recvs.at[n], peer))
        mine = slots.at[self.other]
        for n, (dy, dx) in enumerate(((0, 1), (1, 0), (1, 1))):
            n += self.ways
            peer = device((y + dy) % 2, (x + dx) % 2, z, core)
            self.far.append(remote(mine, mine, sends.at[n], recvs.at[n], peer))

    def total(self, lo, hi):
        value = self.slots[lo]
        for n in range(lo + 1, hi):
            value = value + self.slots[n]
        return value

    def begin(self, value):
        self.slots[self.me] = value
        for copy in self.near:
            copy.start()

    def middle(self):
        for copy in self.near:
            copy.wait()
        self.slots[self.other] = self.total(0, self.ways)
        for copy in self.far:
            copy.start()

    def end(self):
        for copy in self.far:
            copy.wait()
        return self.total(self.ways, self.ways + 4)


class EverywhereHalved:
    def __init__(self, whole, parts, sends, recvs, depth, at):
        y, x, z, core = at
        self.whole, self.parts, self.depth, self.core = whole, parts, depth, core
        other = device(y, x, z, 1 - core)
        self.first = remote(whole.at[0], whole.at[1], sends.at[0], recvs.at[0], other)
        self.spot = (z, depth + y * 2 + x)
        self.along, self.plane = [], []
        mine = parts.at[z]
        for dz in range(1, depth):
            peer = device(y, x, (z + dz) % depth, core)
            self.along.append(remote(mine, mine, sends.at[dz], recvs.at[dz], peer))
        mine = parts.at[self.spot[1]]
        for n, (dy, dx) in enumerate(((0, 1), (1, 0), (1, 1))):
            peer = device((y + dy) % 2, (x + dx) % 2, z, core)
            self.plane.append(remote(mine, mine, sends.at[depth + n], recvs.at[depth + n], peer))
        mine = whole.at[2, core]
        self.last = remote(mine, mine, sends.at[depth + 3], recvs.at[depth + 3], other)

    def total(self, lo, hi):
        value = self.parts[lo]
        for n in range(lo + 1, hi):
            value = value + self.parts[n]
        return value

    def step(self, n, value=None):
        if n == 0:
            self.whole[0] = value.reshape(self.whole.shape[1:])
            self.first.start()
        elif n == 1:
            self.first.wait()
            lower = self.whole[self.core, self.core] + self.whole[1 - self.core, self.core]
            self.parts[self.spot[0]] = lower
            for copy in self.along:
                copy.start()
        elif n == 2:
            for copy in self.along:
                copy.wait()
            self.parts[self.spot[1]] = self.total(0, self.depth)
            for copy in self.plane:
                copy.start()
        elif n == 3:
            for copy in self.plane:
                copy.wait()
            self.whole[2, self.core] = self.total(self.depth, self.depth + 4)
            self.last.start()
        else:
            self.last.wait()
            return self.whole[2].reshape(-1, self.whole.shape[-1])


SCHEDULE = {
    0: [(0, 0, 0)], 1: [(0, 1, 0)], 5: [(0, 0, 1), (0, 2, 0)], 8: [(0, 1, 1), (0, 3, 0)], 9: [(0, 0, 2), (0, 2, 1)],
    10: [(0, 1, 2), (1, 0, 0)], 11: [(0, 3, 1), (0, 2, 2), (1, 1, 0)], 13: [(0, 3, 2), (1, 0, 1)], 14: [(1, 1, 1)], 15: [(1, 0, 2)],
}
LEFT_OVER = [
    (2, 0, 0), (3, 0, 1), (1, 1, 2), (2, 0, 1), (3, 0, 2), (2, 0, 2), (0, 0, 3), (0, 1, 3), (0, 2, 3), (3, 0, 3), (0, 3, 3),
    (1, 0, 3), (1, 1, 3), (2, 0, 3),
]


def last_kernel(depth, plans, counts, *refs):
    ids, d_pre, state_low, mixed_low, tab, gains, taps, w_in, g_tab_a, g_tab_b, small_in, r_down, r_up, g_in = refs[:14]
    r_in, r_out, r_tab, small_o, squares_o = refs[14:19]
    small, g_out, g_tab, qtab, ext, head_s, hot_sum = refs[19:26]
    whole_s, part_s, sq_slots, sends, recvs, sq_sends, sq_recvs = refs[26:33]
    spot = place()
    sums, at = [], 33
    for n, (source, out) in enumerate(((g_in, r_in), (g_out, r_out), (g_tab, r_tab))):
        sums.append(Reduce(plans[n], depth, source, n > 0, out, refs[at : at + counts[n]], spot))
        at += counts[n]
    smalls = EverywhereHalved(whole_s, part_s, sends, recvs, depth, spot)
    squares = Everywhere(sq_slots, sq_sends, sq_recvs, depth, spot)
    step = pl.program_id(0)
    blocks = pl.num_programs(0) // 2
    rows = d_pre.shape[0]
    vocab, width = tab.shape
    kernel = taps.shape[0]
    rim = (kernel - 1) * ROWS

    def run(acts):
        for n, pair, phase in acts:
            if n == 3:
                smalls.step(phase)
            else:
                sums[n].pair(pair, phase)

    @pl.when(step == 0)
    def _():
        greet(*spot, depth)
        sums[0].begin()
        wide = tab[...].astype(BF).astype(F32)
        qtab[...] = (wide * inv_rms(wide) * gains[0:1]).astype(BF)
        g_out[...] = jnp.zeros_like(g_out)
        hot_sum[...] = jnp.zeros_like(hot_sum)
        small[...] = jnp.zeros_like(small)
        small[0:ROWS, :] = small_in[...]
        head_s[...] = jnp.zeros_like(head_s)

    for when, acts in SCHEDULE.items():

        @pl.when(step == when)
        def _(acts=acts):
            run(acts)

    @pl.when(step < blocks)
    def _():
        g_out[...] += tn(state_low[...], mixed_low[...]).reshape(g_out.shape)

    @pl.when(step == blocks - 1)
    def _():
        sums[1].begin()

    @pl.when(step >= blocks)
    def _():
        ext[0:rows, :] = nt(d_pre[...], w_in[...])
        half = lax.broadcasted_iota(jnp.int32, (rim, width), 0) % ROWS < ROWS // 2
        mine = ext[0:rim, :]
        ext[rows:, :] = jnp.where(
            half,
            swap_halves(mine.reshape(kernel - 1, ROWS, width)).reshape(rim, width),
            swap_halves(head_s[...].reshape(kernel - 1, ROWS, width)).reshape(rim, width),
        )
        head_s[...] = mine
        here = ids[0]
        hot = one_hot(here, vocab)
        known = nn(hot, qtab[...])
        d_queue = None
        for k in range(kernel):
            shift = (kernel - 1 - k) * ROWS
            part = ext[shift : shift + rows, :]
            term = taps[k : k + 1] * part
            d_queue = term if d_queue is None else d_queue + term
            small[ROWS + k : ROWS + k + 1, :] += column_sum(part * known)
        hot_sum[...] += tn(hot, d_queue.astype(BF))

    @pl.when(step == 2 * blocks - 1)
    def _():
        wide = tab[...].astype(BF).astype(F32)
        inverse = inv_rms(wide)
        total = hot_sum[...]
        g_tab[...] = (
            g_tab_a[...] + g_tab_b[...] + norm_back(wide, inverse, gains[0:1], total)
        ).reshape(g_tab.shape)
        sums[2].begin()
        small[0:1, :] = column_sum(total * (wide * inverse))
        smalls.step(0, small[...])
        run(LEFT_OVER)
        square = jnp.zeros((1, 1), F32)
        for out in (r_in, r_out, r_tab, r_down, r_up):
            value = out[...]
            square = square + jnp.sum(jnp.sum(value * value, axis=1, keepdims=True), axis=0, keepdims=True)
        squares.begin(jnp.broadcast_to(square, (ROWS, LANES)))
        small_o[...] = smalls.step(4)
        squares.middle()
        squares_o[...] = squares.end()
        for one in sums:
            one.finish()


def run_last(depth, ids, d_pre, state_low, mixed_low, tab, gains, taps, w_in, g_tabs, small, done, g_in):
    blocks = ids.shape[0]
    rows = d_pre.shape[0] // blocks
    vocab, width = tab.shape
    kernel = taps.shape[0]
    rim = (kernel - 1) * ROWS
    last = blocks - 1
    owners = (2, 2, depth, 2)
    hidden = state_low.shape[1]
    shapes = (g_in.shape, owners + (hidden // (8 * depth), width), owners + (vocab // (8 * depth), width))
    plans = [halves([shape], (cuts,)) for shape, cuts in zip(shapes, (4, 2, 1))]
    back = lambda i: jnp.minimum(2 * blocks - 1 - i, last)
    once = lambda cols: pl.BlockSpec((rows, cols), lambda i: (jnp.minimum(i, last), 0))
    moving = [Reduce.scratch(shape, plan, depth, n > 0) for n, (shape, plan) in enumerate(zip(shapes, plans))]
    out = [s[-2:] for s in shapes] + [(2 * ROWS, width), (ROWS, LANES)]
    dma = lambda *shape: pltpu.SemaphoreType.DMA(shape)
    fixed = (tab, gains, taps, w_in) + tuple(g_tabs) + (small,) + tuple(done)
    return pl.pallas_call(
        functools.partial(last_kernel, depth, plans, [len(m) for m in moving]),
        grid=(2 * blocks,),
        in_specs=[
            pl.BlockSpec((1,) + ids.shape[1:], lambda i: (back(i), 0, 0)),
            pl.BlockSpec((rows, d_pre.shape[1]), lambda i: (back(i), 0)),
            once(hidden),
            once(width),
        ]
        + [whole(a.shape) for a in fixed]
        + [pl.BlockSpec(memory_space=pl.ANY)],
        out_specs=[whole(s) for s in out],
        out_shape=[jax.ShapeDtypeStruct(s, F32) for s in out],
        scratch_shapes=[
            pltpu.VMEM((2 * ROWS, width), F32),
            pltpu.VMEM(shapes[1], F32),
            pltpu.VMEM(shapes[2], F32),
            pltpu.VMEM((vocab, width), BF),
            pltpu.VMEM((rim + rows, width), F32),
            pltpu.VMEM((rim, width), F32),
            pltpu.VMEM((vocab, width), F32),
            pltpu.VMEM((3, 2, ROWS, width), F32),
            pltpu.VMEM((depth + 4, ROWS, width), F32),
            pltpu.VMEM((2 * depth + 4, ROWS, LANES), F32),
            dma(depth + 4),
            dma(depth + 4),
            dma(2 * depth + 4),
            dma(2 * depth + 4),
        ]
        + [piece for group in moving for piece in group],
        compiler_params=pltpu.CompilerParams(
            dimension_semantics=("arbitrary",), collective_id=1, has_side_effects=True, vmem_limit_bytes=62 * MIB
        ),
        name="last_back_and_reduce",
    )(ids, d_pre, state_low, mixed_low, *fixed, g_in)


def conv_block(block, ids_s, qtab, taps, conv_s, padq, tail_s):
    _, rows, width = conv_s.shape
    vocab = qtab.shape[0]
    kernel = taps.shape[0]
    rim = (kernel - 1) * ROWS
    queue = nn(one_hot(ids_s[block], vocab), qtab[...])
    padq[rim:, :] = queue
    half = lax.broadcasted_iota(jnp.int32, (rim, width), 0) % ROWS < ROWS // 2
    before = tail_s[...].reshape(kernel - 1, ROWS, width)
    latest = padq[rows:, :].reshape(kernel - 1, ROWS, width)
    padq[0:rim, :] = jnp.where(
        half, swap_halves(before).reshape(rim, width), swap_halves(latest).reshape(rim, width)
    )
    tail_s[...] = padq[rows:, :]
    conv = taps[0:1] * padq[0:rows, :]
    for k in range(1, kernel):
        conv = conv + taps[k : k + 1] * padq[k * ROWS : k * ROWS + rows, :]
    conv_s[block] = conv.astype(BF)


def front_block(conv, bias, w_in, keep_o, p_o, q_o, state_o, carry_s, big):
    rows, hidden = keep_o.shape
    steps = rows // ROWS
    chunk = 256
    low_half = lax.broadcasted_iota(jnp.int32, (ROWS, chunk), 0) < ROWS // 2
    for j in range(hidden // chunk):
        cols = slice(j * chunk, (j + 1) * chunk)
        gate = nn(conv[...], w_in[:, j * chunk : (j + 1) * chunk]) + bias[0:1, cols]
        cand = nn(conv[...], w_in[:, hidden + j * chunk : hidden + (j + 1) * chunk])
        grown = jnp.exp2(jnp.minimum(gate * -LOG2E, 120.0))
        write_gate = pl.reciprocal(1.0 + grown)
        keep_o[:, cols] = grown * write_gate
        small = jnp.exp2(jnp.abs(cand) * -LOG2E)
        one_more = 1.0 + small
        soft = jnp.maximum(cand, 0.0) + (jnp.log(one_more) + (small - (one_more - 1.0)))
        p_o[:, cols] = write_gate
        q_o[:, cols] = write_gate * jnp.exp2((cand - soft) * LOG2E)
        big[:, cols] = write_gate * soft

        carry = carry_s[:, cols]
        end = carry
        for tau in range(steps):
            at = slice(tau * ROWS, (tau + 1) * ROWS)
            end = keep_o[at, cols] * end + big[at, cols]
        state = jnp.where(low_half, carry, swap_halves(end))
        for tau in range(steps):
            at = slice(tau * ROWS, (tau + 1) * ROWS)
            change = big[at, cols] - p_o[at, cols] * state
            p_o[at, cols] = keep_o[at, cols] * change
            state = state + change
            big[at, cols] = state
        state_o[:, cols] = big[:, cols].astype(BF)
        carry_s[:, cols] = jnp.where(low_half, swap_halves(state), 0.0)


GATHER_SCHEDULE = {1: [(0, 1), (3, 0)], 2: [(1, 1), (4, 0)], 3: [(2, 1), (0, 2)], 4: [(3, 1), (1, 2)], 5: [(4, 1), (2, 2)], 6: [(3, 2)], 7: [(4, 2)]}
GATHER_LAST = [(0, 3), (1, 3), (2, 3), (3, 3), (4, 3)]


def front_kernel(
    depth, now, later,
    tokens, targets, counted, table, w_in, w_out, w_up, w_down, gains, taps, bias,
    keep_o, p_o, q_o, state_o, ids_o, tab_o, count_o, conv_o, w_in_o, w_out_o, w_up_o, w_down_o,
    ids, ids_s, tab_s, count_s, in_s, out_s, up_s, down_s, qtab, conv_s, padq, tail_s, carry_s, big,
    ids_send, ids_recv, now_send, now_recv, later_send, later_recv, own_sem, in_sem,
):
    step = pl.program_id(0)
    blocks = pl.num_programs(0)
    spot = place()
    y, x, z, core = spot
    me = z * 2 + core
    onward = [
        pltpu.make_async_copy(in_s, w_in_o, in_sem.at[0]),
        pltpu.make_async_copy(conv_s, conv_o, in_sem.at[1]),
    ]
    first = Gather(now, depth, [None] * 3, [tab_s, count_s, in_s], now_send, now_recv, spot)
    rest = Gather(later, depth, [out_s, up_s, down_s], [w_out_o, w_up_o, w_down_o], later_send, later_recv, spot)
    later_groups = grouped(later)
    own = [
        pltpu.make_async_copy(src, dst.at[y, x, z, core], own_sem.at[n])
        for n, (src, dst) in enumerate(((out_s, w_out_o), (up_s, w_up_o), (down_s, w_down_o)))
    ]
    spread = []
    for dz in range(depth):
        for dc in range(2):
            if dz or dc:
                pz, pc = (z + dz) % depth, (core + dc) % 2
                n = dz * 2 + dc
                spread.append(
                    remote(ids.at[pz * 2 + pc], ids_s.at[me], ids_send.at[n], ids_recv.at[n], device(y, x, pz, pc))
                )

    @pl.when(step == 0)
    def _():
        half = table.shape[1] // 2
        tab_s[y, x, z, core] = jnp.concatenate([table[:, 0:half], table[:, half:]], axis=0).astype(BF)
        share = counted[...].astype(F32)
        share = jnp.sum(jnp.sum(share, axis=1, keepdims=True), axis=0, keepdims=True)
        count_s[y, x, z, core] = jnp.broadcast_to(share, count_o.shape)
        in_s[y, x, z, core] = w_in[...].astype(BF)
        seqs, span = tokens.shape
        seqs //= 2 * depth
        for n in range(2 * depth):
            parts = []
            for array in (tokens, targets, counted):
                mine = array[n * seqs : (n + 1) * seqs, :]
                parts.append(jnp.concatenate([mine[:, 0 : span // 2], mine[:, span // 2 :]], axis=0))
            top = jnp.concatenate([parts[0], parts[1]], axis=1)
            ids[n] = jnp.concatenate([top, jnp.concatenate([parts[2], parts[2]], axis=1)], axis=0)
        ids_s[me] = ids[me]
        greet(*spot, depth)
        pairs = [(i, i + 1) for i in range(0, len(now), 2)]

        def act(pair, phase):
            for i in pairs[pair]:
                first.act(i, phase)

        def begin(pair):
            for i in pairs[pair]:
                first.begin(i)

        begin(0)
        for copy in spread:
            copy.start()
        begin(1)
        begin(2)
        act(0, 0)
        out_s[...] = w_out[...].astype(BF)
        up_s[...] = w_up[...].astype(BF)
        down_s[...] = w_down[...].astype(BF)
        for copy in own:
            copy.start()
        act(1, 0)
        begin(3)
        act(0, 1)
        act(2, 0)
        begin(4)
        for i in (0, 1, 2, 3):
            rest.begin(i)
        act(1, 1)
        act(0, 2)
        act(3, 0)
        act(2, 1)
        act(4, 0)
        for i in range(4, len(later)):
            rest.begin(i)
        act(1, 2)
        act(0, 3)
        act(3, 1)
        for copy in spread:
            copy.wait_recv()
        wide = tab_s[...].astype(F32).reshape(-1, 2 * ROWS, half)
        tab = jnp.concatenate([wide[:, 0:ROWS], wide[:, ROWS:]], axis=-1).reshape(tab_o.shape)
        tab_o[...] = tab
        qtab[...] = (tab * inv_rms(tab) * gains[0:1]).astype(BF)
        tail_s[...] = jnp.zeros_like(tail_s)
        carry_s[...] = jnp.zeros_like(carry_s)

        def convolve(lo, hi):
            def one(block, _):
                conv_block(block, ids_s, qtab, taps, conv_s, padq, tail_s)
                return _

            lax.fori_loop(lo, hi, one, 0)

        for copy in own:
            copy.wait()
        convolve(0, 2)
        act(2, 2)
        act(4, 1)
        convolve(2, 4)
        for i in later_groups[0]:
            rest.act(i, 0)
        act(1, 3)
        act(3, 2)
        convolve(4, 6)
        act(4, 2)
        act(2, 3)
        convolve(6, 8)
        for i in later_groups[1]:
            rest.act(i, 0)
        onward[1].start()
        total = jnp.zeros(count_o.shape, F32)
        for n in range(8 * depth):
            total = total + count_s[n // (4 * depth), n // (2 * depth) % 2, n // 2 % depth, n % 2]
        count_o[...] = total
        act(3, 3)
        act(4, 3)
        onward[0].start()
        for i in later_groups[2]:
            rest.act(i, 0)

    for when, acts in GATHER_SCHEDULE.items():

        @pl.when(step == when)
        def _(acts=acts):
            for group, phase in acts:
                for i in later_groups[group]:
                    rest.act(i, phase)

    ids_o[0] = ids_s[step]
    front_block(conv_s.at[step], bias, FlatRows(in_s), keep_o, p_o, q_o, state_o, carry_s, big)

    @pl.when(step == blocks - 1)
    def _():
        for group, phase in GATHER_LAST:
            for i in later_groups[group]:
                rest.act(i, phase)
        for copy in onward:
            copy.wait()
        for copy in spread:
            copy.wait_send()
        first.finish()
        rest.finish()


class FlatRows:
    def __init__(self, ref):
        self.ref = ref

    def __getitem__(self, index):
        cols = index[1]
        part = self.ref[:, :, :, :, :, cols]
        return part.reshape(-1, part.shape[-1])


def run_front(depth, ids, table, mats, gains, taps, bias):
    blocks = 2 * depth
    seqs, span = ids[0].shape
    rows = seqs * span // blocks
    tile = (blocks, 2 * ROWS, LANES)
    w_in, w_out, w_up, w_down = mats
    width = table.shape[1]
    hidden = bias.shape[1]
    kernel = taps.shape[0]
    total = blocks * rows
    rim = (kernel - 1) * ROWS
    owners = (2, 2, depth, 2)
    devices = 8 * depth
    vocab = devices * table.shape[0]
    cols = w_in.shape[1]
    now = [(0, 0, width // 2, True), (1, 0, LANES, False)]
    for n in range(8):
        now.append((2, n * cols // 8, (n + 1) * cols // 8, n % 2 == 0))
    later = halves([a.shape for a in (w_out, w_up, w_down)], (1, 2, 2))
    wide = pl.BlockSpec((rows, hidden), lambda i: (i, 0))
    any_spec = pl.BlockSpec(memory_space=pl.ANY)
    dma = lambda *shape: pltpu.SemaphoreType.DMA(shape)
    args = tuple(ids) + (table, w_in, w_out, w_up, w_down, gains, taps, bias)
    struct = jax.ShapeDtypeStruct
    return pl.pallas_call(
        functools.partial(front_kernel, depth, now, later),
        grid=(blocks,),
        in_specs=[whole(a.shape) for a in args],
        out_specs=[wide] * 4
        + [pl.BlockSpec((1,) + tile[1:], lambda i: (i, 0, 0)), whole((vocab, width)), whole((ROWS, LANES))]
        + [any_spec] * 5,
        out_shape=[struct((total, hidden), F32)] * 3
        + [struct((total, hidden), BF), struct(tile, jnp.int32), struct((vocab, width), F32)]
        + [struct((ROWS, LANES), F32), struct((blocks, rows, width), BF)]
        + [struct(owners + a.shape, BF) for a in mats],
        scratch_shapes=[
            pltpu.VMEM(tile, jnp.int32),
            pltpu.VMEM(tile, jnp.int32),
            pltpu.VMEM(owners + (2 * ROWS, width // 2), BF),
            pltpu.VMEM(owners + (ROWS, LANES), F32),
            pltpu.VMEM(owners + w_in.shape, BF),
            pltpu.VMEM(w_out.shape, BF),
            pltpu.VMEM(w_up.shape, BF),
            pltpu.VMEM(w_down.shape, BF),
            pltpu.VMEM((vocab, width), BF),
            pltpu.VMEM((blocks, rows, width), BF),
            pltpu.VMEM((rim + rows, width), F32),
            pltpu.VMEM((rim, width), F32),
            pltpu.VMEM((ROWS, hidden), F32),
            pltpu.VMEM((rows, hidden), F32),
            dma(2 * depth),
            dma(2 * depth),
            dma(len(now), depth + 2),
            dma(len(now), depth + 2),
            dma(len(later), depth + 2),
            dma(len(later), depth + 2),
            dma(3),
            dma(2),
        ],
        compiler_params=pltpu.CompilerParams(
            dimension_semantics=("arbitrary",), collective_id=0, has_side_effects=True, vmem_limit_bytes=60 * MIB
        ),
        name="gather_and_front",
    )(*args)


def tail_kernel(
    ids, state_low, tab, count, gains, w_out, w_up, w_down,
    mixed_o, normed_o, final_o, lifted_o, g_down, g_tab, small_o,
    tab_low, slope_s, active,
):
    step = pl.program_id(0)
    rows = state_low.shape[0]
    vocab, width = tab.shape
    ff = w_up.shape[1]
    chunk = 256

    @pl.when(step == 0)
    def _():
        tab_low[...] = tab[...].astype(BF)
        g_down[...] = jnp.zeros_like(g_down)
        g_tab[...] = jnp.zeros_like(g_tab)
        small_o[...] = jnp.zeros_like(small_o)

    here = ids[0]
    hot = one_hot(here, vocab)
    mixed = nn(hot, tab_low[...]) + nn(state_low[...], w_out[...])
    mixed_o[...] = mixed
    inverse_b = inv_rms(mixed)
    normed_o[...] = (mixed * inverse_b * gains[1:2]).astype(BF)
    for j in range(ff // chunk):
        cols = slice(j * chunk, (j + 1) * chunk)
        lifted = nn(normed_o[...], w_up[:, cols])
        square = lifted * lifted
        curve = jnp.tanh(lifted * (GELU_A + (GELU_A * GELU_B) * square))
        cdf = 0.5 + 0.5 * curve
        active[:, cols] = (lifted * cdf).astype(BF)
        slope_s[:, cols] = cdf + (0.5 * lifted) * (1.0 - curve * curve) * (
            GELU_A + (3.0 * GELU_A * GELU_B) * square
        )
    result = mixed_o[...] + nn(active[...], w_down[...])
    inverse_f = inv_rms(result)
    unit_f = result * inverse_f
    normed_f = (unit_f * gains[2:3]).astype(BF)

    logits = nt(normed_f, tab_low[...])
    top = jnp.max(logits, axis=-1, keepdims=True)
    powers = jnp.exp(logits - top)
    total = jnp.sum(powers, axis=-1, keepdims=True)
    lse = jnp.log(total) + top
    target = hits(here, LANES // 2, vocab)
    picked = jnp.sum(target * logits, axis=-1, keepdims=True)
    weight = spread_steps(here, ROWS, 0, vocab).astype(F32)
    loss = column_sum(weight[:, 0:1] * (lse - picked))
    share = weight * (1.0 / count[0:1, 0:1])
    d_logits = ((powers * (1.0 / total) - target) * share).astype(BF)
    g_tab[...] += tn(d_logits, normed_f)
    d_normed_f = nn(d_logits, tab_low[...])
    small_o[2:3, :] += column_sum(d_normed_f * unit_f)
    small_o[3:4, :] += jnp.broadcast_to(loss, (1, width))
    d_final = norm_back(result, inverse_f, gains[2:3], d_normed_f)
    final_o[...] = d_final
    grad_low = d_final.astype(BF)
    for j in range(ff // chunk):
        cols = slice(j * chunk, (j + 1) * chunk)
        d_active = nt(grad_low, w_down[cols, :])
        g_down[cols, :] += tn(active[:, cols], grad_low)
        lifted_o[:, cols] = (d_active * slope_s[:, cols]).astype(BF)


def run_tail(ids, state_low, tab, count, gains, w_out, w_up, w_down):
    blocks = ids.shape[0]
    rows = state_low.shape[0] // blocks
    vocab, width = tab.shape
    hidden = w_out.shape[0]
    ff = w_up.shape[1]
    total = blocks * rows
    block = lambda cols: pl.BlockSpec((rows, cols), lambda i: (i, 0))
    sums = ((ff, width), (vocab, width), (ROWS, width))
    struct = jax.ShapeDtypeStruct
    return pl.pallas_call(
        tail_kernel,
        grid=(blocks,),
        in_specs=[pl.BlockSpec((1,) + ids.shape[1:], lambda i: (i, 0, 0)), block(hidden)]
        + [whole(a.shape) for a in (tab, count, gains, w_out, w_up, w_down)],
        out_specs=[block(width), block(width), block(width), block(ff)] + [whole(s) for s in sums],
        out_shape=[struct((total, width), F32), struct((total, width), BF), struct((total, width), F32), struct((total, ff), BF)]
        + [struct(s, F32) for s in sums],
        scratch_shapes=[
            pltpu.VMEM((vocab, width), BF),
            pltpu.VMEM((rows, ff), F32),
            pltpu.VMEM((rows, ff), BF),
        ],
        compiler_params=pltpu.CompilerParams(
            dimension_semantics=("arbitrary",), vmem_limit_bytes=62 * MIB
        ),
        name="tail_and_head",
    )(ids, state_low, tab, count, gains, w_out, w_up, w_down)


MID_SCHEDULE = {
    2: [(0, 0, 0)], 3: [(0, 1, 0)], 8: [(0, 0, 1)], 9: [(0, 1, 1), (1, 0, 0)], 10: [(1, 1, 0), (0, 0, 2), (0, 1, 2)],
    11: [(1, 0, 1)], 12: [(1, 1, 1)], 13: [(1, 0, 2)], 14: [(1, 1, 2), (0, 0, 3), (0, 1, 3)],
}
MID_LAST = [(1, 0, 3), (1, 1, 3)]


def mid_kernel(depth, plans, counts, *refs):
    ids, mixed, normed, final, lifted, keep, p, q, conv, gains, w_out, w_up, small_in, g_down = refs[:14]
    d_pre, mixed_o, g_in, g_emb, small_o, r_down, r_up = refs[14:21]
    g_up, ds, cand, carry_s = refs[21:25]
    step = pl.program_id(0)
    blocks = pl.num_programs(0) // 2
    spot = place()
    sums, at = [], 25
    for n, (source, out) in enumerate(((g_down, r_down), (g_up, r_up))):
        sums.append(Reduce(plans[n], depth, source, n > 0, out, refs[at : at + counts[n]], spot))
        at += counts[n]
    vocab, width = g_emb.shape
    rows, hidden = keep.shape
    steps = rows // ROWS
    chunk = 256

    def run(acts):
        for n, pair, phase in acts:
            sums[n].pair(pair, phase)

    @pl.when(step == 0)
    def _():
        greet(*spot, depth)
        sums[0].begin()
        g_up[...] = jnp.zeros_like(g_up)
        g_in[...] = jnp.zeros_like(g_in)
        g_emb[...] = jnp.zeros_like(g_emb)
        small_o[...] = small_in[...]
        carry_s[...] = jnp.zeros_like(carry_s)

    for when, acts in MID_SCHEDULE.items():

        @pl.when(step == when)
        def _(acts=acts):
            run(acts)

    @pl.when(step < blocks)
    def _():
        g_up[...] += tn(normed[...], lifted[...]).reshape(g_up.shape)

    @pl.when(step == blocks - 1)
    def _():
        sums[1].begin()

    @pl.when(step >= blocks)
    def _():
        d_normed = nt(lifted[...], w_up[...])
        value = mixed[...]
        inverse = inv_rms(value)
        small_o[1:2, :] += column_sum(d_normed * (value * inverse))
        d_mixed = final[...] + norm_back(value, inverse, gains[1:2], d_normed)
        mixed_low = d_mixed.astype(BF)
        rest = (d_mixed - mixed_low.astype(F32)).astype(BF)
        ds[...] = nt(mixed_low, w_out[...])
        hot = one_hot(ids[0], vocab)
        g_emb[...] += tn(hot, mixed_low) + tn(hot, rest)
        mixed_o[...] = mixed_low

        low_half = lax.broadcasted_iota(jnp.int32, (ROWS, chunk), 0) < ROWS // 2
        for j in range(hidden // chunk):
            cols = slice(j * chunk, (j + 1) * chunk)
            carry = carry_s[:, cols]
            first = carry
            for tau in reversed(range(steps)):
                at = slice(tau * ROWS, (tau + 1) * ROWS)
                first = keep[at, cols] * (ds[at, cols] + first)
            reached = jnp.where(low_half, swap_halves(first), carry)
            total = jnp.zeros((ROWS, chunk), F32)
            for tau in reversed(range(steps)):
                at = slice(tau * ROWS, (tau + 1) * ROWS)
                lam = ds[at, cols] + reached
                reached = keep[at, cols] * lam
                d_gate = lam * p[at, cols]
                ds[at, cols] = d_gate
                cand[at, :] = lam * q[at, cols]
                total = total + d_gate
            d_pre[:, j * chunk : (j + 1) * chunk] = ds[:, cols].astype(BF)
            d_pre[:, hidden + j * chunk : hidden + (j + 1) * chunk] = cand[...].astype(BF)
            carry_s[:, cols] = jnp.where(low_half, 0.0, swap_halves(reached))
            at = j * chunk
            row = 4 + at // width
            small_o[row : row + 1, at % width : at % width + chunk] += column_sum(total)
            for start in (at, hidden + at):
                g_in[:, start : start + chunk] += tn(conv[...], d_pre[:, start : start + chunk])

    @pl.when(step == 2 * blocks - 1)
    def _():
        run(MID_LAST)
        for one in sums:
            one.finish()


def run_mid(depth, ids, mixed, normed, final, lifted, keep, p, q, conv, gains, w_out, w_up, small, g_down, vocab):
    blocks = ids.shape[0]
    rows = mixed.shape[0] // blocks
    width, ff = w_up.shape
    hidden = w_out.shape[0]
    total = blocks * rows
    last = blocks - 1
    owners = (2, 2, depth, 2)
    back = lambda cols: pl.BlockSpec((rows, cols), lambda i: (jnp.minimum(2 * blocks - 1 - i, last), 0))
    once = pl.BlockSpec((rows, width), lambda i: (jnp.minimum(i, last), 0))
    both = pl.BlockSpec((rows, ff), lambda i: (jnp.minimum(i, 2 * blocks - 1 - i), 0))
    up_shape = owners + (width // (8 * depth), ff)
    shapes = (g_down.shape, up_shape)
    plans = [halves([shape], (2,)) for shape in shapes]
    moving = [Reduce.scratch(shape, plan, depth, n > 0) for n, (shape, plan) in enumerate(zip(shapes, plans))]
    sums = ((width, 2 * hidden), (vocab, width), small.shape, g_down.shape[-2:], up_shape[-2:])
    return pl.pallas_call(
        functools.partial(mid_kernel, depth, plans, [len(m) for m in moving]),
        grid=(2 * blocks,),
        in_specs=[
            pl.BlockSpec((1,) + ids.shape[1:], lambda i: (jnp.minimum(2 * blocks - 1 - i, last), 0, 0)),
            back(width), once, back(width), both, back(hidden), back(hidden), back(hidden), back(width),
        ]
        + [whole(a.shape) for a in (gains, w_out, w_up, small)]
        + [pl.BlockSpec(memory_space=pl.ANY)],
        out_specs=[back(2 * hidden), back(width)] + [whole(s) for s in sums],
        out_shape=[jax.ShapeDtypeStruct((total, 2 * hidden), BF), jax.ShapeDtypeStruct((total, width), BF)] + [jax.ShapeDtypeStruct(s, F32) for s in sums],
        scratch_shapes=[
            pltpu.VMEM(up_shape, F32),
            pltpu.VMEM((rows, hidden), F32),
            pltpu.VMEM((rows, 256), F32),
            pltpu.VMEM((ROWS, hidden), F32),
        ]
        + [piece for group in moving for piece in group],
        compiler_params=pltpu.CompilerParams(
            dimension_semantics=("arbitrary",), collective_id=2, has_side_effects=True, vmem_limit_bytes=63 * MIB
        ),
        name="mid_back_and_reduce",
    )(ids, mixed, normed, final, lifted, keep, p, q, conv, gains, w_out, w_up, small, g_down)


def adam_kernel(shapes, small, squares, count, *refs):
    mats = refs[:5]
    weights, firsts, seconds = refs[5:13], refs[13:21], refs[21:29]
    loss_o, count_o, norm_o = refs[29:32]
    new_w, new_m, new_v = refs[32:40], refs[40:48], refs[48:56]
    kernel, bias_rows = shapes
    grads = [m[...] for m in mats]
    grads.append(small[0:3, :])
    grads.append(small[ROWS : ROWS + kernel, :])
    grads.append(jnp.concatenate([small[4 + r : 5 + r, :] for r in range(bias_rows)], axis=1))
    square = squares[0:1, 0:1]
    for grad in grads[5:]:
        square = square + jnp.sum(jnp.sum(grad * grad, axis=1, keepdims=True), axis=0, keepdims=True)
    norm = jnp.sqrt(square)
    scale = jnp.minimum(1.0, CLIP / (norm + 1e-06))
    norm_o[...] = norm
    loss_o[...] = small[3:4, 0:1]
    count_o[...] = count[0:1, 0:1]
    for i in range(8):
        rate = RATE_MATRIX if i < 5 else RATE_VECTOR
        decay = WEIGHT_DECAY if i < 5 else 0.0
        w, m, v = adam(weights[i][...], grads[i] * scale, firsts[i][...], seconds[i][...], rate, decay)
        new_w[i][...] = w
        new_m[i][...] = m
        new_v[i][...] = v


def run_adam(shapes, mats, small, squares, count, weights, firsts, seconds):
    one = jax.ShapeDtypeStruct((1, 1), F32)
    like = [jax.ShapeDtypeStruct(w.shape, F32) for w in weights]
    args = (small, squares, count) + tuple(mats) + tuple(weights) + tuple(firsts) + tuple(seconds)
    return pl.pallas_call(
        functools.partial(adam_kernel, shapes),
        grid=(1,),
        in_specs=[whole(a.shape) for a in args],
        out_specs=[whole(a.shape) for a in [one] * 3 + like * 3],
        out_shape=[one] * 3 + like * 3,
        compiler_params=pltpu.CompilerParams(vmem_limit_bytes=60 * MIB),
        name="adam_update",
    )(*args)


def body_moved(depth, *args):
    weights, firsts, seconds = args[3:11], args[11:19], args[19:27]
    table, w_in, w_out, w_up, w_down, gains, conv_taps, gate_bias = weights
    width = table.shape[1]
    taps = conv_taps[0]
    keep, p, q, state_low, ids, tab, count, conv, *full = run_front(
        depth, args[:3], table, (w_in[0], w_out[0], w_up[0], w_down[0]), gains, taps, gate_bias
    )
    conv = conv.reshape(-1, width)
    full = [a.reshape(-1, a.shape[-1]) for a in full]
    mixed, normed, final, lifted, g_down, g_head, small = run_tail(ids, state_low, tab, count, gains, *full[1:])
    owned = lambda g: g.reshape((2, 2, depth, 2, -1, g.shape[-1]))
    d_pre, mixed_low, g_in, g_emb, small, r_down, r_up = run_mid(
        depth, ids, mixed, normed, final, lifted, keep, p, q, conv, gains, full[1], full[2], small, owned(g_down),
        tab.shape[0],
    )
    r_in, r_out, r_tab, small, squares = run_last(
        depth, ids, d_pre, state_low, mixed_low, tab, gains, taps, full[0], (g_head, g_emb), small, (r_down, r_up), owned(g_in)
    )
    mats = [r_tab, r_in, r_out, r_up, r_down]
    flat = lambda group: [group[0]] + [a[0] for a in group[1:5]] + [group[5], group[6][0], group[7]]
    out = run_adam(
        (conv_taps.shape[1], gate_bias.shape[1] // width),
        mats, small, squares, count, flat(weights), flat(firsts), flat(seconds),
    )
    shaped = [o.reshape(()) for o in out[:3]]
    for i, o in enumerate(out[3:]):
        shaped.append(o.reshape(weights[i % 8].shape))
    return tuple(shaped)


def choose(mesh, *args):
    ways = mesh.shape["seq"]
    seqs, span = args[0].shape
    if mesh.shape["dp"] == 4 and ways == 8 and seqs == 4 * ways and span == LANES:
        return body_moved(ways // 2, *args)
    return body(*args)


def solution(mesh):
    return jax.shard_map(
        functools.partial(choose, mesh),
        mesh=mesh,
        in_specs=(
            P("dp", "seq"),
            P("dp", "seq"),
            P("dp", "seq"),
            P(("dp", "seq"), None),
            P(None, ("dp", "seq"), None),
            P(None, ("dp", "seq"), None),
            P(None, ("dp", "seq"), None),
            P(None, ("dp", "seq"), None),
            P(),
            P(),
            P(),
            P(("dp", "seq"), None),
            P(None, ("dp", "seq"), None),
            P(None, ("dp", "seq"), None),
            P(None, ("dp", "seq"), None),
            P(None, ("dp", "seq"), None),
            P(),
            P(),
            P(),
            P(("dp", "seq"), None),
            P(None, ("dp", "seq"), None),
            P(None, ("dp", "seq"), None),
            P(None, ("dp", "seq"), None),
            P(None, ("dp", "seq"), None),
            P(),
            P(),
            P(),
        ),
        out_specs=(
            P(),
            P(),
            P(),
            P(("dp", "seq"), None),
            P(None, ("dp", "seq"), None),
            P(None, ("dp", "seq"), None),
            P(None, ("dp", "seq"), None),
            P(None, ("dp", "seq"), None),
            P(),
            P(),
            P(),
            P(("dp", "seq"), None),
            P(None, ("dp", "seq"), None),
            P(None, ("dp", "seq"), None),
            P(None, ("dp", "seq"), None),
            P(None, ("dp", "seq"), None),
            P(),
            P(),
            P(),
            P(("dp", "seq"), None),
            P(None, ("dp", "seq"), None),
            P(None, ("dp", "seq"), None),
            P(None, ("dp", "seq"), None),
            P(None, ("dp", "seq"), None),
            P(),
            P(),
            P(),
        ),
        check_vma=False,
    )
```

```python
import functools

import jax
import jax.numpy as jnp
from jax import lax
from jax.experimental import pallas as pl
from jax.experimental.pallas import tpu as pltpu
from jax.sharding import PartitionSpec as P

V = 256
MICRO = 2
STEP = 3


EPS = 1e-06
CLIP = 0.01
BETA_ONE = 0.5
BETA_TWO = 0.5
ADAM_EPS = 1e-08
RATE_MATRIX = 0.03
RATE_VECTOR = 0.3
WEIGHT_DECAY = 0.1


def from_behind(x, axis, by):
    devices = lax.axis_size(axis)
    pairs = [(i, i + by) for i in range(devices) if 0 <= i + by < devices]
    return lax.ppermute(x, axis, pairs)


def carried_in(part, axis, combine, identity, reverse):
    count = lax.axis_size(axis)
    place = lax.axis_index(axis)
    ahead = count - 1 - place if reverse else place
    gathered = jax.tree.map(lambda a: lax.all_gather(a, axis), part)
    state = jax.tree.map(lambda a, e: jnp.zeros_like(a) + jnp.asarray(e, a.dtype), part, identity)

    def one(lap, state):
        source = count - 1 - lap if reverse else lap
        return combine(
            state, jax.tree.map(lambda a: lax.dynamic_index_in_dim(a, source, 0, False), gathered)
        )

    return lax.fori_loop(0, ahead, one, state)


def matmul(left, right):
    return jnp.dot(left, right, preferred_element_type=jnp.float32)


def matmul_tn(left, right):
    return lax.dot_general(
        left, right, (((0,), (0,)), ((), ())), preferred_element_type=jnp.float32
    )


def matmul_nt(left, right):
    return lax.dot_general(
        left, right, (((1,), (1,)), ((), ())), preferred_element_type=jnp.float32
    )


def rms_norm(values, gain):
    return values * lax.rsqrt(jnp.mean(values * values, axis=-1, keepdims=True) + EPS) * gain


def combine(earlier, later):
    return (earlier[0] * later[0], later[0] * earlier[1] + later[1])


def gates(gate, cand):
    return (jax.nn.sigmoid(-gate), jax.nn.sigmoid(gate) * jax.nn.softplus(cand))


def conv_apply(padded, taps, length):
    total = taps[0] * padded[0:length].astype(jnp.float32)
    for k in range(1, taps.shape[0]):
        total = total + taps[k] * padded[k : k + length].astype(jnp.float32)
    return total


def adam(weight, grad, first, second, rate, decay):
    first = BETA_ONE * first + (1.0 - BETA_ONE) * grad
    second = BETA_TWO * second + (1.0 - BETA_TWO) * grad * grad
    fix_one = 1.0 - BETA_ONE**STEP
    fix_two = 1.0 - BETA_TWO**STEP
    update = first / fix_one / (jnp.sqrt(second / fix_two) + ADAM_EPS)
    return (weight - rate * (update + decay * weight), first, second)


def mixer_front(queue, rim, taps, bias, w_in):
    span, seqs, width = queue.shape
    padded = jnp.concatenate([rim, queue], axis=0)
    conv_low = conv_apply(padded, taps, span).astype(jnp.bfloat16)
    pre = matmul(conv_low.reshape(span * seqs, width), w_in).reshape(span, seqs, -1)
    hidden = bias.shape[0]
    keep, write = gates(pre[..., :hidden] + bias, pre[..., hidden:])
    return (padded, conv_low, pre, keep, write)


def block_tail(state, resid, gain_b, w_out, w_up, w_down):
    span, seqs, width = resid.shape
    state_low = state.astype(jnp.bfloat16).reshape(span * seqs, -1)
    mixed = resid + matmul(state_low, w_out).reshape(span, seqs, width)
    normed_low = rms_norm(mixed, gain_b).astype(jnp.bfloat16).reshape(span * seqs, width)
    lifted = matmul(normed_low, w_up)
    active_low = jax.nn.gelu(lifted).astype(jnp.bfloat16)
    result = mixed + matmul(active_low, w_down).reshape(span, seqs, width)
    return (result, (state_low, mixed, normed_low, lifted, active_low))


def layer_forward(resid, taps, gain_a, gain_b, bias, mats):
    span = resid.shape[0]
    kernel = taps.shape[0]
    queue = rms_norm(resid, gain_a).astype(jnp.bfloat16)
    rim = from_behind(queue[span - kernel + 1 :], "seq", 1)
    padded, conv_low, pre, keep, write = mixer_front(queue, rim, taps, bias, mats[0])
    decay, local = lax.associative_scan(combine, (keep, write), axis=0)
    ones = jnp.ones_like(local[0])
    carry_in = carried_in(
        (decay[-1], local[-1]), "seq", combine, (ones, jnp.zeros_like(ones)), False
    )[1]
    state = local + decay * carry_in[None]
    result, unused = block_tail(state, resid, gain_b, mats[1], mats[2], mats[3])
    return (result, rim, carry_in)


def layer_backward(grad, resid, rim, carry_in, taps, gain_a, gain_b, bias, mats):
    w_in, w_out, w_up, w_down = mats
    span, seqs, width = resid.shape
    kernel = taps.shape[0]
    hidden = bias.shape[0]
    normed_a, norm_back = jax.vjp(rms_norm, resid, gain_a)
    queue = normed_a.astype(jnp.bfloat16)
    padded, conv_low, pre, keep, write = mixer_front(queue, rim, taps, bias, w_in)
    decay, local = lax.associative_scan(combine, (keep, write), axis=0)
    state = local + decay * carry_in[None]
    result, (state_low, mixed, normed_low, lifted, active_low) = block_tail(
        state, resid, gain_b, w_out, w_up, w_down
    )
    grad_low = grad.astype(jnp.bfloat16).reshape(span * seqs, width)
    g_down = matmul_tn(active_low, grad_low)
    d_active = matmul_nt(grad_low, w_down)
    d_lifted_low = jax.vjp(jax.nn.gelu, lifted)[1](d_active)[0].astype(jnp.bfloat16)
    g_up = matmul_tn(normed_low, d_lifted_low)
    d_normed = matmul_nt(d_lifted_low, w_up).reshape(span, seqs, width)
    d_mixed, d_gain_b = jax.vjp(rms_norm, mixed, gain_b)[1](d_normed)
    d_mixed = grad + d_mixed
    mixed_low = d_mixed.astype(jnp.bfloat16).reshape(span * seqs, width)
    g_out = matmul_tn(state_low, mixed_low)
    d_state = matmul_nt(mixed_low, w_out).reshape(span, seqs, hidden)
    follow = jnp.concatenate([keep[1:], jnp.ones_like(keep[:1])], axis=0)
    reach, back_local = lax.associative_scan(combine, (follow, d_state), axis=0, reverse=True)
    ones = jnp.ones_like(keep[0])
    summary = (keep[0] * reach[0], keep[0] * back_local[0])
    carry_out = carried_in(summary, "seq", combine, (ones, jnp.zeros_like(ones)), True)[1]
    adjoint = back_local + reach * carry_out[None]
    before = jnp.concatenate([carry_in[None], state[:-1]], axis=0)
    d_gate, d_cand = jax.vjp(gates, pre[..., :hidden] + bias, pre[..., hidden:])[1](
        (adjoint * before, adjoint)
    )
    d_bias = jnp.sum(d_gate, axis=(0, 1))
    d_pre = (
        jnp.concatenate([d_gate, d_cand], axis=-1)
        .astype(jnp.bfloat16)
        .reshape(span * seqs, 2 * hidden)
    )
    g_in = matmul_tn(conv_low.reshape(span * seqs, width), d_pre)
    d_conv = matmul_nt(d_pre, w_in).reshape(span, seqs, width)
    beyond = from_behind(d_conv[: kernel - 1].astype(jnp.bfloat16), "seq", -1).astype(jnp.float32)
    extended = jnp.concatenate([d_conv, beyond], axis=0)
    d_queue = taps[0] * extended[kernel - 1 : kernel - 1 + span]
    tap_grads = [jnp.sum(d_conv * padded[0:span].astype(jnp.float32), axis=(0, 1))]
    for k in range(1, kernel):
        d_queue = d_queue + taps[k] * extended[kernel - 1 - k : kernel - 1 - k + span]
        tap_grads.append(jnp.sum(d_conv * padded[k : k + span].astype(jnp.float32), axis=(0, 1)))
    rounded = lax.optimization_barrier(d_queue.astype(jnp.bfloat16)).astype(jnp.float32)
    d_resid, d_gain_a = norm_back(rounded)
    return (
        d_mixed + d_resid,
        (g_in, g_out, g_up, g_down),
        (jnp.stack(tap_grads), d_gain_a, d_gain_b, d_bias),
    )


def body(
    tokens,
    targets,
    counted,
    table,
    w_in,
    w_out,
    w_up,
    w_down,
    gains,
    conv_taps,
    gate_bias,
    m_table,
    m_in,
    m_out,
    m_up,
    m_down,
    m_gains,
    m_taps,
    m_bias,
    v_table,
    v_in,
    v_out,
    v_up,
    v_down,
    v_gains,
    v_taps,
    v_bias,
):
    layers = w_in.shape[0]
    seq_dev, span = tokens.shape
    rows = seq_dev // MICRO
    width = table.shape[1]
    vocab = V
    mask = counted.astype(jnp.float32)
    count = lax.psum(jnp.sum(mask), ("dp", "seq"))
    shards = (
        w_in.astype(jnp.bfloat16),
        w_out.astype(jnp.bfloat16),
        w_up.astype(jnp.bfloat16),
        w_down.astype(jnp.bfloat16),
    )
    layer_gains = gains[: 2 * layers].reshape(layers, 2, width)
    columns = jnp.arange(vocab, dtype=jnp.int32)

    def forward_step(resid, inputs):
        pieces, taps, pair, bias = inputs
        mats = (
            lax.all_gather(pieces[0], ("dp", "seq"), axis=0, tiled=True),
            lax.all_gather(pieces[1], ("dp", "seq"), axis=0, tiled=True),
            lax.all_gather(pieces[2], ("dp", "seq"), axis=0, tiled=True),
            lax.all_gather(pieces[3], ("dp", "seq"), axis=0, tiled=True),
        )
        result, rim, carry_in = layer_forward(resid, taps, pair[0], pair[1], bias, mats)
        return (result, (resid, rim, carry_in))

    def backward_step(grad, inputs):
        saved, pieces, taps, pair, bias = inputs
        mats = (
            lax.all_gather(pieces[0], ("dp", "seq"), axis=0, tiled=True),
            lax.all_gather(pieces[1], ("dp", "seq"), axis=0, tiled=True),
            lax.all_gather(pieces[2], ("dp", "seq"), axis=0, tiled=True),
            lax.all_gather(pieces[3], ("dp", "seq"), axis=0, tiled=True),
        )
        grad, full, small = layer_backward(
            grad, saved[0], saved[1], saved[2], taps, pair[0], pair[1], bias, mats
        )
        full = (
            lax.psum_scatter(full[0], ("dp", "seq"), scatter_dimension=0, tiled=True),
            lax.psum_scatter(full[1], ("dp", "seq"), scatter_dimension=0, tiled=True),
            lax.psum_scatter(full[2], ("dp", "seq"), scatter_dimension=0, tiled=True),
            lax.psum_scatter(full[3], ("dp", "seq"), scatter_dimension=0, tiled=True),
        )
        return (grad, (full, small))

    loss = jnp.zeros((), jnp.float32)
    g_table = jnp.zeros((vocab, width), jnp.float32)
    acc_full = None
    acc_small = None
    for index in range(MICRO):
        tok = tokens[index * rows : (index + 1) * rows].T.reshape(-1)
        tgt = targets[index * rows : (index + 1) * rows].T.reshape(-1)
        weights = mask[index * rows : (index + 1) * rows].T.reshape(-1)
        tab = lax.all_gather(table.astype(jnp.bfloat16), ("dp", "seq"), axis=0, tiled=True)
        picks = tok[:, None] == columns[None, :]
        resid = matmul(picks.astype(jnp.bfloat16), tab).reshape(span, rows, width)
        final, saved = lax.scan(forward_step, resid, (shards, conv_taps, layer_gains, gate_bias))
        normed_f, final_back = jax.vjp(rms_norm, final, gains[2 * layers])
        normed_low = normed_f.astype(jnp.bfloat16).reshape(span * rows, width)
        logits = matmul_nt(normed_low, tab)
        top = jnp.max(logits, axis=-1, keepdims=True)
        lse = jnp.log(jnp.sum(jnp.exp(logits - top), axis=-1)) + top[:, 0]
        hits = (tgt[:, None] == columns[None, :]).astype(jnp.float32)
        picked = jnp.sum(hits * logits, axis=-1)
        loss = loss + jnp.sum(weights * (lse - picked))
        d_logits = ((jnp.exp(logits - lse[:, None]) - hits) * (weights / count)[:, None]).astype(
            jnp.bfloat16
        )
        g_table = g_table + matmul_tn(d_logits, normed_low)
        d_normed = matmul(d_logits, tab).reshape(span, rows, width)
        d_final, d_gain_f = final_back(d_normed)
        grad0, (full, small) = lax.scan(
            backward_step, d_final, (saved, shards, conv_taps, layer_gains, gate_bias), reverse=True
        )
        g_table = g_table + lax.dot_general(
            picks.astype(jnp.float32),
            grad0.reshape(span * rows, width),
            (((0,), (0,)), ((), ())),
            precision=lax.Precision.HIGHEST,
        )
        layer_gain_grads = jnp.stack([small[1], small[2]], axis=1).reshape(2 * layers, width)
        vectors = (jnp.concatenate([layer_gain_grads, d_gain_f[None]], axis=0), small[0], small[3])
        if index == 0:
            acc_full, acc_small = (full, vectors)
        else:
            acc_full = jax.tree.map(lambda a, b: a + b, acc_full, full)
            acc_small = jax.tree.map(lambda a, b: a + b, acc_small, vectors)
    table_shard = lax.psum_scatter(g_table, ("dp", "seq"), scatter_dimension=0, tiled=True)
    g_gains, g_taps, g_bias = lax.psum((acc_small[0], acc_small[1], acc_small[2]), ("dp", "seq"))
    matrices = (table_shard, acc_full[0], acc_full[1], acc_full[2], acc_full[3])
    squares = jnp.zeros((), jnp.float32)
    for grad in matrices:
        squares = squares + jnp.sum(grad * grad)
    squares_all, loss_all = lax.psum((squares, loss), ("dp", "seq"))
    small_squares = jnp.sum(g_gains * g_gains) + jnp.sum(g_taps * g_taps) + jnp.sum(g_bias * g_bias)
    norm = jnp.sqrt(squares_all + small_squares)
    scale = jnp.minimum(1.0, CLIP / (norm + 1e-06))
    params = (table, w_in, w_out, w_up, w_down, gains, conv_taps, gate_bias)
    grads = matrices + (g_gains, g_taps, g_bias)
    firsts = (m_table, m_in, m_out, m_up, m_down, m_gains, m_taps, m_bias)
    seconds = (v_table, v_in, v_out, v_up, v_down, v_gains, v_taps, v_bias)
    news, next_m, next_v = ([], [], [])
    for index in range(8):
        rate = RATE_MATRIX if index < 5 else RATE_VECTOR
        decay = WEIGHT_DECAY if index < 5 else 0.0
        weight, first, second = adam(
            params[index], grads[index] * scale, firsts[index], seconds[index], rate, decay
        )
        news.append(weight)
        next_m.append(first)
        next_v.append(second)
    return (
        loss_all,
        count,
        norm,
        news[0],
        news[1],
        news[2],
        news[3],
        news[4],
        news[5],
        news[6],
        news[7],
        next_m[0],
        next_m[1],
        next_m[2],
        next_m[3],
        next_m[4],
        next_m[5],
        next_m[6],
        next_m[7],
        next_v[0],
        next_v[1],
        next_v[2],
        next_v[3],
        next_v[4],
        next_v[5],
        next_v[6],
        next_v[7],
    )


BF = jnp.bfloat16
F32 = jnp.float32
MIB = 1 << 20
LANES = 128
ROWS = 8
GELU_A = 0.7978845608028654
GELU_B = 0.044715
LOG2E = 1.4426950408889634


def nn(left, right):
    return jnp.dot(left, right, preferred_element_type=F32)


def tn(left, right):
    return lax.dot_general(left, right, (((0,), (0,)), ((), ())), preferred_element_type=F32)


def nt(left, right):
    return lax.dot_general(left, right, (((1,), (1,)), ((), ())), preferred_element_type=F32)


def inv_rms(values):
    return lax.rsqrt(jnp.mean(values * values, axis=-1, keepdims=True) + EPS)


def norm_back(values, inverse, gain, grad):
    width = values.shape[-1]
    scaled = grad * gain
    dot = jnp.sum(scaled * values, axis=-1, keepdims=True)
    return inverse * scaled - values * (inverse * inverse * inverse * dot * (1.0 / width))


def column_sum(values):
    return jnp.sum(values, axis=0, keepdims=True)


def swap_halves(tile):
    return pltpu.roll(tile, ROWS // 2, tile.ndim - 2)


def spread_steps(tile, row, start, cols):
    parts = []
    for tau in range(LANES // 2):
        piece = tile[row : row + ROWS, start + tau : start + tau + 1]
        parts.append(jnp.broadcast_to(piece, (ROWS, cols)))
    return jnp.concatenate(parts, axis=0)


def hits(tile, start, vocab):
    lane = lax.broadcasted_iota(jnp.int32, (ROWS, vocab), 1)
    parts = []
    for tau in range(LANES // 2):
        piece = tile[0:ROWS, start + tau : start + tau + 1]
        parts.append((piece == lane).astype(F32))
    return jnp.concatenate(parts, axis=0)


def one_hot(tile, vocab):
    return hits(tile, 0, vocab).astype(BF)


def whole(shape):
    zeros = (0,) * len(shape)
    return pl.BlockSpec(shape, lambda i: zeros, pipeline_mode=pl.Buffered(1))


def place():
    dp = lax.axis_index("dp")
    seq = lax.axis_index("seq")
    return dp // 2, dp % 2, seq // 2, seq % 2


def device(y, x, z, core):
    return (y * 2 + x, z * 2 + core)


def greet_all(y, x, z, core, depth):
    barrier = pltpu.get_barrier_semaphore()
    for n in range(1, 8 * depth):
        dy, dx, dz, dc = n // (4 * depth), n // (2 * depth) % 2, n // 2 % depth, n % 2
        peer = device((y + dy) % 2, (x + dx) % 2, (z + dz) % depth, (core + dc) % 2)
        pl.semaphore_signal(barrier, inc=1, device_id=peer, device_id_type=pl.DeviceIdType.MESH)
    pl.semaphore_wait(barrier, 8 * depth - 1)


def greet(y, x, z, core, depth):
    barrier = pltpu.get_barrier_semaphore()
    peers = [device(1 - y, x, z, core), device(y, 1 - x, z, core), device(1 - y, 1 - x, z, core)]
    for dz in range(depth):
        for dc in range(2):
            if dz or dc:
                peers.append(device(y, x, (z + dz) % depth, (core + dc) % 2))
    for peer in peers:
        pl.semaphore_signal(barrier, inc=1, device_id=peer, device_id_type=pl.DeviceIdType.MESH)
    pl.semaphore_wait(barrier, len(peers))


def remote(src, dst, send, recv, peer):
    return pltpu.make_async_remote_copy(
        src_ref=src,
        dst_ref=dst,
        send_sem=send,
        recv_sem=recv,
        device_id=peer,
        device_id_type=pl.DeviceIdType.MESH,
    )


def in_order(groups, phases, act):
    for time in range(len(groups) + phases - 1):
        for phase in range(phases - 1, -1, -1):
            at = time - phase
            if 0 <= at < len(groups):
                for item in groups[at]:
                    act(item, phase)


def grouped(plan):
    return [[i, i + 1] for i in range(0, len(plan), 2)]


class Gather:
    def __init__(self, plan, depth, sources, outs, send, recv, at):
        self.plan, self.depth, self.sources, self.outs, self.send, self.recv = plan, depth, sources, outs, send, recv
        self.y, self.x, self.z, self.core = at

    def copies(self, i, phase):
        t, lo, hi, along_x = self.plan[i]
        cols = pl.ds(lo, hi - lo)
        y, x, z, core = self.y, self.x, self.z, self.core
        out = self.outs[t]
        by_x, by_y = device(y, 1 - x, z, core), device(1 - y, x, z, core)
        if phase == 0:
            mine = out.at[y, x, z, core, :, cols]
            source = mine if self.sources[t] is None else self.sources[t].at[:, cols]
            moves = [(source, mine, device(y, x, (z + dz) % self.depth, core)) for dz in range(1, self.depth)]
        elif phase == 1:
            part = out.at[y, x, :, core, :, cols]
            moves = [(part, part, by_x if along_x else by_y)]
        elif phase == 2:
            part = out.at[y, :, :, core, :, cols] if along_x else out.at[:, x, :, core, :, cols]
            moves = [(part, part, by_y if along_x else by_x)]
        else:
            part = out.at[:, :, :, core, :, cols]
            moves = [(part, part, device(y, x, z, 1 - core))]
        base = 0 if phase == 0 else self.depth - 2 + phase
        return [
            remote(src, dst, self.send.at[i, base + n], self.recv.at[i, base + n], peer)
            for n, (src, dst, peer) in enumerate(moves)
        ]

    def begin(self, i):
        for copy in self.copies(i, 0):
            copy.start()

    def act(self, i, phase):
        for copy in self.copies(i, phase):
            copy.wait_recv()
        if phase < 3:
            for copy in self.copies(i, phase + 1):
                copy.start()

    def finish(self):
        for i in range(len(self.plan)):
            for phase in range(4):
                for copy in self.copies(i, phase):
                    copy.wait_send()


def add_into(target, other):
    lead = [()]
    for d in target.shape[: len(target.shape) - 2]:
        lead = [index + (n,) for index in lead for n in range(d)]
    for index in lead:
        target[index] = target[index] + other[index]


def halves(shapes, cuts=None):
    plan = []
    for t, shape in enumerate(shapes):
        pieces = 2 * (cuts[t] if cuts else 1)
        wide = shape[-1] // pieces
        for n in range(pieces):
            plan.append((t, n * wide, (n + 1) * wide, n % 2 == 0))
    return plan


class Reduce:
    def __init__(self, plan, depth, source, resident, out, refs, at):
        self.plan, self.depth, self.source, self.resident, self.out = plan, depth, source, resident, out
        self.send, self.recv = refs[:2]
        if not resident:
            self.loads, self.own = refs[2:4]
        first = 2 if resident else 4
        self.bufs = [refs[first + 3 * i : first + 3 * i + 3] for i in range(len(plan))]
        self.y, self.x, self.z, self.core = at

    def scratch(shape, plan, depth, resident):
        piece = (shape[-2], plan[0][2] - plan[0][1])
        dma = lambda *n: pltpu.SemaphoreType.DMA(n)
        own = [] if resident else [dma(len(plan)), pltpu.VMEM((len(plan), 2, 2, depth) + piece, F32)]
        each = [
            pltpu.VMEM((2, 2, depth) + piece, F32), pltpu.VMEM((2, depth) + piece, F32), pltpu.VMEM((2, depth) + piece, F32)
        ]
        return [dma(len(plan), depth + 2), dma(len(plan), depth + 2)] + own + each * len(plan)

    def load(self, i):
        t, lo, hi, _ = self.plan[i]
        source = self.source.at[:, :, :, self.core, :, pl.ds(lo, hi - lo)]
        return pltpu.make_async_copy(source, self.own.at[i], self.loads.at[i])

    def copies(self, i, phase):
        t, lo, hi, along_x = self.plan[i]
        y, x, z, core = self.y, self.x, self.z, self.core
        whole, half, quarter = self.bufs[i]
        by_x, by_y = device(y, 1 - x, z, core), device(1 - y, x, z, core)
        if phase == 0:
            source = self.source.at[:, :, :, 1 - core, :, pl.ds(lo, hi - lo)]
            moves = [(source, whole, device(y, x, z, 1 - core))]
        elif phase == 1:
            moves = [(whole.at[1 - y], half, by_y) if along_x else (whole.at[:, 1 - x], half, by_x)]
        elif phase == 2:
            moves = [(half.at[1 - x], quarter.at[0], by_x) if along_x else (half.at[1 - y], quarter.at[0], by_y)]
        else:
            moves = []
            for dz in range(1, self.depth):
                pz = (z + dz) % self.depth
                moves.append((quarter.at[0, pz], quarter.at[1, dz], device(y, x, pz, core)))
        return [
            remote(src, dst, self.send.at[i, phase + n], self.recv.at[i, phase + n], peer)
            for n, (src, dst, peer) in enumerate(moves)
        ]

    def begin(self):
        for i in range(len(self.plan)):
            for copy in self.copies(i, 0):
                copy.start()
            if not self.resident:
                self.load(i).start()

    def pair(self, n, phase):
        for i in (2 * n, 2 * n + 1):
            self.act(i, phase)

    def act(self, i, phase):
        t, lo, hi, along_x = self.plan[i]
        y, x, z, core = self.y, self.x, self.z, self.core
        whole, half, quarter = self.bufs[i]
        for copy in self.copies(i, phase):
            copy.wait_recv()
        if phase == 0:
            if self.resident:
                add_into(whole, self.source.at[:, :, :, core, :, pl.ds(lo, hi - lo)])
            else:
                self.load(i).wait()
                add_into(whole, self.own.at[i])
        elif phase == 1:
            add_into(half, whole.at[y] if along_x else whole.at[:, x])
        elif phase == 2:
            add_into(quarter.at[0], half.at[x] if along_x else half.at[y])
        else:
            total = quarter[0, z]
            for dz in range(1, self.depth):
                total = total + quarter[1, dz]
            self.out[:, lo:hi] = total
            return
        for copy in self.copies(i, phase + 1):
            copy.start()

    def finish(self):
        for i in range(len(self.plan)):
            for phase in range(4):
                for copy in self.copies(i, phase):
                    copy.wait_send()


class Everywhere:
    def __init__(self, slots, sends, recvs, depth, at):
        y, x, z, core = at
        self.slots, self.count = slots, 8 * depth
        self.me = ((y * 2 + x) * depth + z) * 2 + core
        self.copies = []
        mine = slots.at[self.me]
        for n in range(1, self.count):
            dy, dx, dz, dc = n // (4 * depth), n // (2 * depth) % 2, n // 2 % depth, n % 2
            peer = device((y + dy) % 2, (x + dx) % 2, (z + dz) % depth, (core + dc) % 2)
            self.copies.append(remote(mine, mine, sends.at[n], recvs.at[n], peer))

    def begin(self, value):
        self.slots[self.me] = value
        for copy in self.copies:
            copy.start()

    def end(self):
        for copy in self.copies:
            copy.wait()
        value = self.slots[0]
        for n in range(1, self.count):
            value = value + self.slots[n]
        return value


class EverywhereHalved:
    def __init__(self, whole, parts, sends, recvs, depth, at):
        y, x, z, core = at
        self.whole, self.parts, self.depth, self.core = whole, parts, depth, core
        other = device(y, x, z, 1 - core)
        self.first = remote(whole.at[0], whole.at[1], sends.at[0], recvs.at[0], other)
        self.spot = (z, depth + y * 2 + x)
        self.along, self.plane = [], []
        mine = parts.at[z]
        for dz in range(1, depth):
            peer = device(y, x, (z + dz) % depth, core)
            self.along.append(remote(mine, mine, sends.at[dz], recvs.at[dz], peer))
        mine = parts.at[self.spot[1]]
        for n, (dy, dx) in enumerate(((0, 1), (1, 0), (1, 1))):
            peer = device((y + dy) % 2, (x + dx) % 2, z, core)
            self.plane.append(remote(mine, mine, sends.at[depth + n], recvs.at[depth + n], peer))
        mine = whole.at[2, core]
        self.last = remote(mine, mine, sends.at[depth + 3], recvs.at[depth + 3], other)

    def total(self, lo, hi):
        value = self.parts[lo]
        for n in range(lo + 1, hi):
            value = value + self.parts[n]
        return value

    def step(self, n, value=None):
        if n == 0:
            self.whole[0] = value.reshape(self.whole.shape[1:])
            self.first.start()
        elif n == 1:
            self.first.wait()
            lower = self.whole[self.core, self.core] + self.whole[1 - self.core, self.core]
            self.parts[self.spot[0]] = lower
            for copy in self.along:
                copy.start()
        elif n == 2:
            for copy in self.along:
                copy.wait()
            self.parts[self.spot[1]] = self.total(0, self.depth)
            for copy in self.plane:
                copy.start()
        elif n == 3:
            for copy in self.plane:
                copy.wait()
            self.whole[2, self.core] = self.total(self.depth, self.depth + 4)
            self.last.start()
        else:
            self.last.wait()
            return self.whole[2].reshape(-1, self.whole.shape[-1])


SCHEDULE = {
    0: [(0, 0, 0)], 1: [(0, 1, 0)], 5: [(0, 0, 1), (0, 2, 0)], 8: [(0, 1, 1), (0, 3, 0)], 9: [(0, 0, 2), (0, 2, 1)],
    10: [(0, 1, 2), (1, 0, 0)], 11: [(0, 3, 1), (0, 2, 2), (1, 1, 0)], 13: [(0, 3, 2), (1, 0, 1)], 14: [(1, 1, 1)], 15: [(1, 0, 2)],
}
LEFT_OVER = [
    (2, 0, 0), (3, 0, 1), (1, 1, 2), (2, 0, 1), (3, 0, 2), (2, 0, 2), (0, 0, 3), (0, 1, 3), (0, 2, 3), (3, 0, 3), (0, 3, 3),
    (1, 0, 3), (1, 1, 3), (2, 0, 3),
]


def last_kernel(depth, plans, counts, *refs):
    ids, d_pre, state_low, mixed_low, tab, gains, taps, small_in, r_down, r_up, w_in_h, g_tab_ah, g_tab_bh, g_in = refs[:14]
    r_in, r_out, r_tab, small_o, squares_o = refs[14:19]
    small, g_out, g_tab, qtab, ext, head_s, hot_sum, w_in, g_tab_a, g_tab_b, kept_sem = refs[19:30]
    whole_s, part_s, sq_slots, sends, recvs, sq_sends, sq_recvs = refs[30:37]
    spot = place()
    sums, at = [], 37
    for n, (source, out) in enumerate(((g_in, r_in), (g_out, r_out), (g_tab, r_tab))):
        sums.append(Reduce(plans[n], depth, source, n > 0, out, refs[at : at + counts[n]], spot))
        at += counts[n]
    smalls = EverywhereHalved(whole_s, part_s, sends, recvs, depth, spot)
    squares = Everywhere(sq_slots, sq_sends, sq_recvs, depth, spot)
    step = pl.program_id(0)
    kept = [
        pltpu.make_async_copy(src, dst, kept_sem.at[n])
        for n, (src, dst) in enumerate(((w_in_h, w_in), (g_tab_ah, g_tab_a), (g_tab_bh, g_tab_b)))
    ]
    blocks = pl.num_programs(0) // 2
    rows = d_pre.shape[0]
    vocab, width = tab.shape
    kernel = taps.shape[0]
    rim = (kernel - 1) * ROWS

    def run(acts):
        for n, pair, phase in acts:
            if n == 3:
                smalls.step(phase)
            else:
                sums[n].pair(pair, phase)

    @pl.when(step == 0)
    def _():
        greet_all(*spot, depth)
        sums[0].begin()
        for copy in kept:
            copy.start()
        wide = tab[...].astype(BF).astype(F32)
        qtab[...] = (wide * inv_rms(wide) * gains[0:1]).astype(BF)
        g_out[...] = jnp.zeros_like(g_out)
        hot_sum[...] = jnp.zeros_like(hot_sum)
        small[...] = jnp.zeros_like(small)
        small[0:ROWS, :] = small_in[...]
        head_s[...] = jnp.zeros_like(head_s)

    for when, acts in SCHEDULE.items():

        @pl.when(step == when)
        def _(acts=acts):
            run(acts)

    @pl.when(step < blocks)
    def _():
        g_out[...] += tn(state_low[...], mixed_low[...]).reshape(g_out.shape)

    @pl.when(step == blocks - 1)
    def _():
        sums[1].begin()
        for copy in kept:
            copy.wait()

    @pl.when(step >= blocks)
    def _():
        ext[0:rows, :] = nt(d_pre[...], w_in[...])
        half = lax.broadcasted_iota(jnp.int32, (rim, width), 0) % ROWS < ROWS // 2
        mine = ext[0:rim, :]
        ext[rows:, :] = jnp.where(
            half,
            swap_halves(mine.reshape(kernel - 1, ROWS, width)).reshape(rim, width),
            swap_halves(head_s[...].reshape(kernel - 1, ROWS, width)).reshape(rim, width),
        )
        head_s[...] = mine
        here = ids[0]
        hot = one_hot(here, vocab)
        known = nn(hot, qtab[...])
        d_queue = None
        for k in range(kernel):
            shift = (kernel - 1 - k) * ROWS
            part = ext[shift : shift + rows, :]
            term = taps[k : k + 1] * part
            d_queue = term if d_queue is None else d_queue + term
            small[ROWS + k : ROWS + k + 1, :] += column_sum(part * known)
        hot_sum[...] += tn(hot, d_queue.astype(BF))

    @pl.when(step == 2 * blocks - 1)
    def _():
        wide = tab[...].astype(BF).astype(F32)
        inverse = inv_rms(wide)
        total = hot_sum[...]
        g_tab[...] = (
            g_tab_a[...] + g_tab_b[...] + norm_back(wide, inverse, gains[0:1], total)
        ).reshape(g_tab.shape)
        sums[2].begin()
        small[0:1, :] = column_sum(total * (wide * inverse))
        smalls.step(0, small[...])
        run(LEFT_OVER)
        square = jnp.zeros((1, 1), F32)
        for out in (r_in, r_out, r_tab, r_down, r_up):
            value = out[...]
            square = square + jnp.sum(jnp.sum(value * value, axis=1, keepdims=True), axis=0, keepdims=True)
        squares.begin(jnp.broadcast_to(square, (1, LANES)))
        small_o[...] = smalls.step(4)
        squares_o[...] = jnp.broadcast_to(squares.end(), (ROWS, LANES))
        for one in sums:
            one.finish()


def run_last(depth, ids, d_pre, state_low, mixed_low, tab, gains, taps, w_in, g_tabs, small, done, g_in):
    blocks = ids.shape[0]
    rows = d_pre.shape[0] // blocks
    vocab, width = tab.shape
    kernel = taps.shape[0]
    rim = (kernel - 1) * ROWS
    last = blocks - 1
    owners = (2, 2, depth, 2)
    hidden = state_low.shape[1]
    shapes = (g_in.shape, owners + (hidden // (8 * depth), width), owners + (vocab // (8 * depth), width))
    plans = [halves([shape], (cuts,)) for shape, cuts in zip(shapes, (4, 2, 1))]
    back = lambda i: jnp.minimum(2 * blocks - 1 - i, last)
    once = lambda cols: pl.BlockSpec((rows, cols), lambda i: (jnp.minimum(i, last), 0))
    moving = [Reduce.scratch(shape, plan, depth, n > 0) for n, (shape, plan) in enumerate(zip(shapes, plans))]
    out = [s[-2:] for s in shapes] + [(2 * ROWS, width), (ROWS, LANES)]
    dma = lambda *shape: pltpu.SemaphoreType.DMA(shape)
    fixed = (tab, gains, taps, small) + tuple(done)
    return pl.pallas_call(
        functools.partial(last_kernel, depth, plans, [len(m) for m in moving]),
        grid=(2 * blocks,),
        in_specs=[
            pl.BlockSpec((1,) + ids.shape[1:], lambda i: (back(i), 0, 0)),
            pl.BlockSpec((rows, d_pre.shape[1]), lambda i: (back(i), 0)),
            once(hidden),
            once(width),
        ]
        + [whole(a.shape) for a in fixed]
        + [pl.BlockSpec(memory_space=pl.ANY)] * 4,
        out_specs=[whole(s) for s in out],
        out_shape=[jax.ShapeDtypeStruct(s, F32) for s in out],
        scratch_shapes=[
            pltpu.VMEM((2 * ROWS, width), F32),
            pltpu.VMEM(shapes[1], F32),
            pltpu.VMEM(shapes[2], F32),
            pltpu.VMEM((vocab, width), BF),
            pltpu.VMEM((rim + rows, width), F32),
            pltpu.VMEM((rim, width), F32),
            pltpu.VMEM((vocab, width), F32),
            pltpu.VMEM(w_in.shape, BF),
            pltpu.VMEM((vocab, width), F32),
            pltpu.VMEM((vocab, width), F32),
            dma(3),
            pltpu.VMEM((3, 2, ROWS, width), F32),
            pltpu.VMEM((depth + 4, ROWS, width), F32),
            pltpu.VMEM((8 * depth, 1, LANES), F32),
            dma(depth + 4),
            dma(depth + 4),
            dma(8 * depth),
            dma(8 * depth),
        ]
        + [piece for group in moving for piece in group],
        compiler_params=pltpu.CompilerParams(
            dimension_semantics=("arbitrary",), collective_id=1, has_side_effects=True, vmem_limit_bytes=62 * MIB
        ),
        name="last_back_and_reduce",
    )(ids, d_pre, state_low, mixed_low, *fixed, w_in, *g_tabs, g_in)


def conv_block(block, ids_s, qtab, taps, conv_s, padq, tail_s):
    _, rows, width = conv_s.shape
    vocab = qtab.shape[0]
    kernel = taps.shape[0]
    rim = (kernel - 1) * ROWS
    queue = nn(one_hot(ids_s[block], vocab), qtab[...])
    padq[rim:, :] = queue
    half = lax.broadcasted_iota(jnp.int32, (rim, width), 0) % ROWS < ROWS // 2
    before = tail_s[...].reshape(kernel - 1, ROWS, width)
    latest = padq[rows:, :].reshape(kernel - 1, ROWS, width)
    padq[0:rim, :] = jnp.where(
        half, swap_halves(before).reshape(rim, width), swap_halves(latest).reshape(rim, width)
    )
    tail_s[...] = padq[rows:, :]
    conv = taps[0:1] * padq[0:rows, :]
    for k in range(1, kernel):
        conv = conv + taps[k : k + 1] * padq[k * ROWS : k * ROWS + rows, :]
    conv_s[block] = conv.astype(BF)


def front_block(conv, bias, w_in, keep_o, p_o, q_o, state_o, carry_s, big):
    rows, hidden = keep_o.shape
    steps = rows // ROWS
    chunk = 256
    low_half = lax.broadcasted_iota(jnp.int32, (ROWS, chunk), 0) < ROWS // 2
    for j in range(hidden // chunk):
        cols = slice(j * chunk, (j + 1) * chunk)
        gate = nn(conv[...], w_in[:, j * chunk : (j + 1) * chunk]) + bias[0:1, cols]
        cand = nn(conv[...], w_in[:, hidden + j * chunk : hidden + (j + 1) * chunk])
        grown = jnp.exp2(jnp.minimum(gate * -LOG2E, 120.0))
        write_gate = pl.reciprocal(1.0 + grown)
        keep_o[:, cols] = grown * write_gate
        small = jnp.exp2(jnp.abs(cand) * -LOG2E)
        one_more = 1.0 + small
        soft = jnp.maximum(cand, 0.0) + (jnp.log(one_more) + (small - (one_more - 1.0)))
        p_o[:, cols] = write_gate
        q_o[:, cols] = write_gate * jnp.exp2((cand - soft) * LOG2E)
        big[:, cols] = write_gate * soft

        carry = carry_s[:, cols]
        end = carry
        for tau in range(steps):
            at = slice(tau * ROWS, (tau + 1) * ROWS)
            end = keep_o[at, cols] * end + big[at, cols]
        state = jnp.where(low_half, carry, swap_halves(end))
        for tau in range(steps):
            at = slice(tau * ROWS, (tau + 1) * ROWS)
            change = big[at, cols] - p_o[at, cols] * state
            p_o[at, cols] = keep_o[at, cols] * change
            state = state + change
            big[at, cols] = state
        state_o[:, cols] = big[:, cols].astype(BF)
        carry_s[:, cols] = jnp.where(low_half, swap_halves(state), 0.0)


GATHER_SCHEDULE = {1: [(0, 1), (3, 0)], 2: [(1, 1), (4, 0)], 3: [(2, 1), (0, 2)], 4: [(3, 1), (1, 2)], 5: [(4, 1), (2, 2)], 6: [(3, 2)], 7: [(4, 2)]}
GATHER_LAST = [(0, 3), (1, 3), (2, 3), (3, 3), (4, 3)]


def front_kernel(
    depth, now, later,
    tokens, targets, counted, table, w_in, w_out, w_up, w_down, gains, taps, bias,
    keep_o, p_o, q_o, state_o, ids_o, tab_o, count_o, conv_o, w_in_o, w_out_o, w_up_o, w_down_o,
    ids, ids_s, tab_s, count_s, in_s, out_s, up_s, down_s, qtab, conv_s, padq, tail_s, carry_s, big,
    ids_send, ids_recv, now_send, now_recv, later_send, later_recv, own_sem, in_sem,
):
    step = pl.program_id(0)
    blocks = pl.num_programs(0)
    spot = place()
    y, x, z, core = spot
    me = z * 2 + core
    onward = [
        pltpu.make_async_copy(in_s, w_in_o, in_sem.at[0]),
        pltpu.make_async_copy(conv_s, conv_o, in_sem.at[1]),
    ]
    first = Gather(now, depth, [None] * 3, [tab_s, count_s, in_s], now_send, now_recv, spot)
    rest = Gather(later, depth, [out_s, up_s, down_s], [w_out_o, w_up_o, w_down_o], later_send, later_recv, spot)
    later_groups = grouped(later)
    own = [
        pltpu.make_async_copy(src, dst.at[y, x, z, core], own_sem.at[n])
        for n, (src, dst) in enumerate(((out_s, w_out_o), (up_s, w_up_o), (down_s, w_down_o)))
    ]
    spread = []
    for dz in range(depth):
        for dc in range(2):
            if dz or dc:
                pz, pc = (z + dz) % depth, (core + dc) % 2
                n = dz * 2 + dc
                spread.append(
                    remote(ids.at[pz * 2 + pc], ids_s.at[me], ids_send.at[n], ids_recv.at[n], device(y, x, pz, pc))
                )

    @pl.when(step == 0)
    def _():
        half = table.shape[1] // 2
        tab_s[y, x, z, core] = jnp.concatenate([table[:, 0:half], table[:, half:]], axis=0).astype(BF)
        share = counted[...].astype(F32)
        share = jnp.sum(jnp.sum(share, axis=1, keepdims=True), axis=0, keepdims=True)
        count_s[y, x, z, core] = jnp.broadcast_to(share, count_o.shape)
        in_s[y, x, z, core] = w_in[...].astype(BF)
        seqs, span = tokens.shape
        seqs //= 2 * depth
        for n in range(2 * depth):
            parts = []
            for array in (tokens, targets, counted):
                mine = array[n * seqs : (n + 1) * seqs, :]
                parts.append(jnp.concatenate([mine[:, 0 : span // 2], mine[:, span // 2 :]], axis=0))
            top = jnp.concatenate([parts[0], parts[1]], axis=1)
            ids[n] = jnp.concatenate([top, jnp.concatenate([parts[2], parts[2]], axis=1)], axis=0)
        ids_s[me] = ids[me]
        greet(*spot, depth)
        pairs = [(i, i + 1) for i in range(0, len(now), 2)]

        def act(pair, phase):
            for i in pairs[pair]:
                first.act(i, phase)

        def begin(pair):
            for i in pairs[pair]:
                first.begin(i)

        begin(0)
        for copy in spread:
            copy.start()
        begin(1)
        begin(2)
        act(0, 0)
        out_s[...] = w_out[...].astype(BF)
        up_s[...] = w_up[...].astype(BF)
        down_s[...] = w_down[...].astype(BF)
        for copy in own:
            copy.start()
        act(1, 0)
        begin(3)
        act(0, 1)
        act(2, 0)
        begin(4)
        for i in (0, 1, 2, 3):
            rest.begin(i)
        act(1, 1)
        act(0, 2)
        act(3, 0)
        act(2, 1)
        act(4, 0)
        for i in range(4, len(later)):
            rest.begin(i)
        act(1, 2)
        act(0, 3)
        act(3, 1)
        for copy in spread:
            copy.wait_recv()
        wide = tab_s[...].astype(F32).reshape(-1, 2 * ROWS, half)
        tab = jnp.concatenate([wide[:, 0:ROWS], wide[:, ROWS:]], axis=-1).reshape(tab_o.shape)
        tab_o[...] = tab
        qtab[...] = (tab * inv_rms(tab) * gains[0:1]).astype(BF)
        tail_s[...] = jnp.zeros_like(tail_s)
        carry_s[...] = jnp.zeros_like(carry_s)

        def convolve(lo, hi):
            def one(block, _):
                conv_block(block, ids_s, qtab, taps, conv_s, padq, tail_s)
                return _

            lax.fori_loop(lo, hi, one, 0)

        for copy in own:
            copy.wait()
        convolve(0, 2)
        act(2, 2)
        act(4, 1)
        convolve(2, 4)
        for i in later_groups[0]:
            rest.act(i, 0)
        act(1, 3)
        act(3, 2)
        convolve(4, 6)
        act(4, 2)
        act(2, 3)
        convolve(6, 8)
        for i in later_groups[1]:
            rest.act(i, 0)
        onward[1].start()
        total = jnp.zeros(count_o.shape, F32)
        for n in range(8 * depth):
            total = total + count_s[n // (4 * depth), n // (2 * depth) % 2, n // 2 % depth, n % 2]
        count_o[...] = total
        act(3, 3)
        act(4, 3)
        onward[0].start()
        for i in later_groups[2]:
            rest.act(i, 0)

    for when, acts in GATHER_SCHEDULE.items():

        @pl.when(step == when)
        def _(acts=acts):
            for group, phase in acts:
                for i in later_groups[group]:
                    rest.act(i, phase)

    ids_o[0] = ids_s[step]
    front_block(conv_s.at[step], bias, FlatRows(in_s), keep_o, p_o, q_o, state_o, carry_s, big)

    @pl.when(step == blocks - 1)
    def _():
        for group, phase in GATHER_LAST:
            for i in later_groups[group]:
                rest.act(i, phase)
        for copy in onward:
            copy.wait()
        for copy in spread:
            copy.wait_send()
        first.finish()
        rest.finish()


class FlatRows:
    def __init__(self, ref):
        self.ref = ref

    def __getitem__(self, index):
        cols = index[1]
        part = self.ref[:, :, :, :, :, cols]
        return part.reshape(-1, part.shape[-1])


def run_front(depth, ids, table, mats, gains, taps, bias):
    blocks = 2 * depth
    seqs, span = ids[0].shape
    rows = seqs * span // blocks
    tile = (blocks, 2 * ROWS, LANES)
    w_in, w_out, w_up, w_down = mats
    width = table.shape[1]
    hidden = bias.shape[1]
    kernel = taps.shape[0]
    total = blocks * rows
    rim = (kernel - 1) * ROWS
    owners = (2, 2, depth, 2)
    devices = 8 * depth
    vocab = devices * table.shape[0]
    cols = w_in.shape[1]
    now = [(0, 0, width // 2, True), (1, 0, LANES, False)]
    for n in range(8):
        now.append((2, n * cols // 8, (n + 1) * cols // 8, n % 2 == 0))
    later = halves([a.shape for a in (w_out, w_up, w_down)], (1, 2, 2))
    wide = pl.BlockSpec((rows, hidden), lambda i: (i, 0))
    any_spec = pl.BlockSpec(memory_space=pl.ANY)
    dma = lambda *shape: pltpu.SemaphoreType.DMA(shape)
    args = tuple(ids) + (table, w_in, w_out, w_up, w_down, gains, taps, bias)
    struct = jax.ShapeDtypeStruct
    return pl.pallas_call(
        functools.partial(front_kernel, depth, now, later),
        grid=(blocks,),
        in_specs=[whole(a.shape) for a in args],
        out_specs=[wide] * 4
        + [pl.BlockSpec((1,) + tile[1:], lambda i: (i, 0, 0)), whole((vocab, width)), whole((ROWS, LANES))]
        + [any_spec] * 5,
        out_shape=[struct((total, hidden), F32)] * 3
        + [struct((total, hidden), BF), struct(tile, jnp.int32), struct((vocab, width), F32)]
        + [struct((ROWS, LANES), F32), struct((blocks, rows, width), BF)]
        + [struct(owners + a.shape, BF) for a in mats],
        scratch_shapes=[
            pltpu.VMEM(tile, jnp.int32),
            pltpu.VMEM(tile, jnp.int32),
            pltpu.VMEM(owners + (2 * ROWS, width // 2), BF),
            pltpu.VMEM(owners + (ROWS, LANES), F32),
            pltpu.VMEM(owners + w_in.shape, BF),
            pltpu.VMEM(w_out.shape, BF),
            pltpu.VMEM(w_up.shape, BF),
            pltpu.VMEM(w_down.shape, BF),
            pltpu.VMEM((vocab, width), BF),
            pltpu.VMEM((blocks, rows, width), BF),
            pltpu.VMEM((rim + rows, width), F32),
            pltpu.VMEM((rim, width), F32),
            pltpu.VMEM((ROWS, hidden), F32),
            pltpu.VMEM((rows, hidden), F32),
            dma(2 * depth),
            dma(2 * depth),
            dma(len(now), depth + 2),
            dma(len(now), depth + 2),
            dma(len(later), depth + 2),
            dma(len(later), depth + 2),
            dma(3),
            dma(2),
        ],
        compiler_params=pltpu.CompilerParams(
            dimension_semantics=("arbitrary",), collective_id=0, has_side_effects=True, vmem_limit_bytes=60 * MIB
        ),
        name="gather_and_front",
    )(*args)


def tail_kernel(
    ids, state_low, tab, count, gains, w_out, w_up, w_down,
    mixed_o, normed_o, final_o, lifted_o, g_down, g_tab, small_o,
    tab_low, slope_s, active,
):
    step = pl.program_id(0)
    rows = state_low.shape[0]
    vocab, width = tab.shape
    ff = w_up.shape[1]
    chunk = 256

    @pl.when(step == 0)
    def _():
        tab_low[...] = tab[...].astype(BF)
        g_down[...] = jnp.zeros_like(g_down)
        g_tab[...] = jnp.zeros_like(g_tab)
        small_o[...] = jnp.zeros_like(small_o)

    here = ids[0]
    hot = one_hot(here, vocab)
    mixed = nn(hot, tab_low[...]) + nn(state_low[...], w_out[...])
    mixed_o[...] = mixed
    inverse_b = inv_rms(mixed)
    normed_o[...] = (mixed * inverse_b * gains[1:2]).astype(BF)
    for j in range(ff // chunk):
        cols = slice(j * chunk, (j + 1) * chunk)
        lifted = nn(normed_o[...], w_up[:, cols])
        square = lifted * lifted
        curve = jnp.tanh(lifted * (GELU_A + (GELU_A * GELU_B) * square))
        cdf = 0.5 + 0.5 * curve
        active[:, cols] = (lifted * cdf).astype(BF)
        slope_s[:, cols] = cdf + (0.5 * lifted) * (1.0 - curve * curve) * (
            GELU_A + (3.0 * GELU_A * GELU_B) * square
        )
    result = mixed_o[...] + nn(active[...], w_down[...])
    inverse_f = inv_rms(result)
    unit_f = result * inverse_f
    normed_f = (unit_f * gains[2:3]).astype(BF)

    logits = nt(normed_f, tab_low[...])
    top = jnp.max(logits, axis=-1, keepdims=True)
    powers = jnp.exp(logits - top)
    total = jnp.sum(powers, axis=-1, keepdims=True)
    lse = jnp.log(total) + top
    target = hits(here, LANES // 2, vocab)
    picked = jnp.sum(target * logits, axis=-1, keepdims=True)
    weight = spread_steps(here, ROWS, 0, vocab).astype(F32)
    loss = column_sum(weight[:, 0:1] * (lse - picked))
    share = weight * (1.0 / count[0:1, 0:1])
    d_logits = ((powers * (1.0 / total) - target) * share).astype(BF)
    g_tab[...] += tn(d_logits, normed_f)
    d_normed_f = nn(d_logits, tab_low[...])
    small_o[2:3, :] += column_sum(d_normed_f * unit_f)
    small_o[3:4, :] += jnp.broadcast_to(loss, (1, width))
    d_final = norm_back(result, inverse_f, gains[2:3], d_normed_f)
    final_o[...] = d_final
    grad_low = d_final.astype(BF)
    for j in range(ff // chunk):
        cols = slice(j * chunk, (j + 1) * chunk)
        d_active = nt(grad_low, w_down[cols, :])
        g_down[cols, :] += tn(active[:, cols], grad_low)
        lifted_o[:, cols] = (d_active * slope_s[:, cols]).astype(BF)


def run_tail(ids, state_low, tab, count, gains, w_out, w_up, w_down):
    blocks = ids.shape[0]
    rows = state_low.shape[0] // blocks
    vocab, width = tab.shape
    hidden = w_out.shape[0]
    ff = w_up.shape[1]
    total = blocks * rows
    block = lambda cols: pl.BlockSpec((rows, cols), lambda i: (i, 0))
    sums = ((ff, width), (vocab, width), (ROWS, width))
    struct = jax.ShapeDtypeStruct
    return pl.pallas_call(
        tail_kernel,
        grid=(blocks,),
        in_specs=[pl.BlockSpec((1,) + ids.shape[1:], lambda i: (i, 0, 0)), block(hidden)]
        + [whole(a.shape) for a in (tab, count, gains, w_out, w_up, w_down)],
        out_specs=[block(width), block(width), block(width), block(ff)] + [whole(s) for s in sums],
        out_shape=[struct((total, width), F32), struct((total, width), BF), struct((total, width), F32), struct((total, ff), BF)]
        + [struct(s, F32) for s in sums],
        scratch_shapes=[
            pltpu.VMEM((vocab, width), BF),
            pltpu.VMEM((rows, ff), F32),
            pltpu.VMEM((rows, ff), BF),
        ],
        compiler_params=pltpu.CompilerParams(
            dimension_semantics=("arbitrary",), vmem_limit_bytes=62 * MIB
        ),
        name="tail_and_head",
    )(ids, state_low, tab, count, gains, w_out, w_up, w_down)


MID_SCHEDULE = {
    2: [(0, 0, 0)], 3: [(0, 1, 0)], 8: [(0, 0, 1)], 9: [(0, 1, 1), (1, 0, 0)], 10: [(1, 1, 0), (0, 0, 2), (0, 1, 2)],
    11: [(1, 0, 1)], 12: [(1, 1, 1)], 13: [(1, 0, 2)], 14: [(1, 1, 2), (0, 0, 3), (0, 1, 3)],
}
MID_LAST = [(1, 0, 3), (1, 1, 3)]


def mid_kernel(depth, plans, counts, *refs):
    ids, mixed, normed, final, lifted, keep, p, q, conv, gains, w_out, w_up, small_in, g_down = refs[:14]
    d_pre, mixed_o, g_in, g_emb, small_o, r_down, r_up = refs[14:21]
    g_up, ds, cand, carry_s = refs[21:25]
    step = pl.program_id(0)
    blocks = pl.num_programs(0) // 2
    spot = place()
    sums, at = [], 25
    for n, (source, out) in enumerate(((g_down, r_down), (g_up, r_up))):
        sums.append(Reduce(plans[n], depth, source, n > 0, out, refs[at : at + counts[n]], spot))
        at += counts[n]
    vocab, width = g_emb.shape
    rows, hidden = keep.shape
    steps = rows // ROWS
    chunk = 256

    def run(acts):
        for n, pair, phase in acts:
            sums[n].pair(pair, phase)

    @pl.when(step == 0)
    def _():
        greet(*spot, depth)
        sums[0].begin()
        g_up[...] = jnp.zeros_like(g_up)
        g_in[...] = jnp.zeros_like(g_in)
        g_emb[...] = jnp.zeros_like(g_emb)
        small_o[...] = small_in[...]
        carry_s[...] = jnp.zeros_like(carry_s)

    for when, acts in MID_SCHEDULE.items():

        @pl.when(step == when)
        def _(acts=acts):
            run(acts)

    @pl.when(step < blocks)
    def _():
        g_up[...] += tn(normed[...], lifted[...]).reshape(g_up.shape)

    @pl.when(step == blocks - 1)
    def _():
        sums[1].begin()

    @pl.when(step >= blocks)
    def _():
        d_normed = nt(lifted[...], w_up[...])
        value = mixed[...]
        inverse = inv_rms(value)
        small_o[1:2, :] += column_sum(d_normed * (value * inverse))
        d_mixed = final[...] + norm_back(value, inverse, gains[1:2], d_normed)
        mixed_low = d_mixed.astype(BF)
        rest = (d_mixed - mixed_low.astype(F32)).astype(BF)
        ds[...] = nt(mixed_low, w_out[...])
        hot = one_hot(ids[0], vocab)
        g_emb[...] += tn(hot, mixed_low) + tn(hot, rest)
        mixed_o[...] = mixed_low

        low_half = lax.broadcasted_iota(jnp.int32, (ROWS, chunk), 0) < ROWS // 2
        for j in range(hidden // chunk):
            cols = slice(j * chunk, (j + 1) * chunk)
            carry = carry_s[:, cols]
            first = carry
            for tau in reversed(range(steps)):
                at = slice(tau * ROWS, (tau + 1) * ROWS)
                first = keep[at, cols] * (ds[at, cols] + first)
            reached = jnp.where(low_half, swap_halves(first), carry)
            total = jnp.zeros((ROWS, chunk), F32)
            for tau in reversed(range(steps)):
                at = slice(tau * ROWS, (tau + 1) * ROWS)
                lam = ds[at, cols] + reached
                reached = keep[at, cols] * lam
                d_gate = lam * p[at, cols]
                ds[at, cols] = d_gate
                cand[at, :] = lam * q[at, cols]
                total = total + d_gate
            d_pre[:, j * chunk : (j + 1) * chunk] = ds[:, cols].astype(BF)
            d_pre[:, hidden + j * chunk : hidden + (j + 1) * chunk] = cand[...].astype(BF)
            carry_s[:, cols] = jnp.where(low_half, 0.0, swap_halves(reached))
            at = j * chunk
            row = 4 + at // width
            small_o[row : row + 1, at % width : at % width + chunk] += column_sum(total)
            for start in (at, hidden + at):
                g_in[:, start : start + chunk] += tn(conv[...], d_pre[:, start : start + chunk])

    @pl.when(step == 2 * blocks - 1)
    def _():
        run(MID_LAST)
        for one in sums:
            one.finish()


def run_mid(depth, ids, mixed, normed, final, lifted, keep, p, q, conv, gains, w_out, w_up, small, g_down, vocab):
    blocks = ids.shape[0]
    rows = mixed.shape[0] // blocks
    width, ff = w_up.shape
    hidden = w_out.shape[0]
    total = blocks * rows
    last = blocks - 1
    owners = (2, 2, depth, 2)
    back = lambda cols: pl.BlockSpec((rows, cols), lambda i: (jnp.minimum(2 * blocks - 1 - i, last), 0))
    once = pl.BlockSpec((rows, width), lambda i: (jnp.minimum(i, last), 0))
    both = pl.BlockSpec((rows, ff), lambda i: (jnp.minimum(i, 2 * blocks - 1 - i), 0))
    up_shape = owners + (width // (8 * depth), ff)
    shapes = (g_down.shape, up_shape)
    plans = [halves([shape], (2,)) for shape in shapes]
    moving = [Reduce.scratch(shape, plan, depth, n > 0) for n, (shape, plan) in enumerate(zip(shapes, plans))]
    sums = ((width, 2 * hidden), (vocab, width), small.shape, g_down.shape[-2:], up_shape[-2:])
    return pl.pallas_call(
        functools.partial(mid_kernel, depth, plans, [len(m) for m in moving]),
        grid=(2 * blocks,),
        in_specs=[
            pl.BlockSpec((1,) + ids.shape[1:], lambda i: (jnp.minimum(2 * blocks - 1 - i, last), 0, 0)),
            back(width), once, back(width), both, back(hidden), back(hidden), back(hidden), back(width),
        ]
        + [whole(a.shape) for a in (gains, w_out, w_up, small)]
        + [pl.BlockSpec(memory_space=pl.ANY)],
        out_specs=[back(2 * hidden), back(width)] + [whole(s) for s in sums],
        out_shape=[jax.ShapeDtypeStruct((total, 2 * hidden), BF), jax.ShapeDtypeStruct((total, width), BF)] + [jax.ShapeDtypeStruct(s, F32) for s in sums],
        scratch_shapes=[
            pltpu.VMEM(up_shape, F32),
            pltpu.VMEM((rows, hidden), F32),
            pltpu.VMEM((rows, 256), F32),
            pltpu.VMEM((ROWS, hidden), F32),
        ]
        + [piece for group in moving for piece in group],
        compiler_params=pltpu.CompilerParams(
            dimension_semantics=("arbitrary",), collective_id=2, has_side_effects=True, vmem_limit_bytes=63 * MIB
        ),
        name="mid_back_and_reduce",
    )(ids, mixed, normed, final, lifted, keep, p, q, conv, gains, w_out, w_up, small, g_down)


def adam_kernel(shapes, small, squares, count, *refs):
    mats = refs[:5]
    weights, firsts, seconds = refs[5:13], refs[13:21], refs[21:29]
    loss_o, count_o, norm_o = refs[29:32]
    new_w, new_m, new_v = refs[32:40], refs[40:48], refs[48:56]
    kernel, bias_rows = shapes
    grads = [m[...] for m in mats]
    grads.append(small[0:3, :])
    grads.append(small[ROWS : ROWS + kernel, :])
    grads.append(jnp.concatenate([small[4 + r : 5 + r, :] for r in range(bias_rows)], axis=1))
    square = squares[0:1, 0:1]
    for grad in grads[5:]:
        square = square + jnp.sum(jnp.sum(grad * grad, axis=1, keepdims=True), axis=0, keepdims=True)
    norm = jnp.sqrt(square)
    scale = jnp.minimum(1.0, CLIP / (norm + 1e-06))
    norm_o[...] = norm
    loss_o[...] = small[3:4, 0:1]
    count_o[...] = count[0:1, 0:1]
    for i in range(8):
        rate = RATE_MATRIX if i < 5 else RATE_VECTOR
        decay = WEIGHT_DECAY if i < 5 else 0.0
        w, m, v = adam(weights[i][...], grads[i] * scale, firsts[i][...], seconds[i][...], rate, decay)
        new_w[i][...] = w
        new_m[i][...] = m
        new_v[i][...] = v


def run_adam(shapes, mats, small, squares, count, weights, firsts, seconds):
    one = jax.ShapeDtypeStruct((1, 1), F32)
    like = [jax.ShapeDtypeStruct(w.shape, F32) for w in weights]
    args = (small, squares, count) + tuple(mats) + tuple(weights) + tuple(firsts) + tuple(seconds)
    return pl.pallas_call(
        functools.partial(adam_kernel, shapes),
        grid=(1,),
        in_specs=[whole(a.shape) for a in args],
        out_specs=[whole(a.shape) for a in [one] * 3 + like * 3],
        out_shape=[one] * 3 + like * 3,
        compiler_params=pltpu.CompilerParams(vmem_limit_bytes=60 * MIB),
        name="adam_update",
    )(*args)


def body_moved(depth, *args):
    weights, firsts, seconds = args[3:11], args[11:19], args[19:27]
    table, w_in, w_out, w_up, w_down, gains, conv_taps, gate_bias = weights
    width = table.shape[1]
    taps = conv_taps[0]
    keep, p, q, state_low, ids, tab, count, conv, *full = run_front(
        depth, args[:3], table, (w_in[0], w_out[0], w_up[0], w_down[0]), gains, taps, gate_bias
    )
    conv = conv.reshape(-1, width)
    full = [a.reshape(-1, a.shape[-1]) for a in full]
    mixed, normed, final, lifted, g_down, g_head, small = run_tail(ids, state_low, tab, count, gains, *full[1:])
    owned = lambda g: g.reshape((2, 2, depth, 2, -1, g.shape[-1]))
    d_pre, mixed_low, g_in, g_emb, small, r_down, r_up = run_mid(
        depth, ids, mixed, normed, final, lifted, keep, p, q, conv, gains, full[1], full[2], small, owned(g_down),
        tab.shape[0],
    )
    r_in, r_out, r_tab, small, squares = run_last(
        depth, ids, d_pre, state_low, mixed_low, tab, gains, taps, full[0], (g_head, g_emb), small, (r_down, r_up), owned(g_in)
    )
    mats = [r_tab, r_in, r_out, r_up, r_down]
    flat = lambda group: [group[0]] + [a[0] for a in group[1:5]] + [group[5], group[6][0], group[7]]
    out = run_adam(
        (conv_taps.shape[1], gate_bias.shape[1] // width),
        mats, small, squares, count, flat(weights), flat(firsts), flat(seconds),
    )
    shaped = [o.reshape(()) for o in out[:3]]
    for i, o in enumerate(out[3:]):
        shaped.append(o.reshape(weights[i % 8].shape))
    return tuple(shaped)


def choose(mesh, *args):
    ways = mesh.shape["seq"]
    seqs, span = args[0].shape
    if mesh.shape["dp"] == 4 and ways == 8 and seqs == 4 * ways and span == LANES:
        return body_moved(ways // 2, *args)
    return body(*args)


def solution(mesh):
    return jax.shard_map(
        functools.partial(choose, mesh),
        mesh=mesh,
        in_specs=(
            P("dp", "seq"),
            P("dp", "seq"),
            P("dp", "seq"),
            P(("dp", "seq"), None),
            P(None, ("dp", "seq"), None),
            P(None, ("dp", "seq"), None),
            P(None, ("dp", "seq"), None),
            P(None, ("dp", "seq"), None),
            P(),
            P(),
            P(),
            P(("dp", "seq"), None),
            P(None, ("dp", "seq"), None),
            P(None, ("dp", "seq"), None),
            P(None, ("dp", "seq"), None),
            P(None, ("dp", "seq"), None),
            P(),
            P(),
            P(),
            P(("dp", "seq"), None),
            P(None, ("dp", "seq"), None),
            P(None, ("dp", "seq"), None),
            P(None, ("dp", "seq"), None),
            P(None, ("dp", "seq"), None),
            P(),
            P(),
            P(),
        ),
        out_specs=(
            P(),
            P(),
            P(),
            P(("dp", "seq"), None),
            P(None, ("dp", "seq"), None),
            P(None, ("dp", "seq"), None),
            P(None, ("dp", "seq"), None),
            P(None, ("dp", "seq"), None),
            P(),
            P(),
            P(),
            P(("dp", "seq"), None),
            P(None, ("dp", "seq"), None),
            P(None, ("dp", "seq"), None),
            P(None, ("dp", "seq"), None),
            P(None, ("dp", "seq"), None),
            P(),
            P(),
            P(),
            P(("dp", "seq"), None),
            P(None, ("dp", "seq"), None),
            P(None, ("dp", "seq"), None),
            P(None, ("dp", "seq"), None),
            P(None, ("dp", "seq"), None),
            P(),
            P(),
            P(),
        ),
        check_vma=False,
    )
```
